128 devices in a mesh: lon: 16 (over z_lo, x, core), lat: 8 (over y, z_hi).
Axes of the slice: x: 4, y: 4, z: 4 (z_hi: 2, z_lo: 2; z = z_hi * 2 + z_lo), core: 2. Of those that a mesh axis runs over, the one named last changes fastest.
Arguments:
- fields: bfloat16 [8, 16, 13, 80, 128], P('lat', 'lon'), may hold values from -6 to 6
- embed_weight: bfloat16 [80, 512], replicated, may hold values from -1 to 1
- level_code: float32 [13, 512], replicated, may hold values from -6 to 6
- encoder_gain: float32 [512], replicated, may hold values from 0.1 to 1.9
- key_weight: bfloat16 [512, 512], replicated, may hold values from -0.25 to 0.25
- value_weight: bfloat16 [512, 512], replicated, may hold values from -0.25 to 0.25
- latent_query: float32 [4, 512], replicated, may hold values from -6 to 6
- encoder_scale: float32 [16], replicated, may hold values from 4 to 20
- latent_weight: bfloat16 [512, 512], replicated, may hold values from -0.25 to 0.25
- latent_base: float32 [4, 512], replicated, may hold values from -6 to 6
- first_project: bfloat16 [512, 1536], replicated, may hold values from -1 to 1
- first_scale: float32 [16], replicated, may hold values from 4 to 20
- first_output: bfloat16 [512, 512], replicated, may hold values from -1 to 1
- first_gain: float32 [512], replicated, may hold values from 0.1 to 1.9
- second_project: bfloat16 [512, 1536], replicated, may hold values from -1 to 1
- second_scale: float32 [16], replicated, may hold values from 4 to 20
- second_output: bfloat16 [512, 512], replicated, may hold values from -1 to 1
- second_gain: float32 [512], replicated, may hold values from 0.1 to 1.9
Outputs:
- processed: bfloat16 [128, 128, 4, 512], P('lat', 'lon')
The draws below stay inside these ranges and needn't reach their ends.
All inputs are finite; a program needn't handle non-finite values.
Results may differ from the reference program's by a relative error of at most 0.023.
Values may be sent and summed in bfloat16 or wider, within the bound.
No kernel may reach another device: no remote copies, remote signals or barrier semaphores. Data moves between devices by JAX's collectives and lax.ppermute only.
A program may use at most 128 MiB of HBM per device.

```python
import math
import jax
import jax.numpy as jnp
from jax import lax

D = 512
HEADS = 16
LEVELS = 13
LATENT = 4
WIN = 8
HEAD = 32
PV = 80
HALF = 4
TLAT = 16
BANDS = 8
LATP = 128
LONP = 128


def shaped_weight(scale_key, raw_entries, fan_in, spread):
    column_key = jax.random.fold_in(scale_key, 0)
    column_scale = spread ** (jax.random.uniform(column_key, (1, raw_entries.shape[1]), jnp.float32) - 0.5)
    weight = raw_entries * column_scale * fan_in ** (-0.5)
    return jnp.clip(weight, -1.0, 1.0).astype(jnp.bfloat16)


def spread_draw(key, row_count, column_count, fan_in, spread):
    entry_key, scale_key = jax.random.split(key)
    raw_entries = jnp.clip(jax.random.normal(entry_key, (row_count, column_count), jnp.float32), -5.0, 5.0)
    return shaped_weight(scale_key, raw_entries, fan_in, spread)


def draw_embed_weight(key, part):
    key = jax.random.fold_in(key, 11)
    return spread_draw(key, PV, D, PV, 10.0)


def draw_first_project(key, part):
    key = jax.random.fold_in(key, 12)
    return spread_draw(key, D, 3 * D, D, 10.0)


def draw_first_output(key, part):
    key = jax.random.fold_in(key, 13)
    return spread_draw(key, D, D, D, 10.0)


def draw_second_project(key, part):
    key = jax.random.fold_in(key, 14)
    return spread_draw(key, D, 3 * D, D, 10.0)


def draw_second_output(key, part):
    key = jax.random.fold_in(key, 15)
    return spread_draw(key, D, D, D, 10.0)


def block_levels(own_key, shape, shards, least, high):
    factor_of = 1.0
    for position, blocks in shards:
        heights = jax.random.uniform(jax.random.fold_in(jax.random.fold_in(own_key, 6), position), (blocks,), jnp.float32, least / len(shards), high / len(shards))
        factor_of = factor_of * jnp.repeat(jnp.exp(heights), shape[position] // blocks).reshape((-1,) + (1,) * (len(shape) - 1 - position))
    return factor_of


def gaussian(rng, dims, scale, limit, cuts=(), kind=jnp.bfloat16):
    values = jax.random.normal(rng, dims, jnp.float32) * scale
    if len(cuts) > 0:
        values = block_levels(rng, dims, cuts, -0.22, 0.18) * values
    return jnp.clip(values, min=-limit, max=limit).astype(kind)


def setup_inputs(seed: int = 0) -> dict:
    streams_of = jax.random.split(jax.random.key(seed), 19)
    fields = gaussian(streams_of[0], (BANDS, TLAT, LEVELS, PV, LONP), 1.0, 6.0, ((0, 8), (1, 16)))
    embed_weight = draw_embed_weight(jax.random.fold_in(streams_of[18], 71), 0)
    level_code = gaussian(streams_of[2], (LEVELS, D), 1.0, 6.0, (), jnp.float32)
    encoder_gain = jnp.clip(1.0 + 0.18 * jax.random.normal(streams_of[3], (D,), jnp.float32), 0.1, 1.9)
    key_weight = gaussian(streams_of[4], (D, D), D ** -0.5, 0.25)
    value_weight = gaussian(streams_of[5], (D, D), D ** -0.5, 0.25)
    latent_query = gaussian(streams_of[6], (LATENT, D), 1.0, 6.0, (), jnp.float32)
    encoder_scale = jnp.clip(jnp.exp(jax.random.uniform(streams_of[7], (HEADS,), jnp.float32, math.log(4.0), math.log(20.0))), 4.0, 20.0)
    latent_weight = gaussian(streams_of[8], (D, D), D ** -0.5, 0.25)
    latent_base = gaussian(streams_of[9], (LATENT, D), 1.0, 6.0, (), jnp.float32)
    first_project = draw_first_project(jax.random.fold_in(streams_of[18], 71), 0)
    first_scale = jnp.clip(jnp.exp(jax.random.uniform(streams_of[11], (HEADS,), jnp.float32, math.log(4.0), math.log(20.0))), 4.0, 20.0)
    first_output = draw_first_output(jax.random.fold_in(streams_of[18], 71), 0)
    first_gain = jnp.clip(1.0 + 0.18 * jax.random.normal(streams_of[13], (D,), jnp.float32), 0.1, 1.9)
    second_project = draw_second_project(jax.random.fold_in(streams_of[18], 71), 0)
    second_scale = jnp.clip(jnp.exp(jax.random.uniform(streams_of[15], (HEADS,), jnp.float32, math.log(4.0), math.log(20.0))), 4.0, 20.0)
    second_output = draw_second_output(jax.random.fold_in(streams_of[18], 71), 0)
    second_gain = jnp.clip(1.0 + 0.18 * jax.random.normal(streams_of[17], (D,), jnp.float32), 0.1, 1.9)
    return dict(fields=fields, embed_weight=embed_weight, level_code=level_code, encoder_gain=encoder_gain, key_weight=key_weight, value_weight=value_weight, latent_query=latent_query, encoder_scale=encoder_scale, latent_weight=latent_weight, latent_base=latent_base, first_project=first_project, first_scale=first_scale, first_output=first_output, first_gain=first_gain, second_project=second_project, second_scale=second_scale, second_output=second_output, second_gain=second_gain)


NORM_EPS = 1e-05
DIR_EPS = 1e-06

def layer_norm(entries, gains):
    centre = entries - lax.optimization_barrier(jnp.mean(entries, axis=-1, keepdims=True))
    spread = lax.optimization_barrier(jnp.mean(centre * centre, axis=-1, keepdims=True))
    return centre / jnp.sqrt(spread + NORM_EPS) * gains

def head_direction(vectors):
    shaped = vectors.reshape(vectors.shape[:-1] + (HEADS, HEAD))
    length = jnp.sqrt(lax.optimization_barrier(jnp.sum(shaped * shaped, axis=-1, keepdims=True)) + DIR_EPS)
    return (shaped / length).astype(jnp.bfloat16)

def rounded(entries):
    return lax.optimization_barrier(entries.astype(jnp.bfloat16)).astype(jnp.float32)

def encode_row(patch_block, embed_weight, level_code, encoder_gain, key_weight, value_weight, latent_dir, encoder_scale, latent_weight, latent_base):
    patch_count = patch_block.shape[-1]
    embedded = jnp.einsum('kvn,vd->nkd', patch_block.astype(jnp.float32), embed_weight.astype(jnp.float32)) + level_code[None]
    normed = layer_norm(embedded, encoder_gain).astype(jnp.bfloat16).reshape(patch_count * LEVELS, D)
    enc_keys = jnp.dot(normed, key_weight, preferred_element_type=jnp.float32).astype(jnp.bfloat16)
    enc_values = jnp.dot(normed, value_weight, preferred_element_type=jnp.float32).astype(jnp.bfloat16)
    key_dir = head_direction(enc_keys.astype(jnp.float32)).reshape(patch_count, LEVELS, HEADS, HEAD)
    scores = jnp.einsum('lhe,nkhe->nhlk', latent_dir.astype(jnp.float32), key_dir.astype(jnp.float32))
    exponent = jnp.exp(scores * encoder_scale[None, :, None, None])
    weights = rounded(exponent / lax.optimization_barrier(jnp.sum(exponent, axis=-1, keepdims=True)))
    value_heads = enc_values.reshape(patch_count, LEVELS, HEADS, HEAD).astype(jnp.float32)
    mixture = jnp.einsum('nhlk,nkhe->nlhe', weights, value_heads).astype(jnp.bfloat16)
    merged = jnp.dot(mixture.reshape(patch_count * LATENT, D), latent_weight, preferred_element_type=jnp.float32)
    return (merged.reshape(patch_count, LATENT, D) + latent_base[None]).astype(jnp.bfloat16)

def to_windows(token_grid, win_rows, win_cols):
    grid_rows, grid_cols = (token_grid.shape[0], token_grid.shape[1])
    shaped = token_grid.reshape((grid_rows // win_rows, win_rows, grid_cols // win_cols, win_cols) + token_grid.shape[2:])
    return jnp.swapaxes(shaped, 1, 2).reshape((-1, win_rows * win_cols * token_grid.shape[2], token_grid.shape[-1]))

def from_windows(windows, grid_rows, grid_cols, win_rows, win_cols):
    shaped = windows.reshape(grid_rows // win_rows, grid_cols // win_cols, win_rows, win_cols, LATENT, D)
    return jnp.swapaxes(shaped, 1, 2).reshape(grid_rows, grid_cols, LATENT, D)

def window_layer(tokens, live_mask, project, head_scale, output, gains):
    window_count, window_tokens = (tokens.shape[0], tokens.shape[1])
    flat_tokens = tokens.reshape(window_count * window_tokens, D)
    projected = jnp.dot(flat_tokens, project, preferred_element_type=jnp.float32).reshape(window_count, window_tokens, 3 * D)
    query_dir = head_direction(projected[..., :D]).astype(jnp.float32)
    key_dir = head_direction(projected[..., D:2 * D]).astype(jnp.float32)
    value_heads = projected[..., 2 * D:].astype(jnp.bfloat16).reshape(window_count, window_tokens, HEADS, HEAD).astype(jnp.float32)
    scores = jnp.einsum('wqhe,wkhe->whqk', query_dir, key_dir) * head_scale[None, :, None, None]
    exponent = jnp.exp(scores) * live_mask[:, None, None, :, 0]
    weights = rounded(exponent / lax.optimization_barrier(jnp.sum(exponent, axis=-1, keepdims=True)))
    mixture = jnp.einsum('whqk,wkhe->wqhe', weights, value_heads).astype(jnp.bfloat16).reshape(window_count * window_tokens, D)
    branch = layer_norm(jnp.dot(mixture, output, preferred_element_type=jnp.float32), gains)
    return (flat_tokens.astype(jnp.float32) + branch).astype(jnp.bfloat16).reshape(window_count, window_tokens, D)

def reference(fields, embed_weight, level_code, encoder_gain, key_weight, value_weight, latent_query, encoder_scale, latent_weight, latent_base, first_project, first_scale, first_output, first_gain, second_project, second_scale, second_output, second_gain):
    rows_grid = fields.reshape(LATP, LEVELS, PV, LONP)
    latent_dir = head_direction(latent_query)

    def encode_one(patch_block):
        return encode_row(patch_block, embed_weight, level_code, encoder_gain, key_weight, value_weight, latent_dir, encoder_scale, latent_weight, latent_base)
    encoded = lax.map(encode_one, rows_grid)
    ones_grid = to_windows(jnp.ones((WIN, LONP, LATENT, 1), jnp.float32), WIN, WIN)

    def first_band(band_rows):
        attended = window_layer(to_windows(band_rows, WIN, WIN), ones_grid, first_project, first_scale, first_output, first_gain)
        return from_windows(attended, WIN, LONP, WIN, WIN)
    first_out = lax.map(first_band, encoded.reshape(LATP // WIN, WIN, LONP, LATENT, D)).reshape(LATP, LONP, LATENT, D)
    rolled = jnp.roll(first_out, -HALF, axis=1)
    padded = jnp.pad(rolled, ((HALF, HALF), (0, 0), (0, 0), (0, 0)))
    row_index = jnp.arange(LATP + WIN, dtype=jnp.int32)
    alive_rows = jnp.where((row_index >= HALF) & (row_index < LATP + HALF), 1.0, 0.0).astype(jnp.float32)
    alive_grid = jnp.broadcast_to(alive_rows.reshape((LATP + WIN) // WIN, WIN, 1, 1, 1), ((LATP + WIN) // WIN, WIN, LONP, LATENT, 1))

    def second_band(band_pair):
        band_rows, band_alive = band_pair
        attended = window_layer(to_windows(band_rows, WIN, WIN), to_windows(band_alive, WIN, WIN), second_project, second_scale, second_output, second_gain)
        return from_windows(attended, WIN, LONP, WIN, WIN)
    second = lax.map(second_band, (padded.reshape((LATP + WIN) // WIN, WIN, LONP, LATENT, D), alive_grid))
    second = second.reshape(LATP + WIN, LONP, LATENT, D)[HALF:HALF + LATP]
    return jnp.roll(second, HALF, axis=1)
```

```python
import jax
import jax.numpy as jnp
from jax import lax
from jax.experimental import pallas as pl
from jax.experimental.pallas import tpu as pltpu
from jax.sharding import PartitionSpec as P

D = 512
HEADS = 16
LEVELS = 13
LATENT = 4
PV = 80
HEAD = 32
HALF = 4
LANES = 128
GROUPS = D // LANES
IN_GROUP = LANES // HEAD
NORM_EPS = 1e-05
DIR_EPS = 1e-06
LOG2E = 1.4426950408889634
BF = jnp.bfloat16
F32 = jnp.float32
ENC_SPANS = [(256 * i, 256) for i in range(6)] + [(1536, 128)]


def iota(shape, dim):
    return lax.broadcasted_iota(jnp.int32, shape, dim)


def matmul(a, b):
    return jnp.dot(a, b, preferred_element_type=F32)


def matmul_nt(a, b):
    return lax.dot_general(a, b, (((1,), (1,)), ((), ())), preferred_element_type=F32)


def matmul_tn(a, b):
    return lax.dot_general(a, b, (((0,), (0,)), ((), ())), preferred_element_type=F32)


def halves(value):
    high = value.astype(BF)
    return high, (value - high.astype(F32)).astype(BF)


def scale_row(scale_ref):
    head = iota((1, D), 1) // HEAD
    row = jnp.zeros((1, D), F32)
    for h in range(HEADS):
        row = jnp.where(head == h, scale_ref[h] * LOG2E, row)
    return row


def head_blocks():
    return (iota((256, 256), 0) // HEAD == iota((256, 256), 1) // HEAD).astype(F32).astype(BF)


def head_squares(value, blocks):
    square = (value * value).astype(BF)
    return jnp.concatenate(
        [matmul(square[:, i : i + 256], blocks) for i in range(0, D, 256)], axis=1
    )


def direction(value, blocks):
    return value * lax.rsqrt(head_squares(value, blocks) + DIR_EPS)


def lane_masks():
    head = iota((1, LANES), 1) // HEAD
    return [(head == h).astype(F32).astype(BF) for h in range(IN_GROUP)]


def attend(queries, keys, values, masks, alive):
    count = queries.shape[0]
    tokens = keys.shape[0]
    parts = []
    for g in range(GROUPS):
        lanes = slice(g * LANES, (g + 1) * LANES)
        q, k, v = queries[:, lanes], keys[:, lanes], values[:, lanes]
        if alive is not None:
            v = v * alive
        stacked = jnp.concatenate([q * m for m in masks], axis=0)
        weight = jnp.exp2(matmul_nt(stacked, k)).astype(BF)
        spread = jnp.concatenate(
            [weight[h * count : (h + 1) * count] for h in range(IN_GROUP)], axis=1
        )
        ones = [jnp.broadcast_to(m, (tokens, LANES)) for m in masks]
        if alive is not None:
            ones = [o * alive for o in ones]
        extended = jnp.concatenate(
            [jnp.concatenate([v * m, o], axis=1) for m, o in zip(masks, ones)], axis=0
        )
        both = matmul(spread, extended)
        parts.append((both[:, :LANES] / both[:, LANES:]).astype(BF))
    return jnp.concatenate(parts, axis=1)


def finish(tokens, mixture, output, gain):
    branch = matmul(mixture, output)
    centre = branch - jnp.mean(branch, axis=-1, keepdims=True)
    spread = jnp.mean(centre * centre, axis=-1, keepdims=True)
    return tokens.astype(F32) + centre * lax.rsqrt(spread + NORM_EPS) * gain


def encode_kernel(
    fields, embed, code, gain, key_w, value_w, query, scale, latent_w, base, out,
    f2, wide, mats, vals, wts, mix,
):
    wide[...] = jnp.zeros((128, D), F32)
    w = embed[...].astype(F32)
    wide[0:PV] = w - jnp.mean(w, axis=-1, keepdims=True)
    c = code[...]
    wide[PV : PV + LEVELS] = c - jnp.mean(c, axis=-1, keepdims=True)
    centred = wide[...]
    high, low = halves(centred * gain[...])
    both = jnp.concatenate([high, low], axis=0)
    for i, weight in enumerate((key_w, value_w)):
        product = matmul(both, weight[...])
        product = product[:128] + product[128:]
        h, l = halves(product.T)
        mats[i * D : (i + 1) * D] = jnp.concatenate([h, l], axis=1)
        if i == 0:
            own = iota((HEADS, D), 1) // HEAD == iota((HEADS, D), 0)
            rows = jnp.concatenate(
                [jnp.where(own, query[l : l + 1, :], 0.0) for l in range(LATENT)], axis=0
            )
            length = jnp.sum(rows * rows, axis=-1, keepdims=True) + DIR_EPS
            rows = (rows * lax.rsqrt(length) * scale_row(scale)).astype(BF)
            kh, kl = halves(product)
            raw = matmul_nt(rows, kh) + matmul_nt(rows, kl)
            h, l = halves(raw)
            mats[3 * D : 3 * D + 64] = jnp.concatenate([h, l], axis=1)
    h, l = halves(centred.T)
    mats[2 * D : 3 * D] = jnp.concatenate([h, l], axis=1)

    level = (iota((48, LEVELS * LANES), 0) == iota((48, LEVELS * LANES), 1) // LANES)
    level = level.astype(F32).astype(BF)
    for top in (0, 128):
        f2[top + PV : top + 128, :] = level
        for k in range(LEVELS):
            f2[top : top + PV, k * LANES : (k + 1) * LANES] = fields[k]

    gather = (iota((HEADS, 128), 1) // 8 == iota((HEADS, 128), 0)).astype(F32).astype(BF)
    total = jnp.zeros((64, LANES), F32)
    for start, width in ENC_SPANS:
        rhs = f2[:, start : start + width]
        keys = matmul(mats[0:D], rhs)
        part = jnp.sum((keys * keys).reshape(HEADS, 4, 8, width), axis=1).reshape(128, width)
        squares = matmul(gather, part.astype(BF))
        centre = matmul(mats[2 * D : 3 * D], rhs)
        part = jnp.sum((centre * centre).reshape(64, 8, width), axis=0)
        spread = jnp.sum(part, axis=0, keepdims=True) * (1.0 / D) + NORM_EPS
        factor = lax.rsqrt(squares + DIR_EPS * spread)
        scores = matmul(mats[3 * D : 3 * D + 64], rhs) * jnp.concatenate([factor] * LATENT, axis=0)
        weights = jnp.exp2(scores)
        scaled = weights * lax.rsqrt(spread)
        values = matmul(mats[D : 2 * D], rhs)
        for i in range(width // LANES):
            k = start // LANES + i
            lanes = slice(i * LANES, (i + 1) * LANES)
            total = total + weights[:, lanes]
            wts[k] = scaled[:, lanes]
            vals[k] = values[:, lanes]
    wts[LEVELS] = 1.0 / total

    for h in range(HEADS):
        rows = slice(h * HEAD, (h + 1) * HEAD)
        sums = [jnp.zeros((HEAD, LANES), F32) for _ in range(LATENT)]
        for k in range(LEVELS):
            v = vals[k, rows, :]
            for l in range(LATENT):
                sums[l] = sums[l] + wts[k, l * HEADS + h : l * HEADS + h + 1, :] * v
        for l in range(LATENT):
            r = wts[LEVELS, l * HEADS + h : l * HEADS + h + 1, :]
            mix[l, rows, :] = (sums[l] * r).astype(BF)
    for l in range(LATENT):
        merged = matmul_tn(mix[l], latent_w[...]) + base[l : l + 1, :]
        out[:, l * D : (l + 1) * D] = merged.astype(BF)


def column_order(to_halves):
    a, b = (0, 1) if to_halves else (1, 0)
    i, j = iota((128, 128), a), iota((128, 128), b)
    source = ((i % 64) // 4) * 8 + (i // 64) * 4 + i % 4
    return (source == j).astype(F32).astype(BF)


def block_tokens(ref, first, count):
    return jnp.concatenate(
        [ref[first : first + count, l * D : (l + 1) * D] for l in range(LATENT)], axis=0
    )


def first_kernel(x, project, scale, output, gain, y, top, bottom, px):
    order = column_order(True)
    px[...] = matmul(order, x[...]).astype(BF)
    blocks, masks, srow = head_blocks(), lane_masks(), scale_row(scale)
    for w in range(2):
        tokens = jnp.concatenate(
            [block_tokens(px, ch * 64 + w * 32, 32) for ch in range(2)], axis=0
        )
        q = matmul(tokens, project[:, 0:D])
        q = (direction(q, blocks) * srow).astype(BF)
        k = direction(matmul(tokens, project[:, D : 2 * D]), blocks).astype(BF)
        v = matmul(tokens, project[:, 2 * D : 3 * D]).astype(BF)
        mixture = attend(q, k, v, masks, None)
        done = finish(tokens, mixture, output[...], gain[...]).astype(BF)
        for ch in range(2):
            for l in range(LATENT):
                at = (ch * LATENT + l) * 32
                lanes = slice(l * D, (l + 1) * D)
                y[ch * 64 + w * 32 : ch * 64 + w * 32 + 32, lanes] = done[at : at + 32]
                if w == 0:
                    top[ch * 16 : ch * 16 + 16, lanes] = done[at : at + 16]
                else:
                    bottom[ch * 16 : ch * 16 + 16, lanes] = done[at + 16 : at + 32]


def second_kernel(
    west, own, east, edges, project, scale, output, gain, out, keys, values, done
):
    blocks, masks, srow = head_blocks(), lane_masks(), scale_row(scale)
    pieces = [west, own.at[0], own.at[1], east]
    for p, piece in enumerate(pieces):
        for a in range(3):
            tokens = block_tokens(piece, a * 32, 32)
            k = matmul(tokens, project[:, D : 2 * D])
            keys[p, a] = direction(k, blocks).astype(BF)
            values[p, a] = matmul(tokens, project[:, 2 * D : 3 * D]).astype(BF)
    row = (iota((256, LANES), 0) % 32) // 4
    first = jnp.where((row >= HALF) | (edges[0] == 0), 1.0, 0.0).astype(BF)
    last = jnp.where((row < HALF) | (edges[1] == 0), 1.0, 0.0).astype(BF)
    alive = [first, None, last]
    for ch in range(2):
        for a, (begin, count) in enumerate(((16, 16), (32, 32), (64, 16))):
            tokens = block_tokens(own.at[ch], begin, count)
            q = (direction(matmul(tokens, project[:, 0:D]), blocks) * srow).astype(BF)
            k = jnp.concatenate([keys[2 * ch, a], keys[2 * ch + 1, a]], axis=0)
            v = jnp.concatenate([values[2 * ch, a], values[2 * ch + 1, a]], axis=0)
            mixture = attend(q, k, v, masks, alive[a])
            result = finish(tokens, mixture, output[...], gain[...]).astype(BF)
            for l in range(LATENT):
                at = ch * 64 + begin - 16
                done[at : at + count, l * D : (l + 1) * D] = result[l * count : (l + 1) * count]
    out[...] = matmul(column_order(False), done[...]).astype(BF)


VMEM = pl.BlockSpec(memory_space=pltpu.VMEM)
SMEM = pl.BlockSpec(memory_space=pltpu.SMEM)
MIB = 1024 * 1024


def shifted(value, axis, by):
    size = lax.axis_size(axis)
    return lax.ppermute(value, axis, [(i, (i + by) % size) for i in range(size)])


def encode_call(stripe, embed_weight, level_code, encoder_gain, key_weight, value_weight,
                latent_query, encoder_scale, latent_weight, latent_base):
    return pl.pallas_call(
        encode_kernel,
        out_shape=jax.ShapeDtypeStruct((128, LATENT * D), BF),
        in_specs=[VMEM] * 7 + [SMEM] + [VMEM] * 2,
        out_specs=VMEM,
        scratch_shapes=[
            pltpu.VMEM((256, LEVELS * LANES), BF),
            pltpu.VMEM((128, D), F32),
            pltpu.VMEM((3 * D + 64, 256), BF),
            pltpu.VMEM((LEVELS, D, LANES), F32),
            pltpu.VMEM((LEVELS + 1, 64, LANES), F32),
            pltpu.VMEM((LATENT, D, LANES), BF),
        ],
        compiler_params=pltpu.CompilerParams(vmem_limit_bytes=32 * MIB),
        name="encode",
    )(stripe, embed_weight, level_code, encoder_gain.reshape(1, D), key_weight, value_weight,
      latent_query, encoder_scale, latent_weight, latent_base)


def first_call(x, project, scale, output, gain):
    rows = jax.ShapeDtypeStruct((32, LATENT * D), BF)
    return pl.pallas_call(
        first_kernel,
        out_shape=[jax.ShapeDtypeStruct((128, LATENT * D), BF), rows, rows],
        in_specs=[VMEM, VMEM, SMEM, VMEM, VMEM],
        out_specs=[VMEM] * 3,
        scratch_shapes=[pltpu.VMEM((128, LATENT * D), BF)],
        compiler_params=pltpu.CompilerParams(vmem_limit_bytes=32 * MIB),
        name="first_layer",
    )(x, project, scale, output, gain.reshape(1, D))


def second_call(west, own, east, edges, project, scale, output, gain):
    return pl.pallas_call(
        second_kernel,
        out_shape=jax.ShapeDtypeStruct((128, LATENT * D), BF),
        in_specs=[VMEM, VMEM, VMEM, SMEM, VMEM, SMEM, VMEM, VMEM],
        out_specs=VMEM,
        scratch_shapes=[
            pltpu.VMEM((4, 3, 128, D), BF),
            pltpu.VMEM((4, 3, 128, D), BF),
            pltpu.VMEM((128, LATENT * D), BF),
        ],
        compiler_params=pltpu.CompilerParams(vmem_limit_bytes=32 * MIB),
        name="second_layer",
    )(west, own, east, edges, project, scale, output, gain.reshape(1, D))


def per_device(
    fields,
    embed_weight,
    level_code,
    encoder_gain,
    key_weight,
    value_weight,
    latent_query,
    encoder_scale,
    latent_weight,
    latent_base,
    first_project,
    first_scale,
    first_output,
    first_gain,
    second_project,
    second_scale,
    second_output,
    second_gain,
):
    encoded = encode_call(
        fields.reshape(LEVELS, PV, LANES), embed_weight, level_code, encoder_gain, key_weight,
        value_weight, latent_query, encoder_scale, latent_weight, latent_base,
    )
    tile = lax.all_to_all(encoded, "lon", split_axis=0, concat_axis=0, tiled=True)
    middle, top, bottom = first_call(tile, first_project, first_scale, first_output, first_gain)
    below = shifted(top, "lat", -1)
    above = shifted(bottom, "lat", 1)
    own = jnp.concatenate(
        [above.reshape(2, 16, -1), middle.reshape(2, 64, -1), below.reshape(2, 16, -1)], axis=1
    )
    east = shifted(own[0], "lon", -1)
    west = shifted(own[1], "lon", 1)
    lat = lax.axis_index("lat")
    edges = jnp.stack([lat == 0, lat == lax.axis_size("lat") - 1]).astype(jnp.int32)
    out = second_call(
        west, own, east, edges, second_project, second_scale, second_output, second_gain
    )
    return out.reshape(16, 8, LATENT, D)


def solution(mesh):
    in_specs = (P("lat", "lon", None, None, None),) + (P(),) * 17
    out_specs = P("lat", "lon", None, None)
    return jax.shard_map(
        per_device, mesh=mesh, in_specs=in_specs, out_specs=out_specs, check_vma=False
    )
```

```python
import jax
import jax.numpy as jnp
from jax import lax
from jax.experimental import pallas as pl
from jax.experimental.pallas import tpu as pltpu
from jax.sharding import PartitionSpec as P

D = 512
HEADS = 16
LEVELS = 13
LATENT = 4
PV = 80
HEAD = 32
HALF = 4
LANES = 128
GROUPS = D // LANES
IN_GROUP = LANES // HEAD
NORM_EPS = 1e-05
DIR_EPS = 1e-06
LOG2E = 1.4426950408889634
BF = jnp.bfloat16
F32 = jnp.float32
ENC_SPANS = [(256 * i, 256) for i in range(6)] + [(1536, 128)]


def iota(shape, dim):
    return lax.broadcasted_iota(jnp.int32, shape, dim)


def matmul(a, b):
    return jnp.dot(a, b, preferred_element_type=F32)


def matmul_nt(a, b):
    return lax.dot_general(a, b, (((1,), (1,)), ((), ())), preferred_element_type=F32)


def matmul_tn(a, b):
    return lax.dot_general(a, b, (((0,), (0,)), ((), ())), preferred_element_type=F32)


def halves(value):
    high = value.astype(BF)
    return high, (value - high.astype(F32)).astype(BF)


def scale_row(scale_ref):
    head = iota((1, D), 1) // HEAD
    row = jnp.zeros((1, D), F32)
    for h in range(HEADS):
        row = jnp.where(head == h, scale_ref[h] * LOG2E, row)
    return row


def head_blocks():
    return (iota((256, 256), 0) // HEAD == iota((256, 256), 1) // HEAD).astype(F32).astype(BF)


def head_squares(value, blocks):
    square = (value * value).astype(BF)
    return jnp.concatenate(
        [matmul(square[:, i : i + 256], blocks) for i in range(0, D, 256)], axis=1
    )


def direction(value, blocks):
    return value * lax.rsqrt(head_squares(value, blocks) + DIR_EPS)


def lane_masks():
    head = iota((1, LANES), 1) // HEAD
    return [(head == h).astype(F32).astype(BF) for h in range(IN_GROUP)]


def attend(queries, keys, values, masks, alive):
    count = queries.shape[0]
    tokens = keys.shape[0]
    head = iota((count, LANES), 1) // HEAD
    ones = jnp.ones((tokens, LANES), BF) if alive is None else alive
    parts = []
    for g in range(GROUPS):
        lanes = slice(g * LANES, (g + 1) * LANES)
        q, k, v = queries[:, lanes], keys[:, lanes], values[:, lanes]
        if alive is not None:
            v = v * alive
        stacked = jnp.concatenate([q * m for m in masks], axis=0)
        weight = jnp.exp2(matmul_nt(stacked, k)).astype(BF)
        both = matmul(weight, jnp.concatenate([v, ones], axis=1))
        picked = both[:count]
        over, under = picked[:, :LANES], picked[:, LANES:]
        for h in range(1, IN_GROUP):
            block = both[h * count : (h + 1) * count]
            over = jnp.where(head == h, block[:, :LANES], over)
            under = jnp.where(head == h, block[:, LANES:], under)
        parts.append((over / under).astype(BF))
    return jnp.concatenate(parts, axis=1)


def finish(tokens, mixture, output, gain):
    branch = matmul(mixture, output)
    centre = branch - jnp.mean(branch, axis=-1, keepdims=True)
    spread = jnp.mean(centre * centre, axis=-1, keepdims=True)
    return tokens.astype(F32) + centre * lax.rsqrt(spread + NORM_EPS) * gain


def encode_kernel(*refs):
    sources, out, landed = refs[:10], refs[10], refs[11:21]
    f2, wide, mats, vals, wts, mix, sems = refs[21:]
    copies = [
        pltpu.make_async_copy(source, target, sems.at[i])
        for i, (source, target) in enumerate(zip(sources, landed))
    ]
    fields, embed, code, gain, key_w, value_w, query, scale, latent_w, base = landed
    for i in (1, 2, 3, 4, 5, 6, 7, 0, 8, 9):
        copies[i].start()
    for i in (1, 2, 3, 4, 5, 6, 7, 0, 8, 9):
        copies[i].wait()
    wide[...] = jnp.zeros((128, D), F32)
    w = embed[...].astype(F32)
    wide[0:PV] = w - jnp.mean(w, axis=-1, keepdims=True)
    c = code[...]
    wide[PV : PV + LEVELS] = c - jnp.mean(c, axis=-1, keepdims=True)
    centred = wide[...]
    high, low = halves(centred * gain[...])
    both = jnp.concatenate([high, low], axis=0)
    for i, weight in enumerate((key_w, value_w)):
        product = matmul(both, weight[...])
        product = product[:128] + product[128:]
        h, l = halves(product.T)
        mats[i * D : (i + 1) * D] = jnp.concatenate([h, l], axis=1)
        if i == 0:
            own = iota((HEADS, D), 1) // HEAD == iota((HEADS, D), 0)
            rows = jnp.concatenate(
                [jnp.where(own, query[l : l + 1, :], 0.0) for l in range(LATENT)], axis=0
            )
            length = jnp.sum(rows * rows, axis=-1, keepdims=True) + DIR_EPS
            rows = (rows * lax.rsqrt(length) * scale_row(scale)).astype(BF)
            kh, kl = halves(product)
            raw = matmul_nt(rows, kh) + matmul_nt(rows, kl)
            h, l = halves(raw)
            mats[3 * D : 3 * D + 64] = jnp.concatenate([h, l], axis=1)
    h, l = halves(centred.T)
    mats[2 * D : 3 * D] = jnp.concatenate([h, l], axis=1)

    level = (iota((48, LEVELS * LANES), 0) == iota((48, LEVELS * LANES), 1) // LANES)
    level = level.astype(F32).astype(BF)
    for top in (0, 128):
        f2[top + PV : top + 128, :] = level
        for k in range(LEVELS):
            f2[top : top + PV, k * LANES : (k + 1) * LANES] = fields[k]

    gather = (iota((HEADS, 128), 1) // 8 == iota((HEADS, 128), 0)).astype(F32).astype(BF)
    total = jnp.zeros((64, LANES), F32)
    for start, width in ENC_SPANS:
        rhs = f2[:, start : start + width]
        keys = matmul(mats[0:D], rhs)
        part = jnp.sum((keys * keys).reshape(HEADS, 4, 8, width), axis=1).reshape(128, width)
        squares = matmul(gather, part.astype(BF))
        centre = matmul(mats[2 * D : 3 * D], rhs)
        part = jnp.sum((centre * centre).reshape(64, 8, width), axis=0)
        spread = jnp.sum(part, axis=0, keepdims=True) * (1.0 / D) + NORM_EPS
        factor = lax.rsqrt(squares + DIR_EPS * spread)
        scores = matmul(mats[3 * D : 3 * D + 64], rhs) * jnp.concatenate([factor] * LATENT, axis=0)
        weights = jnp.exp2(scores)
        scaled = weights * lax.rsqrt(spread)
        values = matmul(mats[D : 2 * D], rhs)
        for i in range(width // LANES):
            k = start // LANES + i
            lanes = slice(i * LANES, (i + 1) * LANES)
            total = total + weights[:, lanes]
            wts[k] = scaled[:, lanes]
            vals[k] = values[:, lanes]
    wts[LEVELS] = 1.0 / total

    for h in range(HEADS):
        rows = slice(h * HEAD, (h + 1) * HEAD)
        sums = [jnp.zeros((HEAD, LANES), F32) for _ in range(LATENT)]
        for k in range(LEVELS):
            v = vals[k, rows, :]
            for l in range(LATENT):
                sums[l] = sums[l] + wts[k, l * HEADS + h : l * HEADS + h + 1, :] * v
        for l in range(LATENT):
            r = wts[LEVELS, l * HEADS + h : l * HEADS + h + 1, :]
            mix[l, rows, :] = (sums[l] * r).astype(BF)
    for l in range(LATENT):
        merged = matmul_tn(mix[l], latent_w[...]) + base[l : l + 1, :]
        out[:, l * D : (l + 1) * D] = merged.astype(BF)


def halves_order():
    i, j = iota((128, 128), 0), iota((128, 128), 1)
    source = ((i % 64) // 4) * 8 + (i // 64) * 4 + i % 4
    return (source == j).astype(F32).astype(BF)


def natural_order(rows):
    size = rows * 32
    i, j = iota((size, size), 0), iota((size, size), 1)
    half, column, level = (i % 32) // 16, (i % 16) // 4, i % 4
    source = half * (16 * rows) + level * (4 * rows) + (i // 32) * 4 + column
    return (source == j).astype(F32).astype(BF)


def block_tokens(ref, first, count):
    return [ref[first : first + count, l * D : (l + 1) * D] for l in range(LATENT)]


def project_keys(tokens, project, blocks):
    k = direction(matmul(tokens, project[:, D : 2 * D]), blocks).astype(BF)
    return k, matmul(tokens, project[:, 2 * D : 3 * D]).astype(BF)


def project_queries(tokens, project, blocks, srow):
    return (direction(matmul(tokens, project[:, 0:D]), blocks) * srow).astype(BF)


def first_edges_kernel(x, project, scale, output, gain, top, bottom, tokens, keys, values, px):
    px[...] = matmul(halves_order(), x[...]).astype(BF)
    blocks, masks, srow = head_blocks(), lane_masks(), scale_row(scale)
    for w in range(2):
        for ch in range(2):
            at = (w * 2 + ch) * 128
            tokens[at : at + 128] = jnp.concatenate(block_tokens(px, ch * 64 + w * 32, 32), axis=0)
    keys[...], values[...] = project_keys(tokens[...], project, blocks)
    edge = jnp.concatenate(
        [tokens[b * 32 + (b // 8) * 16 : b * 32 + (b // 8) * 16 + 16] for b in range(16)], axis=0
    )
    q = project_queries(edge, project, blocks, srow)
    mixture = jnp.concatenate(
        [
            attend(
                q[w * 128 : w * 128 + 128],
                keys[w * 256 : w * 256 + 256],
                values[w * 256 : w * 256 + 256],
                masks,
                None,
            )
            for w in range(2)
        ],
        axis=0,
    )
    done = finish(edge, mixture, output[...], gain[...]).astype(BF)
    for w, ref in enumerate((top, bottom)):
        for ch in range(2):
            for l in range(LATENT):
                at = ((w * 2 + ch) * LATENT + l) * 16
                ref[ch * 16 : ch * 16 + 16, l * D : (l + 1) * D] = done[at : at + 16]


def first_middle_kernel(tokens, keys, values, project, scale, output, gain, middle):
    blocks, masks, srow = head_blocks(), lane_masks(), scale_row(scale)
    inner = jnp.concatenate(
        [tokens[b * 32 + 16 - (b // 8) * 16 : b * 32 + 32 - (b // 8) * 16] for b in range(16)],
        axis=0,
    )
    q = project_queries(inner, project, blocks, srow)
    mixture = jnp.concatenate(
        [
            attend(
                q[w * 128 : w * 128 + 128],
                keys[w * 256 : w * 256 + 256],
                values[w * 256 : w * 256 + 256],
                masks,
                None,
            )
            for w in range(2)
        ],
        axis=0,
    )
    done = finish(inner, mixture, output[...], gain[...]).astype(BF)
    for w in range(2):
        for ch in range(2):
            for l in range(LATENT):
                at = ((w * 2 + ch) * LATENT + l) * 16
                to = ch * 32 + w * 16
                middle[to : to + 16, l * D : (l + 1) * D] = done[at : at + 16]


def second_own_kernel(own0, own1, project, scale, queries, tokens, keys, values):
    blocks, srow = head_blocks(), scale_row(scale)
    own = (own0, own1)
    full = jnp.concatenate(
        [t for ref in own for a in range(3) for t in block_tokens(ref, a * 32, 32)], axis=0
    )
    keys[...], values[...] = project_keys(full, project, blocks)
    mine = jnp.concatenate(
        [
            t
            for begin, count in ((16, 16), (32, 32), (64, 16))
            for ref in own
            for t in block_tokens(ref, begin, count)
        ],
        axis=0,
    )
    tokens[...] = mine
    queries[...] = project_queries(mine, project, blocks, srow)


def second_kernel(
    west, east, queries, tokens, keys, values, edges, project, output, gain, out, k2, v2, mix
):
    blocks, masks = head_blocks(), lane_masks()
    full = jnp.concatenate(
        [t for ref in (west, east) for a in range(3) for t in block_tokens(ref, a * 32, 32)],
        axis=0,
    )
    k2[...], v2[...] = project_keys(full, project, blocks)
    row = (iota((256, LANES), 0) % 32) // 4
    first = jnp.where((row >= HALF) | (edges[0] == 0), 1.0, 0.0).astype(BF)
    last = jnp.where((row < HALF) | (edges[1] == 0), 1.0, 0.0).astype(BF)
    alive = [first, None, last]
    at = 0
    for a, count in enumerate((64, 128, 64)):
        for ch in range(2):
            rows = slice((ch * 3 + a) * 128, (ch * 3 + a) * 128 + 128)
            k = jnp.concatenate([keys[rows], k2[rows]], axis=0)
            v = jnp.concatenate([values[rows], v2[rows]], axis=0)
            mix[at : at + count] = attend(queries[at : at + count], k, v, masks, alive[a])
            at += count
    result = finish(tokens[...], mix[...], output[...], gain[...]).astype(BF)
    narrow, broad = natural_order(4), natural_order(8)
    for first, count, order in ((0, 128, narrow), (128, 256, broad), (384, 128, narrow)):
        block = matmul(order, result[first : first + count])
        block = block.reshape(count // LATENT, LATENT, D).astype(BF)
        out[first // LATENT : (first + count) // LATENT] = block


VMEM = pl.BlockSpec(memory_space=pltpu.VMEM)
SMEM = pl.BlockSpec(memory_space=pltpu.SMEM)
MIB = 1024 * 1024


def shifted(value, axis, by):
    size = lax.axis_size(axis)
    return lax.ppermute(value, axis, [(i, (i + by) % size) for i in range(size)])


def params(mib):
    return pltpu.CompilerParams(vmem_limit_bytes=mib * MIB)


def cost(flops, exps):
    return pl.CostEstimate(flops=flops, bytes_accessed=4 * MIB, transcendentals=exps)


def wide_rows(count):
    return jax.ShapeDtypeStruct((count, LATENT * D), BF)


def token_rows(count):
    return jax.ShapeDtypeStruct((count, D), BF)


def encode_call(stripe, embed_weight, level_code, encoder_gain, key_weight, value_weight,
                latent_query, encoder_scale, latent_weight, latent_base):
    operands = (stripe, embed_weight, level_code, encoder_gain.reshape(1, D), key_weight,
                value_weight, latent_query, encoder_scale, latent_weight, latent_base)
    return pl.pallas_call(
        encode_kernel,
        out_shape=wide_rows(128),
        in_specs=[pl.BlockSpec(memory_space=pltpu.HBM)] * len(operands),
        out_specs=VMEM,
        scratch_shapes=[
            (pltpu.SMEM if x.shape == (HEADS,) else pltpu.VMEM)(x.shape, x.dtype) for x in operands
        ]
        + [
            pltpu.VMEM((256, LEVELS * LANES), BF),
            pltpu.VMEM((128, D), F32),
            pltpu.VMEM((3 * D + 64, 256), BF),
            pltpu.VMEM((LEVELS, D, LANES), F32),
            pltpu.VMEM((LEVELS + 1, 64, LANES), F32),
            pltpu.VMEM((LATENT, D, LANES), BF),
            pltpu.SemaphoreType.DMA((len(operands),)),
        ],
        compiler_params=params(62),
        name="encode",
    )(*operands)


def first_edges_call(x, project, scale, output, gain):
    return pl.pallas_call(
        first_edges_kernel,
        out_shape=[wide_rows(32)] * 2 + [token_rows(512)] * 3,
        in_specs=[VMEM, VMEM, SMEM, VMEM, VMEM],
        out_specs=[VMEM] * 5,
        scratch_shapes=[pltpu.VMEM((128, LATENT * D), BF)],
        compiler_params=params(24),
        name="first_edges",
    )(x, project, scale, output, gain)


def first_middle_call(tokens, keys, values, project, scale, output, gain):
    return pl.pallas_call(
        first_middle_kernel,
        out_shape=wide_rows(64),
        in_specs=[VMEM] * 4 + [SMEM, VMEM, VMEM],
        out_specs=VMEM,
        compiler_params=params(24),
        cost_estimate=cost(2 * 256 * D * D * 6, 256 * 256 * HEADS),
        name="first_middle",
    )(tokens, keys, values, project, scale, output, gain)


def second_own_call(own0, own1, project, scale):
    return pl.pallas_call(
        second_own_kernel,
        out_shape=[token_rows(512)] * 2 + [token_rows(768)] * 2,
        in_specs=[VMEM] * 3 + [SMEM],
        out_specs=[VMEM] * 4,
        compiler_params=params(24),
        cost_estimate=cost(2 * 768 * D * D * 4, 768 * D),
        name="second_own",
    )(own0, own1, project, scale)


def second_call(west, east, queries, tokens, keys, values, edges, project, output, gain):
    return pl.pallas_call(
        second_kernel,
        out_shape=jax.ShapeDtypeStruct((128, LATENT, D), BF),
        in_specs=[VMEM] * 6 + [SMEM, VMEM, VMEM, VMEM],
        out_specs=VMEM,
        scratch_shapes=[pltpu.VMEM((768, D), BF)] * 2 + [pltpu.VMEM((512, D), BF)],
        compiler_params=params(24),
        name="second_layer",
    )(west, east, queries, tokens, keys, values, edges, project, output, gain)


def per_device(
    fields,
    embed_weight,
    level_code,
    encoder_gain,
    key_weight,
    value_weight,
    latent_query,
    encoder_scale,
    latent_weight,
    latent_base,
    first_project,
    first_scale,
    first_output,
    first_gain,
    second_project,
    second_scale,
    second_output,
    second_gain,
):
    encoded = encode_call(
        fields.reshape(LEVELS, PV, LANES), embed_weight, level_code, encoder_gain, key_weight,
        value_weight, latent_query, encoder_scale, latent_weight, latent_base,
    )
    tile = lax.all_to_all(encoded, "lon", split_axis=0, concat_axis=0, tiled=True)
    gain = first_gain.reshape(1, D)
    top, bottom, tokens, keys, values = first_edges_call(
        tile, first_project, first_scale, first_output, gain
    )
    below = shifted(top, "lat", -1)
    above = shifted(bottom, "lat", 1)
    middle = first_middle_call(
        tokens, keys, values, first_project, first_scale, first_output, gain
    )
    own = [
        jnp.concatenate(
            [x[i * n : (i + 1) * n] for x, n in
             ((above, 16), (top, 16), (middle, 32), (bottom, 16), (below, 16))],
            axis=0,
        )
        for i in range(2)
    ]
    east = shifted(own[0], "lon", -1)
    west = shifted(own[1], "lon", 1)
    queries, tokens, keys, values = second_own_call(*own, second_project, second_scale)
    lat = lax.axis_index("lat")
    edges = jnp.stack([lat == 0, lat == lax.axis_size("lat") - 1]).astype(jnp.int32)
    out = second_call(
        west, east, queries, tokens, keys, values, edges, second_project, second_output,
        second_gain.reshape(1, D),
    )
    return out.reshape(16, 8, LATENT, D)


def solution(mesh):
    in_specs = (P("lat", "lon", None, None, None),) + (P(),) * 17
    out_specs = P("lat", "lon", None, None)
    return jax.shard_map(
        per_device, mesh=mesh, in_specs=in_specs, out_specs=out_specs, check_vma=False
    )
```

```python
import jax
import jax.numpy as jnp
from jax import lax
from jax.experimental import pallas as pl
from jax.experimental.pallas import tpu as pltpu
from jax.sharding import PartitionSpec as P

D = 512
HEADS = 16
LEVELS = 13
LATENT = 4
PV = 80
HEAD = 32
HALF = 4
LANES = 128
GROUPS = D // LANES
IN_GROUP = LANES // HEAD
NORM_EPS = 1e-05
DIR_EPS = 1e-06
LOG2E = 1.4426950408889634
BF = jnp.bfloat16
F32 = jnp.float32
ENC_SPANS = [(256 * i, 256) for i in range(6)] + [(1536, 128)]


def iota(shape, dim):
    return lax.broadcasted_iota(jnp.int32, shape, dim)


def matmul(a, b):
    return jnp.dot(a, b, preferred_element_type=F32)


def matmul_nt(a, b):
    return lax.dot_general(a, b, (((1,), (1,)), ((), ())), preferred_element_type=F32)


def matmul_tn(a, b):
    return lax.dot_general(a, b, (((0,), (0,)), ((), ())), preferred_element_type=F32)


def halves(value):
    high = value.astype(BF)
    return high, (value - high.astype(F32)).astype(BF)


def scale_row(scale_ref):
    head = iota((1, D), 1) // HEAD
    row = jnp.zeros((1, D), F32)
    for h in range(HEADS):
        row = jnp.where(head == h, scale_ref[h] * LOG2E, row)
    return row


def head_blocks():
    return (iota((256, 256), 0) // HEAD == iota((256, 256), 1) // HEAD).astype(F32).astype(BF)


def head_squares(value, blocks):
    square = (value * value).astype(BF)
    return jnp.concatenate(
        [matmul(square[:, i : i + 256], blocks) for i in range(0, D, 256)], axis=1
    )


def direction(value, blocks):
    return value * lax.rsqrt(head_squares(value, blocks) + DIR_EPS)


def lane_masks():
    head = iota((1, LANES), 1) // HEAD
    return [(head == h).astype(F32).astype(BF) for h in range(IN_GROUP)]


def attend(queries, keys, values, masks, alive):
    count = queries.shape[0]
    tokens = keys.shape[0]
    head = iota((count, LANES), 1) // HEAD
    ones = jnp.ones((tokens, LANES), BF) if alive is None else alive
    parts = []
    for g in range(GROUPS):
        lanes = slice(g * LANES, (g + 1) * LANES)
        q, k, v = queries[:, lanes], keys[:, lanes], values[:, lanes]
        if alive is not None:
            v = v * alive
        stacked = jnp.concatenate([q * m for m in masks], axis=0)
        weight = jnp.exp2(matmul_nt(stacked, k)).astype(BF)
        both = matmul(weight, jnp.concatenate([v, ones], axis=1))
        picked = both[:count]
        over, under = picked[:, :LANES], picked[:, LANES:]
        for h in range(1, IN_GROUP):
            block = both[h * count : (h + 1) * count]
            over = jnp.where(head == h, block[:, :LANES], over)
            under = jnp.where(head == h, block[:, LANES:], under)
        parts.append((over / under).astype(BF))
    return jnp.concatenate(parts, axis=1)


def finish(tokens, mixture, output, gain):
    branch = matmul(mixture, output)
    centre = branch - jnp.mean(branch, axis=-1, keepdims=True)
    spread = jnp.mean(centre * centre, axis=-1, keepdims=True)
    return tokens.astype(F32) + centre * lax.rsqrt(spread + NORM_EPS) * gain


def encode_kernel(*refs):
    sources, out, landed = refs[:10], refs[10], refs[11:21]
    f2, wide, mats, vals, wts, mix, sems = refs[21:]
    copies = [
        pltpu.make_async_copy(source, target, sems.at[i])
        for i, (source, target) in enumerate(zip(sources, landed))
    ]
    fields, embed, code, gain, key_w, value_w, query, scale, latent_w, base = landed
    for i in (1, 2, 3, 4, 6, 7, 5, 0, 8, 9):
        copies[i].start()
    for i in (1, 2, 3):
        copies[i].wait()
    wide[...] = jnp.zeros((128, D), F32)
    w = embed[...].astype(F32)
    wide[0:PV] = w - jnp.mean(w, axis=-1, keepdims=True)
    c = code[...]
    wide[PV : PV + LEVELS] = c - jnp.mean(c, axis=-1, keepdims=True)
    centred = wide[...]
    high, low = halves(centred * gain[...])
    both = jnp.concatenate([high, low], axis=0)
    for i, weight in enumerate((key_w, value_w)):
        for j in ((4, 6, 7), (5,))[i]:
            copies[j].wait()
        product = matmul(both, weight[...])
        product = product[:128] + product[128:]
        h, l = halves(product.T)
        mats[i * D : (i + 1) * D] = jnp.concatenate([h, l], axis=1)
        if i == 0:
            own = iota((HEADS, D), 1) // HEAD == iota((HEADS, D), 0)
            rows = jnp.concatenate(
                [jnp.where(own, query[l : l + 1, :], 0.0) for l in range(LATENT)], axis=0
            )
            length = jnp.sum(rows * rows, axis=-1, keepdims=True) + DIR_EPS
            rows = (rows * lax.rsqrt(length) * scale_row(scale)).astype(BF)
            kh, kl = halves(product)
            raw = matmul_nt(rows, kh) + matmul_nt(rows, kl)
            h, l = halves(raw)
            mats[3 * D : 3 * D + 64] = jnp.concatenate([h, l], axis=1)
    h, l = halves(centred.T)
    mats[2 * D : 3 * D] = jnp.concatenate([h, l], axis=1)

    copies[0].wait()
    level = (iota((48, LEVELS * LANES), 0) == iota((48, LEVELS * LANES), 1) // LANES)
    level = level.astype(F32).astype(BF)
    for top in (0, 128):
        f2[top + PV : top + 128, :] = level
        for k in range(LEVELS):
            f2[top : top + PV, k * LANES : (k + 1) * LANES] = fields[k]

    gather = (iota((HEADS, 128), 1) // 8 == iota((HEADS, 128), 0)).astype(F32).astype(BF)
    total = jnp.zeros((64, LANES), F32)
    for start, width in ENC_SPANS:
        rhs = f2[:, start : start + width]
        keys = matmul(mats[0:D], rhs)
        part = jnp.sum((keys * keys).reshape(HEADS, 4, 8, width), axis=1).reshape(128, width)
        squares = matmul(gather, part.astype(BF))
        centre = matmul(mats[2 * D : 3 * D], rhs)
        part = jnp.sum((centre * centre).reshape(64, 8, width), axis=0)
        spread = jnp.sum(part, axis=0, keepdims=True) * (1.0 / D) + NORM_EPS
        factor = lax.rsqrt(squares + DIR_EPS * spread)
        scores = matmul(mats[3 * D : 3 * D + 64], rhs) * jnp.concatenate([factor] * LATENT, axis=0)
        weights = jnp.exp2(scores)
        scaled = weights * lax.rsqrt(spread)
        values = matmul(mats[D : 2 * D], rhs)
        for i in range(width // LANES):
            k = start // LANES + i
            lanes = slice(i * LANES, (i + 1) * LANES)
            total = total + weights[:, lanes]
            wts[k] = scaled[:, lanes]
            vals[k] = values[:, lanes]
    wts[LEVELS] = 1.0 / total

    copies[8].wait()
    copies[9].wait()
    for h in range(HEADS):
        rows = slice(h * HEAD, (h + 1) * HEAD)
        sums = [jnp.zeros((HEAD, LANES), F32) for _ in range(LATENT)]
        for k in range(LEVELS):
            v = vals[k, rows, :]
            for l in range(LATENT):
                sums[l] = sums[l] + wts[k, l * HEADS + h : l * HEADS + h + 1, :] * v
        for l in range(LATENT):
            r = wts[LEVELS, l * HEADS + h : l * HEADS + h + 1, :]
            mix[l, rows, :] = (sums[l] * r).astype(BF)
    for l in range(LATENT):
        merged = matmul_tn(mix[l], latent_w[...]) + base[l : l + 1, :]
        out[:, l * D : (l + 1) * D] = merged.astype(BF)


def halves_order():
    i, j = iota((128, 128), 0), iota((128, 128), 1)
    source = ((i % 64) // 4) * 8 + (i // 64) * 4 + i % 4
    return (source == j).astype(F32).astype(BF)


def natural_order(rows):
    size = rows * 32
    i, j = iota((size, size), 0), iota((size, size), 1)
    half, column, level = (i % 32) // 16, (i % 16) // 4, i % 4
    source = half * (16 * rows) + level * (4 * rows) + (i // 32) * 4 + column
    return (source == j).astype(F32).astype(BF)


def block_tokens(ref, first, count):
    return [ref[first : first + count, l * D : (l + 1) * D] for l in range(LATENT)]


def project_keys(tokens, project, blocks):
    k = direction(matmul(tokens, project[:, D : 2 * D]), blocks).astype(BF)
    return k, matmul(tokens, project[:, 2 * D : 3 * D]).astype(BF)


def project_queries(tokens, project, blocks, srow):
    return (direction(matmul(tokens, project[:, 0:D]), blocks) * srow).astype(BF)


def first_edges_kernel(x, project, scale, output, gain, top, bottom, tokens, keys, values, px):
    px[...] = matmul(halves_order(), x[...]).astype(BF)
    blocks, masks, srow = head_blocks(), lane_masks(), scale_row(scale)
    for w in range(2):
        for ch in range(2):
            at = (w * 2 + ch) * 128
            tokens[at : at + 128] = jnp.concatenate(block_tokens(px, ch * 64 + w * 32, 32), axis=0)
    keys[...], values[...] = project_keys(tokens[...], project, blocks)
    edge = jnp.concatenate(
        [tokens[b * 32 + (b // 8) * 16 : b * 32 + (b // 8) * 16 + 16] for b in range(16)], axis=0
    )
    q = project_queries(edge, project, blocks, srow)
    mixture = jnp.concatenate(
        [
            attend(
                q[w * 128 : w * 128 + 128],
                keys[w * 256 : w * 256 + 256],
                values[w * 256 : w * 256 + 256],
                masks,
                None,
            )
            for w in range(2)
        ],
        axis=0,
    )
    done = finish(edge, mixture, output[...], gain[...]).astype(BF)
    for w, ref in enumerate((top, bottom)):
        for ch in range(2):
            for l in range(LATENT):
                at = ((w * 2 + ch) * LATENT + l) * 16
                ref[ch * 16 : ch * 16 + 16, l * D : (l + 1) * D] = done[at : at + 16]


def first_middle_kernel(
    tokens, keys, values, top, bottom, project, scale, output, gain, own0, own1
):
    own = (own0, own1)
    blocks, masks, srow = head_blocks(), lane_masks(), scale_row(scale)
    inner = jnp.concatenate(
        [tokens[b * 32 + 16 - (b // 8) * 16 : b * 32 + 32 - (b // 8) * 16] for b in range(16)],
        axis=0,
    )
    q = project_queries(inner, project, blocks, srow)
    mixture = jnp.concatenate(
        [
            attend(
                q[w * 128 : w * 128 + 128],
                keys[w * 256 : w * 256 + 256],
                values[w * 256 : w * 256 + 256],
                masks,
                None,
            )
            for w in range(2)
        ],
        axis=0,
    )
    done = finish(inner, mixture, output[...], gain[...]).astype(BF)
    for ch in range(2):
        own[ch][0:16] = top[ch * 16 : ch * 16 + 16]
        own[ch][48:64] = bottom[ch * 16 : ch * 16 + 16]
        for w in range(2):
            for l in range(LATENT):
                at = ((w * 2 + ch) * LATENT + l) * 16
                own[ch][16 + w * 16 : 32 + w * 16, l * D : (l + 1) * D] = done[at : at + 16]


PARTS = ((0, 16), (16, 32), (48, 16))


def tile_tokens(halves_of):
    return jnp.concatenate(
        [
            t
            for first, count in PARTS
            for ref in halves_of
            for t in block_tokens(ref, first, count)
        ],
        axis=0,
    )


def second_own_kernel(own0, own1, project, scale, queries, tokens, keys, values):
    blocks, srow = head_blocks(), scale_row(scale)
    tokens[...] = tile_tokens((own0, own1))
    keys[...], values[...] = project_keys(tokens[...], project, blocks)
    queries[...] = project_queries(tokens[...], project, blocks, srow)


def second_middle_kernel(
    west, east, queries, tokens, keys, values, project, output, gain, out, side_keys, side_values
):
    blocks, masks = head_blocks(), lane_masks()
    side_keys[...], side_values[...] = project_keys(tile_tokens((west, east)), project, blocks)
    mixture = jnp.concatenate(
        [
            attend(
                queries[at : at + 128],
                jnp.concatenate([keys[at : at + 128], side_keys[at : at + 128]], axis=0),
                jnp.concatenate([values[at : at + 128], side_values[at : at + 128]], axis=0),
                masks,
                None,
            )
            for at in (128, 256)
        ],
        axis=0,
    )
    result = finish(tokens[128:384], mixture, output[...], gain[...]).astype(BF)
    out[...] = matmul(natural_order(8), result).reshape(64, LATENT, D).astype(BF)


def second_outer_kernel(
    west, above, below, east, queries, tokens, keys, values, side_keys, side_values, middle, edges,
    project, output, gain, out, halo_keys, halo_values,
):
    blocks, masks = head_blocks(), lane_masks()
    out[32:96] = middle[...]
    order = [
        (above, 0), (west, 0), (above, 16), (east, 0),
        (below, 0), (west, 16), (below, 16), (east, 16),
    ]
    full = jnp.concatenate([t for ref, at in order for t in block_tokens(ref, at, 16)], axis=0)
    halo_keys[...], halo_values[...] = project_keys(full, project, blocks)
    halo = iota((256, LANES), 0) < 128
    mixtures = []
    for a, first in enumerate((0, 384)):
        alive = jnp.where(halo & (edges[a] != 0), 0.0, 1.0).astype(BF)
        for ch in range(2):
            at, far = first + ch * 64, a * 256 + ch * 128
            k = [halo_keys[far : far + 128], keys[at : at + 64], side_keys[at : at + 64]]
            v = [halo_values[far : far + 128], values[at : at + 64], side_values[at : at + 64]]
            mixtures.append(
                attend(
                    queries[at : at + 64],
                    jnp.concatenate(k, axis=0),
                    jnp.concatenate(v, axis=0),
                    masks,
                    alive,
                )
            )
    own = jnp.concatenate([tokens[0:128], tokens[384:512]], axis=0)
    mixture = jnp.concatenate(mixtures, axis=0)
    result = finish(own, mixture, output[...], gain[...]).astype(BF)
    natural = natural_order(4)
    for a, first in enumerate((0, 96)):
        block = matmul(natural, result[a * 128 : a * 128 + 128])
        out[first : first + 32] = block.reshape(32, LATENT, D).astype(BF)


VMEM = pl.BlockSpec(memory_space=pltpu.VMEM)
SMEM = pl.BlockSpec(memory_space=pltpu.SMEM)
MIB = 1024 * 1024


def shifted(value, axis, by):
    size = lax.axis_size(axis)
    return lax.ppermute(value, axis, [(i, (i + by) % size) for i in range(size)])


def params(mib):
    return pltpu.CompilerParams(vmem_limit_bytes=mib * MIB)


def cost(flops, exps):
    return pl.CostEstimate(flops=flops, bytes_accessed=4 * MIB, transcendentals=exps)


def wide_rows(count):
    return jax.ShapeDtypeStruct((count, LATENT * D), BF)


def token_rows(count):
    return jax.ShapeDtypeStruct((count, D), BF)


def encode_call(stripe, embed_weight, level_code, encoder_gain, key_weight, value_weight,
                latent_query, encoder_scale, latent_weight, latent_base):
    operands = (stripe, embed_weight, level_code, encoder_gain.reshape(1, D), key_weight,
                value_weight, latent_query, encoder_scale, latent_weight, latent_base)
    return pl.pallas_call(
        encode_kernel,
        out_shape=wide_rows(128),
        in_specs=[pl.BlockSpec(memory_space=pltpu.HBM)] * len(operands),
        out_specs=VMEM,
        scratch_shapes=[
            (pltpu.SMEM if x.shape == (HEADS,) else pltpu.VMEM)(x.shape, x.dtype) for x in operands
        ]
        + [
            pltpu.VMEM((256, LEVELS * LANES), BF),
            pltpu.VMEM((128, D), F32),
            pltpu.VMEM((3 * D + 64, 256), BF),
            pltpu.VMEM((LEVELS, D, LANES), F32),
            pltpu.VMEM((LEVELS + 1, 64, LANES), F32),
            pltpu.VMEM((LATENT, D, LANES), BF),
            pltpu.SemaphoreType.DMA((len(operands),)),
        ],
        compiler_params=params(60),
        name="encode",
    )(*operands)


def first_edges_call(x, project, scale, output, gain):
    return pl.pallas_call(
        first_edges_kernel,
        out_shape=[wide_rows(32)] * 2 + [token_rows(512)] * 3,
        in_specs=[VMEM, VMEM, SMEM, VMEM, VMEM],
        out_specs=[VMEM] * 5,
        scratch_shapes=[pltpu.VMEM((128, LATENT * D), BF)],
        compiler_params=params(24),
        name="first_edges",
    )(x, project, scale, output, gain)


def first_middle_call(tokens, keys, values, top, bottom, project, scale, output, gain):
    return pl.pallas_call(
        first_middle_kernel,
        out_shape=[wide_rows(64)] * 2,
        in_specs=[VMEM] * 6 + [SMEM, VMEM, VMEM],
        out_specs=[VMEM] * 2,
        compiler_params=params(24),
        cost_estimate=cost(2 * 256 * D * D * 6, 256 * 256 * HEADS),
        name="first_middle",
    )(tokens, keys, values, top, bottom, project, scale, output, gain)


def second_own_call(own0, own1, project, scale):
    return pl.pallas_call(
        second_own_kernel,
        out_shape=[token_rows(512)] * 4,
        in_specs=[VMEM] * 3 + [SMEM],
        out_specs=[VMEM] * 4,
        compiler_params=params(24),
        cost_estimate=cost(2 * 512 * D * D * 4, 512 * D),
        name="second_own",
    )(own0, own1, project, scale)


def second_middle_call(west, east, queries, tokens, keys, values, project, output, gain):
    return pl.pallas_call(
        second_middle_kernel,
        out_shape=[jax.ShapeDtypeStruct((64, LATENT, D), BF)] + [token_rows(512)] * 2,
        in_specs=[VMEM] * 9,
        out_specs=[VMEM] * 3,
        compiler_params=params(24),
        cost_estimate=cost(2 * 512 * D * D * 8, 256 * 256 * HEADS),
        name="second_middle",
    )(west, east, queries, tokens, keys, values, project, output, gain)


def second_outer_call(*operands):
    return pl.pallas_call(
        second_outer_kernel,
        out_shape=jax.ShapeDtypeStruct((128, LATENT, D), BF),
        in_specs=[VMEM] * 11 + [SMEM] + [VMEM] * 3,
        out_specs=VMEM,
        scratch_shapes=[pltpu.VMEM((512, D), BF)] * 2,
        compiler_params=params(24),
        name="second_outer",
    )(*operands)


def per_device(
    fields,
    embed_weight,
    level_code,
    encoder_gain,
    key_weight,
    value_weight,
    latent_query,
    encoder_scale,
    latent_weight,
    latent_base,
    first_project,
    first_scale,
    first_output,
    first_gain,
    second_project,
    second_scale,
    second_output,
    second_gain,
):
    encoded = encode_call(
        fields.reshape(LEVELS, PV, LANES), embed_weight, level_code, encoder_gain, key_weight,
        value_weight, latent_query, encoder_scale, latent_weight, latent_base,
    )
    tile = lax.all_to_all(encoded, "lon", split_axis=0, concat_axis=0, tiled=True)
    gain = first_gain.reshape(1, D)
    top, bottom, tokens, keys, values = first_edges_call(
        tile, first_project, first_scale, first_output, gain
    )
    below = shifted(top, "lat", -1)
    above = shifted(bottom, "lat", 1)
    own = first_middle_call(
        tokens, keys, values, top, bottom, first_project, first_scale, first_output, gain
    )
    east = shifted(own[0], "lon", -1)
    west = shifted(own[1], "lon", 1)
    gain = second_gain.reshape(1, D)
    queries, tokens, keys, values = second_own_call(*own, second_project, second_scale)
    corners = [
        jnp.concatenate([above[i : i + 16], below[i : i + 16]], axis=0) for i in (0, 16)
    ]
    east_corners = shifted(corners[0], "lon", -1)
    west_corners = shifted(corners[1], "lon", 1)
    middle, side_keys, side_values = second_middle_call(
        west, east, queries, tokens, keys, values, second_project, second_output, gain
    )
    lat = lax.axis_index("lat")
    edges = jnp.stack([lat == 0, lat == lax.axis_size("lat") - 1]).astype(jnp.int32)
    out = second_outer_call(
        west_corners, above, below, east_corners, queries, tokens, keys, values, side_keys,
        side_values, middle, edges, second_project, second_output, gain,
    )
    return out.reshape(16, 8, LATENT, D)


def solution(mesh):
    in_specs = (P("lat", "lon", None, None, None),) + (P(),) * 17
    out_specs = P("lat", "lon", None, None)
    return jax.shard_map(
        per_device, mesh=mesh, in_specs=in_specs, out_specs=out_specs, check_vma=False
    )
```

```python
import jax
import jax.numpy as jnp
from jax import lax
from jax.experimental import pallas as pl
from jax.experimental.pallas import tpu as pltpu
from jax.sharding import PartitionSpec as P

D = 512
HEADS = 16
LEVELS = 13
LATENT = 4
PV = 80
HEAD = 32
HALF = 4
LANES = 128
GROUPS = D // LANES
IN_GROUP = LANES // HEAD
NORM_EPS = 1e-05
DIR_EPS = 1e-06
LOG2E = 1.4426950408889634
BF = jnp.bfloat16
F32 = jnp.float32
ENC_SPANS = [(256 * i, 256) for i in range(6)] + [(1536, 128)]


def iota(shape, dim):
    return lax.broadcasted_iota(jnp.int32, shape, dim)


def matmul(a, b):
    return jnp.dot(a, b, preferred_element_type=F32)


def matmul_nt(a, b):
    return lax.dot_general(a, b, (((1,), (1,)), ((), ())), preferred_element_type=F32)


def matmul_tn(a, b):
    return lax.dot_general(a, b, (((0,), (0,)), ((), ())), preferred_element_type=F32)


def halves(value):
    high = value.astype(BF)
    return high, (value - high.astype(F32)).astype(BF)


def scale_row(scale_ref):
    head = iota((1, D), 1) // HEAD
    row = jnp.zeros((1, D), F32)
    for h in range(HEADS):
        row = jnp.where(head == h, scale_ref[h] * LOG2E, row)
    return row


def head_blocks():
    return (iota((256, 256), 0) // HEAD == iota((256, 256), 1) // HEAD).astype(F32).astype(BF)


def head_squares(value, blocks):
    square = (value * value).astype(BF)
    return jnp.concatenate(
        [matmul(square[:, i : i + 256], blocks) for i in range(0, D, 256)], axis=1
    )


def direction(value, blocks):
    return value * lax.rsqrt(head_squares(value, blocks) + DIR_EPS)


def lane_masks():
    head = iota((1, LANES), 1) // HEAD
    return [(head == h).astype(F32).astype(BF) for h in range(IN_GROUP)]


def attend(queries, keys, values, masks, alive):
    count = queries.shape[0]
    tokens = keys.shape[0]
    head = iota((count, LANES), 1) // HEAD
    ones = jnp.ones((tokens, LANES), BF) if alive is None else alive
    parts = []
    for g in range(GROUPS):
        lanes = slice(g * LANES, (g + 1) * LANES)
        q, k, v = queries[:, lanes], keys[:, lanes], values[:, lanes]
        if alive is not None:
            v = v * alive
        stacked = jnp.concatenate([q * m for m in masks], axis=0)
        weight = jnp.exp2(matmul_nt(stacked, k)).astype(BF)
        both = matmul(weight, jnp.concatenate([v, ones], axis=1))
        picked = both[:count]
        over, under = picked[:, :LANES], picked[:, LANES:]
        for h in range(1, IN_GROUP):
            block = both[h * count : (h + 1) * count]
            over = jnp.where(head == h, block[:, :LANES], over)
            under = jnp.where(head == h, block[:, LANES:], under)
        parts.append((over / under).astype(BF))
    return jnp.concatenate(parts, axis=1)


def finish(tokens, mixture, output, gain):
    branch = matmul(mixture, output)
    centre = branch - jnp.mean(branch, axis=-1, keepdims=True)
    spread = jnp.mean(centre * centre, axis=-1, keepdims=True)
    return tokens.astype(F32) + centre * lax.rsqrt(spread + NORM_EPS) * gain


def fold_kernel(*refs):
    sources, mats, landed, wide, sems = refs[:7], refs[7], refs[8:15], refs[15], refs[16]
    copies = [
        pltpu.make_async_copy(source, target, sems.at[i])
        for i, (source, target) in enumerate(zip(sources, landed))
    ]
    embed, code, gain, key_w, value_w, query, scale = landed
    for copy in copies:
        copy.start()
    for copy in copies:
        copy.wait()
    wide[...] = jnp.zeros((128, D), F32)
    w = embed[...].astype(F32)
    wide[0:PV] = w - jnp.mean(w, axis=-1, keepdims=True)
    c = code[...]
    wide[PV : PV + LEVELS] = c - jnp.mean(c, axis=-1, keepdims=True)
    centred = wide[...]
    high, low = halves(centred * gain[...])
    both = jnp.concatenate([high, low], axis=0)
    for i, weight in enumerate((key_w, value_w)):
        product = matmul(both, weight[...])
        product = product[:128] + product[128:]
        h, l = halves(product.T)
        mats[i * D : (i + 1) * D] = jnp.concatenate([h, l], axis=1)
        if i == 0:
            own = iota((HEADS, D), 1) // HEAD == iota((HEADS, D), 0)
            rows = jnp.concatenate(
                [jnp.where(own, query[l : l + 1, :], 0.0) for l in range(LATENT)], axis=0
            )
            length = jnp.sum(rows * rows, axis=-1, keepdims=True) + DIR_EPS
            rows = (rows * lax.rsqrt(length) * scale_row(scale)).astype(BF)
            kh, kl = halves(product)
            raw = matmul_nt(rows, kh) + matmul_nt(rows, kl)
            h, l = halves(raw)
            mats[3 * D : 3 * D + 64] = jnp.concatenate([h, l], axis=1)
    h, l = halves(centred.T)
    mats[2 * D : 3 * D] = jnp.concatenate([h, l], axis=1)


def encode_kernel(x, order, mats, mix, f2, flat, vals, wts):
    flat[...] = matmul(order[...], x[...]).astype(BF).T
    level = (iota((48, LEVELS * LANES), 0) == iota((48, LEVELS * LANES), 1) // LANES)
    level = level.astype(F32).astype(BF)
    for top in (0, 128):
        f2[top + PV : top + 128, :] = level
        for k in range(LEVELS):
            f2[top : top + PV, k * LANES : (k + 1) * LANES] = flat[k * PV : (k + 1) * PV]

    gather = (iota((HEADS, 128), 1) // 8 == iota((HEADS, 128), 0)).astype(F32).astype(BF)
    total = jnp.zeros((64, LANES), F32)
    for start, width in ENC_SPANS:
        rhs = f2[:, start : start + width]
        keys = matmul(mats[0:D], rhs)
        part = jnp.sum((keys * keys).reshape(HEADS, 4, 8, width), axis=1).reshape(128, width)
        squares = matmul(gather, part.astype(BF))
        centre = matmul(mats[2 * D : 3 * D], rhs)
        part = jnp.sum((centre * centre).reshape(64, 8, width), axis=0)
        spread = jnp.sum(part, axis=0, keepdims=True) * (1.0 / D) + NORM_EPS
        factor = lax.rsqrt(squares + DIR_EPS * spread)
        scores = matmul(mats[3 * D : 3 * D + 64], rhs) * jnp.concatenate([factor] * LATENT, axis=0)
        weights = jnp.exp2(scores)
        scaled = weights * lax.rsqrt(spread)
        values = matmul(mats[D : 2 * D], rhs)
        for i in range(width // LANES):
            k = start // LANES + i
            lanes = slice(i * LANES, (i + 1) * LANES)
            total = total + weights[:, lanes]
            wts[k] = scaled[:, lanes]
            vals[k] = values[:, lanes]
    wts[LEVELS] = 1.0 / total

    for h in range(HEADS):
        rows = slice(h * HEAD, (h + 1) * HEAD)
        sums = [jnp.zeros((HEAD, LANES), F32) for _ in range(LATENT)]
        for k in range(LEVELS):
            v = vals[k, rows, :]
            for l in range(LATENT):
                sums[l] = sums[l] + wts[k, l * HEADS + h : l * HEADS + h + 1, :] * v
        for l in range(LATENT):
            r = wts[LEVELS, l * HEADS + h : l * HEADS + h + 1, :]
            mix[l, rows, :] = (sums[l] * r).astype(BF)


def parities():
    lat, lon = lax.axis_index("lat"), lax.axis_index("lon")
    return lax.rem(lat, 2), lax.rem(lon, 2)


def one_hot(source, size):
    return (source == iota((size, size), 1)).astype(F32).astype(BF)


def tile_order():
    odd_lat, odd_lon = parities()
    i = iota((128, 128), 0)
    half, side, inner, row, column = i // 64, (i // 32) % 2, (i // 16) % 2, (i // 4) % 4, i % 4
    start = jnp.where(side == 1 - odd_lat, 4 * inner, 12 - 4 * inner)
    right = jnp.where(odd_lon == 1, half, 1 - half)
    return one_hot((start + row) * 8 + right * 4 + column, 128)


def edge_order():
    odd_lat, odd_lon = parities()
    i = iota((128, 128), 0)
    row, right, column, level = i // 32, (i // 16) % 2, (i // 4) % 4, i % 4
    half = jnp.where(odd_lon == 1, right, 1 - right)
    return one_hot(half * 64 + level * 16 + row * 4 + column, 128)


def middle_order():
    odd_lat, odd_lon = parities()
    i = iota((256, 256), 0)
    window, row, right = i // 128, (i // 32) % 4, (i // 16) % 2
    column, level = (i // 4) % 4, i % 4
    half = jnp.where(odd_lon == 1, right, 1 - right)
    side = jnp.where(odd_lat == 1, window, 1 - window)
    return one_hot(half * 128 + level * 32 + side * 16 + row * 4 + column, 256)


def block_tokens(ref, first, count):
    return [ref[first : first + count, l * D : (l + 1) * D] for l in range(LATENT)]


def project_keys(tokens, project, blocks):
    k = direction(matmul(tokens, project[:, D : 2 * D]), blocks).astype(BF)
    return k, matmul(tokens, project[:, 2 * D : 3 * D]).astype(BF)


def project_queries(tokens, project, blocks, scale):
    return (direction(matmul(tokens, project[:, 0:D]), blocks) * scale).astype(BF)


def setup_kernel(
    mats, first_scale, second_scale, staged, scales, order, blocks
):
    staged[...] = mats[...]
    scales[0:1] = scale_row(first_scale)
    scales[1:2] = scale_row(second_scale)
    order[...] = tile_order()
    blocks[...] = head_blocks()


def first_half(picked, keys, values, project, scale, output, gain, blocks):
    masks = lane_masks()
    q = project_queries(picked, project, blocks, scale)
    mixture = jnp.concatenate(
        [
            attend(
                q[w * 128 : w * 128 + 128],
                keys[w * 256 : w * 256 + 256],
                values[w * 256 : w * 256 + 256],
                masks,
                None,
            )
            for w in range(2)
        ],
        axis=0,
    )
    return finish(picked, mixture, output[...], gain[...]).astype(BF)


def first_edges_kernel(
    mix, latent_w, base, blocks, project, scales, output, gain,
    side0, side1, tokens, keys, values,
):
    for l in range(LATENT):
        merged = (matmul_tn(mix[l], latent_w[...]) + base[l : l + 1, :]).astype(BF)
        for side in range(2):
            for half in range(2):
                at, first = (side * 2 + half) * 128 + l * 32, half * 64 + side * 32
                tokens[at : at + 32] = merged[first : first + 32]
    keys[...], values[...] = project_keys(tokens[...], project, blocks[...])
    picked = jnp.concatenate([tokens[b * 32 : b * 32 + 16] for b in range(16)], axis=0)
    done = first_half(
        picked, keys, values, project, scales[0:1], output, gain, blocks[...]
    )
    for side, ref in enumerate((side0, side1)):
        for half in range(2):
            for l in range(LATENT):
                at = ((side * 2 + half) * LATENT + l) * 16
                ref[half * 16 : half * 16 + 16, l * D : (l + 1) * D] = done[at : at + 16]


def first_middle_kernel(
    tokens, keys, values, side0, side1, blocks, project, scales, output, gain, own0, own1
):
    picked = jnp.concatenate([tokens[b * 32 + 16 : b * 32 + 32] for b in range(16)], axis=0)
    done = first_half(
        picked, keys, values, project, scales[0:1], output, gain, blocks[...]
    )
    for half, own in enumerate((own0, own1)):
        own[0:16] = side0[half * 16 : half * 16 + 16]
        own[48:64] = side1[half * 16 : half * 16 + 16]
        for side in range(2):
            for l in range(LATENT):
                at = ((side * 2 + half) * LATENT + l) * 16
                own[16 + side * 16 : 32 + side * 16, l * D : (l + 1) * D] = done[at : at + 16]


PARTS = ((0, 16), (16, 32), (48, 16))


def tile_tokens(halves_of):
    return jnp.concatenate(
        [
            t
            for first, count in PARTS
            for ref in halves_of
            for t in block_tokens(ref, first, count)
        ],
        axis=0,
    )


def second_own_kernel(own0, own1, blocks, project, scales, queries, tokens, keys, values):
    tokens[...] = tile_tokens((own0, own1))
    keys[...], values[...] = project_keys(tokens[...], project, blocks[...])
    queries[...] = project_queries(tokens[...], project, blocks[...], scales[1:2])


def second_middle_kernel(
    far0, far1, queries, tokens, keys, values, blocks, project, output, gain,
    out, far_keys, far_values,
):
    far_keys[...], far_values[...] = project_keys(
        tile_tokens((far0, far1)), project, blocks[...]
    )
    masks = lane_masks()
    mixture = jnp.concatenate(
        [
            attend(
                queries[at : at + 128],
                jnp.concatenate([keys[at : at + 128], far_keys[at : at + 128]], axis=0),
                jnp.concatenate([values[at : at + 128], far_values[at : at + 128]], axis=0),
                masks,
                None,
            )
            for at in (128, 256)
        ],
        axis=0,
    )
    result = finish(tokens[128:384], mixture, output[...], gain[...]).astype(BF)
    out[...] = matmul(middle_order(), result).reshape(64, LATENT, D).astype(BF)


def second_outer_kernel(
    beyond0, beyond1, corner0, corner1, queries, tokens, keys, values, far_keys, far_values,
    middle, blocks, project, output, gain, out, halo_keys, halo_values,
):
    lat = lax.axis_index("lat")
    odd = lax.rem(lat, 2)
    nothing = (lat == 0) | (lat == lax.axis_size("lat") - 1)
    masks = lane_masks()
    out[32:96] = middle[...]
    full = [
        t
        for side, beyond in enumerate((beyond0, beyond1))
        for half, corner in enumerate((corner0, corner1))
        for ref, at in ((beyond, half * 16), (corner, side * 16))
        for t in block_tokens(ref, at, 16)
    ]
    halo_keys[...], halo_values[...] = project_keys(
        jnp.concatenate(full, axis=0), project, blocks[...]
    )
    outside = (iota((256, LANES), 0) < 128) & nothing
    alive = [None, jnp.where(outside, 0.0, 1.0).astype(BF)]
    mixtures = []
    for side in range(2):
        for half in range(2):
            at, far = side * 384 + half * 64, side * 256 + half * 128
            k = [halo_keys[far : far + 128], keys[at : at + 64], far_keys[at : at + 64]]
            v = [halo_values[far : far + 128], values[at : at + 64], far_values[at : at + 64]]
            mixtures.append(
                attend(
                    queries[at : at + 64],
                    jnp.concatenate(k, axis=0),
                    jnp.concatenate(v, axis=0),
                    masks,
                    alive[side],
                )
            )
    own = jnp.concatenate([tokens[0:128], tokens[384:512]], axis=0)
    mixture = jnp.concatenate(mixtures, axis=0)
    result = finish(own, mixture, output[...], gain[...]).astype(BF)
    order = edge_order()
    for side in range(2):
        block = matmul(order, result[side * 128 : side * 128 + 128])
        first = jnp.where(odd == side, 96, 0)
        out[pl.ds(first, 32)] = block.reshape(32, LATENT, D).astype(BF)


VMEM = pl.BlockSpec(memory_space=pltpu.VMEM)
HBM = pl.BlockSpec(memory_space=pltpu.HBM)
SMEM = pl.BlockSpec(memory_space=pltpu.SMEM)
MIB = 1024 * 1024


def swapped(value, axis, first):
    size = lax.axis_size(axis)
    step = 0 if first else 1
    route = [(i, ((i + step) ^ 1) - step) for i in range(size)]
    return lax.ppermute(value, axis, [(i, j % size) for i, j in route])


def params(mib):
    return pltpu.CompilerParams(vmem_limit_bytes=mib * MIB)


def cost(microseconds):
    return pl.CostEstimate(
        flops=int(microseconds * 1e9), bytes_accessed=MIB, transcendentals=1 << 18
    )


def wide_rows(count):
    return jax.ShapeDtypeStruct((count, LATENT * D), BF)


def token_rows(count):
    return jax.ShapeDtypeStruct((count, D), BF)


def pack_kernel(x, out):
    out[...] = x[...].T


def pack_call(stripe):
    return pl.pallas_call(
        pack_kernel,
        out_shape=jax.ShapeDtypeStruct((LANES, LEVELS * PV), BF),
        in_specs=[VMEM],
        out_specs=VMEM,
        compiler_params=params(24),
        cost_estimate=cost(0.8),
        name="pack",
    )(stripe)


def fold_call(*operands):
    return pl.pallas_call(
        fold_kernel,
        out_shape=jax.ShapeDtypeStruct((3 * D + 64, 256), BF),
        in_specs=[HBM] * len(operands),
        out_specs=VMEM,
        scratch_shapes=[
            (pltpu.SMEM if x.shape == (HEADS,) else pltpu.VMEM)(x.shape, x.dtype) for x in operands
        ]
        + [pltpu.VMEM((128, D), F32), pltpu.SemaphoreType.DMA((len(operands),))],
        compiler_params=params(60),
        cost_estimate=cost(3.0),
        name="fold",
    )(*operands)


def encode_call(*operands):
    return pl.pallas_call(
        encode_kernel,
        out_shape=jax.ShapeDtypeStruct((LATENT, D, LANES), BF),
        in_specs=[VMEM] * len(operands),
        out_specs=VMEM,
        scratch_shapes=[
            pltpu.VMEM((256, LEVELS * LANES), BF),
            pltpu.VMEM((LEVELS * PV, LANES), BF),
            pltpu.VMEM((LEVELS, D, LANES), F32),
            pltpu.VMEM((LEVELS + 1, 64, LANES), F32),
        ],
        compiler_params=params(24),
        cost_estimate=cost(3.0),
        name="encode",
    )(*operands)


def setup_call(mats, first_scale, second_scale):
    square = lambda size: jax.ShapeDtypeStruct((size, size), BF)
    return pl.pallas_call(
        setup_kernel,
        out_shape=[
            jax.ShapeDtypeStruct(mats.shape, BF), jax.ShapeDtypeStruct((2, D), F32),
            square(128), square(256),
        ],
        in_specs=[VMEM, SMEM, SMEM],
        out_specs=[VMEM] * 4,
        compiler_params=params(24),
        cost_estimate=cost(0.8),
        name="setup",
    )(mats, first_scale, second_scale)


def first_edges_call(*operands):
    return pl.pallas_call(
        first_edges_kernel,
        out_shape=[wide_rows(32)] * 2 + [token_rows(512)] * 3,
        in_specs=[VMEM] * len(operands),
        out_specs=[VMEM] * 5,
        compiler_params=params(24),
        cost_estimate=cost(3.0),
        name="first_edges",
    )(*operands)


def first_middle_call(*operands):
    return pl.pallas_call(
        first_middle_kernel,
        out_shape=[wide_rows(64)] * 2,
        in_specs=[VMEM] * len(operands),
        out_specs=[VMEM] * 2,
        compiler_params=params(24),
        cost_estimate=cost(2.0),
        name="first_middle",
    )(*operands)


def second_own_call(*operands):
    return pl.pallas_call(
        second_own_kernel,
        out_shape=[token_rows(512)] * 4,
        in_specs=[VMEM] * len(operands),
        out_specs=[VMEM] * 4,
        compiler_params=params(24),
        cost_estimate=cost(1.3),
        name="second_own",
    )(*operands)


def second_middle_call(*operands):
    return pl.pallas_call(
        second_middle_kernel,
        out_shape=[jax.ShapeDtypeStruct((64, LATENT, D), BF)] + [token_rows(512)] * 2,
        in_specs=[VMEM] * len(operands),
        out_specs=[VMEM] * 3,
        compiler_params=params(24),
        cost_estimate=cost(2.6),
        name="second_middle",
    )(*operands)


def second_outer_call(*operands):
    return pl.pallas_call(
        second_outer_kernel,
        out_shape=jax.ShapeDtypeStruct((128, LATENT, D), BF),
        in_specs=[VMEM] * len(operands),
        out_specs=VMEM,
        scratch_shapes=[pltpu.VMEM((512, D), BF)] * 2,
        compiler_params=params(24),
        cost_estimate=cost(3.3),
        name="second_outer",
    )(*operands)


def per_device(
    fields,
    embed_weight,
    level_code,
    encoder_gain,
    key_weight,
    value_weight,
    latent_query,
    encoder_scale,
    latent_weight,
    latent_base,
    first_project,
    first_scale,
    first_output,
    first_gain,
    second_project,
    second_scale,
    second_output,
    second_gain,
):
    packed = pack_call(fields.reshape(LEVELS * PV, LANES))
    received = lax.all_to_all(packed, "lon", split_axis=0, concat_axis=0, tiled=True)
    mats = fold_call(
        embed_weight, level_code, encoder_gain.reshape(1, D), key_weight, value_weight,
        latent_query, encoder_scale,
    )
    mats, scales, order, blocks = setup_call(mats, first_scale, second_scale)
    mix = encode_call(received, order, mats)
    weights = (blocks, first_project, scales, first_output, first_gain.reshape(1, D))
    side0, side1, tokens, keys, values = first_edges_call(
        mix, latent_weight, latent_base, *weights
    )
    beyond = [swapped(side0, "lat", True), swapped(side1, "lat", False)]
    own = first_middle_call(tokens, keys, values, side0, side1, *weights)
    far = [swapped(own[0], "lon", True), swapped(own[1], "lon", False)]
    weights = (blocks, second_project, second_output, second_gain.reshape(1, D))
    mine = second_own_call(*own, blocks, second_project, scales)
    corners = [
        swapped(jnp.concatenate([x[i : i + 16] for x in beyond], axis=0), "lon", i == 0)
        for i in (0, 16)
    ]
    done, far_keys, far_values = second_middle_call(*far, *mine, *weights)
    out = second_outer_call(*beyond, *corners, *mine, far_keys, far_values, done, *weights)
    return out.reshape(16, 8, LATENT, D)


def solution(mesh):
    in_specs = (P("lat", "lon", None, None, None),) + (P(),) * 17
    out_specs = P("lat", "lon", None, None)
    return jax.shard_map(
        per_device, mesh=mesh, in_specs=in_specs, out_specs=out_specs, check_vma=False
    )
```

```python
import jax
import jax.numpy as jnp
from jax import lax
from jax.experimental import pallas as pl
from jax.experimental.pallas import tpu as pltpu
from jax.sharding import PartitionSpec as P

D = 512
HEADS = 16
LEVELS = 13
LATENT = 4
PV = 80
HEAD = 32
HALF = 4
LANES = 128
GROUPS = D // LANES
IN_GROUP = LANES // HEAD
NORM_EPS = 1e-05
DIR_EPS = 1e-06
GRAM = 2 * D
LOG2E = 1.4426950408889634
BF = jnp.bfloat16
F32 = jnp.float32
ENC_SPANS = [(0, 512), (512, 512), (1024, 512), (1536, 128)]


def iota(shape, dim):
    return lax.broadcasted_iota(jnp.int32, shape, dim)


def matmul(a, b):
    return jnp.dot(a, b, preferred_element_type=F32)


def matmul_nt(a, b):
    return lax.dot_general(a, b, (((1,), (1,)), ((), ())), preferred_element_type=F32)


def matmul_tn(a, b):
    return lax.dot_general(a, b, (((0,), (0,)), ((), ())), preferred_element_type=F32)


def halves(value):
    high = value.astype(BF)
    return high, (value - high.astype(F32)).astype(BF)


def scale_row(scale_ref):
    head = iota((1, D), 1) // HEAD
    row = jnp.zeros((1, D), F32)
    for h in range(HEADS):
        row = jnp.where(head == h, scale_ref[h] * LOG2E, row)
    return row


def head_blocks():
    return (iota((256, 256), 0) // HEAD == iota((256, 256), 1) // HEAD).astype(F32).astype(BF)


def head_squares(value, blocks):
    square = (value * value).astype(BF)
    return jnp.concatenate(
        [matmul(square[:, i : i + 256], blocks) for i in range(0, D, 256)], axis=1
    )


def direction(value, blocks):
    return value * lax.rsqrt(head_squares(value, blocks) + DIR_EPS)


def lane_masks():
    head = iota((1, LANES), 1) // HEAD
    return [(head == h).astype(F32).astype(BF) for h in range(IN_GROUP)]


def attend(windows):
    masks = lane_masks()
    groups = [slice(g * LANES, (g + 1) * LANES) for g in range(GROUPS)]
    weights = []
    for queries, keys, values, alive in windows:
        for lanes in groups:
            stacked = jnp.concatenate([queries[:, lanes] * m for m in masks], axis=0)
            weights.append(jnp.exp2(matmul_nt(stacked, keys[:, lanes])).astype(BF))
    mixtures = []
    for w, (queries, keys, values, alive) in enumerate(windows):
        count, tokens = queries.shape[0], keys.shape[0]
        head = iota((count, LANES), 1) // HEAD
        ones = jnp.ones((tokens, LANES), BF) if alive is None else alive
        parts = []
        for g, lanes in enumerate(groups):
            v = values[:, lanes] if alive is None else values[:, lanes] * alive
            both = matmul(weights[w * GROUPS + g], jnp.concatenate([v, ones], axis=1))
            picked = both[:count]
            over, under = picked[:, :LANES], picked[:, LANES:]
            for h in range(1, IN_GROUP):
                block = both[h * count : (h + 1) * count]
                over = jnp.where(head == h, block[:, :LANES], over)
                under = jnp.where(head == h, block[:, LANES:], under)
            parts.append((over / under).astype(BF))
        mixtures.append(jnp.concatenate(parts, axis=1))
    return jnp.concatenate(mixtures, axis=0)


def finish(tokens, mixture, output, gain):
    branch = matmul(mixture, output)
    centre = branch - jnp.mean(branch, axis=-1, keepdims=True)
    spread = jnp.mean(centre * centre, axis=-1, keepdims=True)
    return tokens.astype(F32) + centre * lax.rsqrt(spread + NORM_EPS) * gain


def fold_kernel(*refs):
    sources, mats, landed, wide, sems = refs[:7], refs[7], refs[8:15], refs[15], refs[16]
    copies = [
        pltpu.make_async_copy(source, target, sems.at[i])
        for i, (source, target) in enumerate(zip(sources, landed))
    ]
    embed, code, gain, key_w, value_w, query, scale = landed
    for copy in copies:
        copy.start()
    for copy in copies:
        copy.wait()
    wide[...] = jnp.zeros((128, D), F32)
    w = embed[...].astype(F32)
    wide[0:PV] = w - jnp.mean(w, axis=-1, keepdims=True)
    c = code[...]
    wide[PV : PV + LEVELS] = c - jnp.mean(c, axis=-1, keepdims=True)
    centred = wide[...]
    high, low = halves(centred * gain[...])
    both = jnp.concatenate([high, low], axis=0)
    for i, weight in enumerate((key_w, value_w)):
        product = matmul(both, weight[...])
        product = product[:128] + product[128:]
        h, l = halves(product.T)
        mats[i * D : (i + 1) * D] = jnp.concatenate([h, l], axis=1)
        if i == 0:
            own = iota((HEADS, D), 1) // HEAD == iota((HEADS, D), 0)
            rows = jnp.concatenate(
                [jnp.where(own, query[l : l + 1, :], 0.0) for l in range(LATENT)], axis=0
            )
            length = jnp.sum(rows * rows, axis=-1, keepdims=True) + DIR_EPS
            rows = (rows * lax.rsqrt(length) * scale_row(scale)).astype(BF)
            kh, kl = halves(product)
            raw = matmul_nt(rows, kh) + matmul_nt(rows, kl)
            h, l = halves(raw)
            mats[GRAM + 128 : GRAM + 192] = jnp.concatenate([h, l], axis=1)
    h, l = halves(centred)
    cross = matmul_nt(h, l)
    h, l = halves((matmul_nt(h, h) + (cross + cross.T)) * (1.0 / D))
    mats[GRAM : GRAM + 128] = jnp.concatenate([h, l], axis=1)


def encode_kernel(x, order, mats, mix, f2, flat, vals, wts):
    flat[...] = matmul(order[...], x[...]).astype(BF).T
    level = (iota((48, LEVELS * LANES), 0) == iota((48, LEVELS * LANES), 1) // LANES)
    level = level.astype(F32).astype(BF)
    for top in (0, 128):
        f2[top + PV : top + 128, :] = level
        for k in range(LEVELS):
            f2[top : top + PV, k * LANES : (k + 1) * LANES] = flat[k * PV : (k + 1) * PV]

    gather = (iota((HEADS, 128), 1) // 8 == iota((HEADS, 128), 0)).astype(F32).astype(BF)
    total = jnp.zeros((64, LANES), F32)
    for start, width in ENC_SPANS:
        rhs = f2[:, start : start + width]
        keys = matmul(mats[0:D], rhs)
        part = jnp.sum((keys * keys).reshape(HEADS, 4, 8, width), axis=1).reshape(128, width)
        squares = matmul(gather, part.astype(BF))
        square = matmul(mats[GRAM : GRAM + 128], rhs) * f2[0:128, start : start + width].astype(F32)
        part = jnp.sum(square.reshape(16, 8, width), axis=0)
        spread = jnp.maximum(jnp.sum(part, axis=0, keepdims=True), 0.0) + NORM_EPS
        factor = lax.rsqrt(squares + DIR_EPS * spread)
        scores = matmul(mats[GRAM + 128 : GRAM + 192], rhs) * jnp.concatenate([factor] * LATENT, axis=0)
        weights = jnp.exp2(scores)
        scaled = weights * lax.rsqrt(spread)
        values = matmul(mats[D : 2 * D], rhs)
        for i in range(width // LANES):
            k = start // LANES + i
            lanes = slice(i * LANES, (i + 1) * LANES)
            total = total + weights[:, lanes]
            wts[k] = scaled[:, lanes]
            vals[k] = values[:, lanes]
    wts[LEVELS] = 1.0 / total

    for h in range(HEADS):
        rows = slice(h * HEAD, (h + 1) * HEAD)
        sums = [jnp.zeros((HEAD, LANES), F32) for _ in range(LATENT)]
        for k in range(LEVELS):
            v = vals[k, rows, :]
            for l in range(LATENT):
                sums[l] = sums[l] + wts[k, l * HEADS + h : l * HEADS + h + 1, :] * v
        for l in range(LATENT):
            r = wts[LEVELS, l * HEADS + h : l * HEADS + h + 1, :]
            mix[rows, l * LANES : (l + 1) * LANES] = (sums[l] * r).astype(BF)


def parities():
    lat, lon = lax.axis_index("lat"), lax.axis_index("lon")
    return lax.rem(lat, 2), lax.rem(lon, 2)


def one_hot(source, size):
    return (source == iota((size, size), 1)).astype(F32).astype(BF)


def tile_order():
    odd_lat, odd_lon = parities()
    i = iota((128, 128), 0)
    half, side, inner, row, column = i // 64, (i // 32) % 2, (i // 16) % 2, (i // 4) % 4, i % 4
    start = jnp.where(side == 1 - odd_lat, 4 * inner, 12 - 4 * inner)
    right = jnp.where(odd_lon == 1, half, 1 - half)
    return one_hot((start + row) * 8 + right * 4 + column, 128)


def edge_order():
    odd_lat, odd_lon = parities()
    i = iota((128, 128), 0)
    row, right, column, level = i // 32, (i // 16) % 2, (i // 4) % 4, i % 4
    half = jnp.where(odd_lon == 1, right, 1 - right)
    return one_hot(half * 64 + level * 16 + row * 4 + column, 128)


def middle_order():
    odd_lat, odd_lon = parities()
    i = iota((256, 256), 0)
    window, row, right = i // 128, (i // 32) % 4, (i // 16) % 2
    column, level = (i // 4) % 4, i % 4
    half = jnp.where(odd_lon == 1, right, 1 - right)
    side = jnp.where(odd_lat == 1, window, 1 - window)
    return one_hot(half * 128 + level * 32 + side * 16 + row * 4 + column, 256)


def block_tokens(ref, first, count):
    return [ref[first : first + count, l * D : (l + 1) * D] for l in range(LATENT)]


def project_keys(tokens, project, blocks):
    k = direction(matmul(tokens, project[:, D : 2 * D]), blocks).astype(BF)
    return k, matmul(tokens, project[:, 2 * D : 3 * D]).astype(BF)


def project_queries(tokens, project, blocks, scale):
    return (direction(matmul(tokens, project[:, 0:D]), blocks) * scale).astype(BF)


def setup_kernel(
    mats, first_scale, second_scale, staged, scales, order, blocks
):
    staged[...] = mats[...]
    scales[0:1] = scale_row(first_scale)
    scales[1:2] = scale_row(second_scale)
    order[...] = tile_order()
    blocks[...] = head_blocks()


def first_half(picked, keys, values, project, scale, output, gain, blocks):
    q = project_queries(picked, project, blocks, scale)
    windows = []
    for w in range(2):
        near, window = slice(w * 128, w * 128 + 128), slice(w * 256, w * 256 + 256)
        windows.append((q[near], keys[window], values[window], None))
    return finish(picked, attend(windows), output[...], gain[...]).astype(BF)


def first_edges_kernel(
    mix, latent_w, base, blocks, project, scales, output, gain,
    side0, side1, tokens, keys, values,
):
    levels = matmul_tn(mix[...], latent_w[...])
    for l in range(LATENT):
        merged = (levels[l * LANES : (l + 1) * LANES] + base[l : l + 1, :]).astype(BF)
        for side in range(2):
            for half in range(2):
                at, first = (side * 2 + half) * 128 + l * 32, half * 64 + side * 32
                tokens[at : at + 32] = merged[first : first + 32]
    keys[...], values[...] = project_keys(tokens[...], project, blocks[...])
    picked = jnp.concatenate([tokens[b * 32 : b * 32 + 16] for b in range(16)], axis=0)
    done = first_half(
        picked, keys, values, project, scales[0:1], output, gain, blocks[...]
    )
    for side, ref in enumerate((side0, side1)):
        for half in range(2):
            for l in range(LATENT):
                at = ((side * 2 + half) * LATENT + l) * 16
                ref[half * 16 : half * 16 + 16, l * D : (l + 1) * D] = done[at : at + 16]


def first_middle_kernel(
    tokens, keys, values, side0, side1, blocks, project, scales, output, gain, own0, own1
):
    picked = jnp.concatenate([tokens[b * 32 + 16 : b * 32 + 32] for b in range(16)], axis=0)
    done = first_half(
        picked, keys, values, project, scales[0:1], output, gain, blocks[...]
    )
    for half, own in enumerate((own0, own1)):
        own[0:16] = side0[half * 16 : half * 16 + 16]
        own[48:64] = side1[half * 16 : half * 16 + 16]
        for side in range(2):
            for l in range(LATENT):
                at = ((side * 2 + half) * LATENT + l) * 16
                own[16 + side * 16 : 32 + side * 16, l * D : (l + 1) * D] = done[at : at + 16]


PARTS = ((0, 16), (16, 32), (48, 16))


def tile_tokens(halves_of):
    return jnp.concatenate(
        [
            t
            for first, count in PARTS
            for ref in halves_of
            for t in block_tokens(ref, first, count)
        ],
        axis=0,
    )


def second_own_kernel(own0, own1, blocks, project, scales, queries, tokens, keys, values):
    tokens[...] = tile_tokens((own0, own1))
    keys[...], values[...] = project_keys(tokens[...], project, blocks[...])
    queries[...] = project_queries(tokens[...], project, blocks[...], scales[1:2])


def second_middle_kernel(
    far0, far1, queries, tokens, keys, values, blocks, project, output, gain,
    out, far_keys, far_values,
):
    far_keys[...], far_values[...] = project_keys(
        tile_tokens((far0, far1)), project, blocks[...]
    )
    windows = []
    for at in (slice(128, 256), slice(256, 384)):
        k = jnp.concatenate([keys[at], far_keys[at]], axis=0)
        v = jnp.concatenate([values[at], far_values[at]], axis=0)
        windows.append((queries[at], k, v, None))
    mixture = attend(windows)
    result = finish(tokens[128:384], mixture, output[...], gain[...]).astype(BF)
    out[...] = matmul(middle_order(), result).reshape(64, LATENT, D).astype(BF)


def second_outer_kernel(
    beyond0, beyond1, corner0, corner1, queries, tokens, keys, values, far_keys, far_values,
    middle, blocks, project, output, gain, out, halo_keys, halo_values, ends, sems,
):
    lat = lax.axis_index("lat")
    odd = lax.rem(lat, 2)
    nothing = (lat == 0) | (lat == lax.axis_size("lat") - 1)
    copies = [pltpu.make_async_copy(middle, out.at[pl.ds(32, 64)], sems.at[2])]
    for side in range(2):
        first = jnp.where(odd == side, 96, 0)
        copies.append(
            pltpu.make_async_copy(ends.at[side], out.at[pl.ds(first, 32)], sems.at[side])
        )
    copies[0].start()
    full = [
        t
        for side, beyond in enumerate((beyond0, beyond1))
        for half, corner in enumerate((corner0, corner1))
        for ref, at in ((beyond, half * 16), (corner, side * 16))
        for t in block_tokens(ref, at, 16)
    ]
    halo_keys[...], halo_values[...] = project_keys(
        jnp.concatenate(full, axis=0), project, blocks[...]
    )
    outside = (iota((256, LANES), 0) < 128) & nothing
    alive = [None, jnp.where(outside, 0.0, 1.0).astype(BF)]
    windows = []
    for side in range(2):
        for half in range(2):
            at, far = side * 384 + half * 64, side * 256 + half * 128
            at, far = slice(at, at + 64), slice(far, far + 128)
            k = [halo_keys[far], keys[at], far_keys[at]]
            v = [halo_values[far], values[at], far_values[at]]
            k, v = jnp.concatenate(k, axis=0), jnp.concatenate(v, axis=0)
            windows.append((queries[at], k, v, alive[side]))
    own = jnp.concatenate([tokens[0:128], tokens[384:512]], axis=0)
    mixture = attend(windows)
    result = finish(own, mixture, output[...], gain[...]).astype(BF)
    order = edge_order()
    for side in range(2):
        block = matmul(order, result[side * 128 : side * 128 + 128])
        ends[side] = block.reshape(32, LATENT, D).astype(BF)
        copies[1 + side].start()
    for copy in copies:
        copy.wait()


VMEM = pl.BlockSpec(memory_space=pltpu.VMEM)
HBM = pl.BlockSpec(memory_space=pltpu.HBM)
SMEM = pl.BlockSpec(memory_space=pltpu.SMEM)
MIB = 1024 * 1024


def swapped(value, axis, first):
    size = lax.axis_size(axis)
    step = 0 if first else 1
    route = [(i, ((i + step) ^ 1) - step) for i in range(size)]
    return lax.ppermute(value, axis, [(i, j % size) for i, j in route])


def params(mib):
    return pltpu.CompilerParams(vmem_limit_bytes=mib * MIB)


def cost(microseconds):
    return pl.CostEstimate(
        flops=int(microseconds * 1e9), bytes_accessed=MIB, transcendentals=1 << 18
    )


def wide_rows(count):
    return jax.ShapeDtypeStruct((count, LATENT * D), BF)


def token_rows(count):
    return jax.ShapeDtypeStruct((count, D), BF)


def pack_kernel(x, out):
    out[...] = x[...].T


def pack_call(stripe):
    return pl.pallas_call(
        pack_kernel,
        out_shape=jax.ShapeDtypeStruct((LANES, LEVELS * PV), BF),
        in_specs=[VMEM],
        out_specs=VMEM,
        compiler_params=params(24),
        cost_estimate=cost(0.8),
        name="pack",
    )(stripe)


def fold_call(*operands):
    return pl.pallas_call(
        fold_kernel,
        out_shape=jax.ShapeDtypeStruct((GRAM + 192, 256), BF),
        in_specs=[HBM] * len(operands),
        out_specs=VMEM,
        scratch_shapes=[
            (pltpu.SMEM if x.shape == (HEADS,) else pltpu.VMEM)(x.shape, x.dtype) for x in operands
        ]
        + [pltpu.VMEM((128, D), F32), pltpu.SemaphoreType.DMA((len(operands),))],
        compiler_params=params(60),
        cost_estimate=cost(3.0),
        name="fold",
    )(*operands)


def encode_call(*operands):
    return pl.pallas_call(
        encode_kernel,
        out_shape=jax.ShapeDtypeStruct((D, LATENT * LANES), BF),
        in_specs=[VMEM] * len(operands),
        out_specs=VMEM,
        scratch_shapes=[
            pltpu.VMEM((256, LEVELS * LANES), BF),
            pltpu.VMEM((LEVELS * PV, LANES), BF),
            pltpu.VMEM((LEVELS, D, LANES), F32),
            pltpu.VMEM((LEVELS + 1, 64, LANES), F32),
        ],
        compiler_params=params(24),
        cost_estimate=cost(3.0),
        name="encode",
    )(*operands)


def setup_call(mats, first_scale, second_scale):
    square = lambda size: jax.ShapeDtypeStruct((size, size), BF)
    return pl.pallas_call(
        setup_kernel,
        out_shape=[
            jax.ShapeDtypeStruct(mats.shape, BF), jax.ShapeDtypeStruct((2, D), F32),
            square(128), square(256),
        ],
        in_specs=[VMEM, SMEM, SMEM],
        out_specs=[VMEM] * 4,
        compiler_params=params(24),
        cost_estimate=cost(0.8),
        name="setup",
    )(mats, first_scale, second_scale)


def first_edges_call(*operands):
    return pl.pallas_call(
        first_edges_kernel,
        out_shape=[wide_rows(32)] * 2 + [token_rows(512)] * 3,
        in_specs=[VMEM] * len(operands),
        out_specs=[VMEM] * 5,
        compiler_params=params(24),
        cost_estimate=cost(3.0),
        name="first_edges",
    )(*operands)


def first_middle_call(*operands):
    return pl.pallas_call(
        first_middle_kernel,
        out_shape=[wide_rows(64)] * 2,
        in_specs=[VMEM] * len(operands),
        out_specs=[VMEM] * 2,
        compiler_params=params(24),
        cost_estimate=cost(2.0),
        name="first_middle",
    )(*operands)


def second_own_call(*operands):
    return pl.pallas_call(
        second_own_kernel,
        out_shape=[token_rows(512)] * 4,
        in_specs=[VMEM] * len(operands),
        out_specs=[VMEM] * 4,
        compiler_params=params(24),
        cost_estimate=cost(1.3),
        name="second_own",
    )(*operands)


def second_middle_call(*operands):
    return pl.pallas_call(
        second_middle_kernel,
        out_shape=[jax.ShapeDtypeStruct((64, LATENT, D), BF)] + [token_rows(512)] * 2,
        in_specs=[VMEM] * len(operands),
        out_specs=[VMEM] * 3,
        compiler_params=params(24),
        cost_estimate=cost(2.6),
        name="second_middle",
    )(*operands)


def second_outer_call(*operands):
    return pl.pallas_call(
        second_outer_kernel,
        out_shape=jax.ShapeDtypeStruct((128, LATENT, D), BF),
        in_specs=[VMEM] * len(operands),
        out_specs=HBM,
        scratch_shapes=[pltpu.VMEM((512, D), BF)] * 2
        + [pltpu.VMEM((2, 32, LATENT, D), BF), pltpu.SemaphoreType.DMA((3,))],
        compiler_params=params(24),
        cost_estimate=cost(3.3),
        name="second_outer",
    )(*operands)


def per_device(
    fields,
    embed_weight,
    level_code,
    encoder_gain,
    key_weight,
    value_weight,
    latent_query,
    encoder_scale,
    latent_weight,
    latent_base,
    first_project,
    first_scale,
    first_output,
    first_gain,
    second_project,
    second_scale,
    second_output,
    second_gain,
):
    packed = pack_call(fields.reshape(LEVELS * PV, LANES))
    received = lax.all_to_all(packed, "lon", split_axis=0, concat_axis=0, tiled=True)
    mats = fold_call(
        embed_weight, level_code, encoder_gain.reshape(1, D), key_weight, value_weight,
        latent_query, encoder_scale,
    )
    mats, scales, order, blocks = setup_call(mats, first_scale, second_scale)
    mix = encode_call(received, order, mats)
    weights = (blocks, first_project, scales, first_output, first_gain.reshape(1, D))
    side0, side1, tokens, keys, values = first_edges_call(
        mix, latent_weight, latent_base, *weights
    )
    beyond = [swapped(side0, "lat", True), swapped(side1, "lat", False)]
    own = first_middle_call(tokens, keys, values, side0, side1, *weights)
    far = [swapped(own[0], "lon", True), swapped(own[1], "lon", False)]
    weights = (blocks, second_project, second_output, second_gain.reshape(1, D))
    mine = second_own_call(*own, blocks, second_project, scales)
    corners = [
        swapped(jnp.concatenate([x[i : i + 16] for x in beyond], axis=0), "lon", i == 0)
        for i in (0, 16)
    ]
    done, far_keys, far_values = second_middle_call(*far, *mine, *weights)
    out = second_outer_call(*beyond, *corners, *mine, far_keys, far_values, done, *weights)
    return out.reshape(16, 8, LATENT, D)


def solution(mesh):
    in_specs = (P("lat", "lon", None, None, None),) + (P(),) * 17
    out_specs = P("lat", "lon", None, None)
    return jax.shard_map(
        per_device, mesh=mesh, in_specs=in_specs, out_specs=out_specs, check_vma=False
    )
```

```python
import jax
import jax.numpy as jnp
from jax import lax
from jax.experimental import pallas as pl
from jax.experimental.pallas import tpu as pltpu
from jax.sharding import PartitionSpec as P

D = 512
HEADS = 16
LEVELS = 13
LATENT = 4
PV = 80
HEAD = 32
HALF = 4
LANES = 128
GROUPS = D // LANES
IN_GROUP = LANES // HEAD
NORM_EPS = 1e-05
DIR_EPS = 1e-06
GRAM = 2 * D
LOG2E = 1.4426950408889634
BF = jnp.bfloat16
F32 = jnp.float32
ENC_SPANS = [(0, 512), (512, 512), (1024, 512), (1536, 128)]


def iota(shape, dim):
    return lax.broadcasted_iota(jnp.int32, shape, dim)


def matmul(a, b):
    return jnp.dot(a, b, preferred_element_type=F32)


def matmul_nt(a, b):
    return lax.dot_general(a, b, (((1,), (1,)), ((), ())), preferred_element_type=F32)


def matmul_tn(a, b):
    return lax.dot_general(a, b, (((0,), (0,)), ((), ())), preferred_element_type=F32)


def halves(value):
    high = value.astype(BF)
    return high, (value - high.astype(F32)).astype(BF)


def scale_row(scale_ref):
    head = iota((1, D), 1) // HEAD
    row = jnp.zeros((1, D), F32)
    for h in range(HEADS):
        row = jnp.where(head == h, scale_ref[h] * LOG2E, row)
    return row


def head_blocks():
    return (iota((256, 256), 0) // HEAD == iota((256, 256), 1) // HEAD).astype(F32).astype(BF)


def head_squares(value, blocks):
    square = (value * value).astype(BF)
    return jnp.concatenate(
        [matmul(square[:, i : i + 256], blocks) for i in range(0, D, 256)], axis=1
    )


def direction(value, blocks):
    return value * lax.rsqrt(head_squares(value, blocks) + DIR_EPS)


def lane_masks():
    head = iota((1, LANES), 1) // HEAD
    return [(head == h).astype(F32).astype(BF) for h in range(IN_GROUP)]


def attend(windows):
    masks = lane_masks()
    groups = [slice(g * LANES, (g + 1) * LANES) for g in range(GROUPS)]
    weights = []
    for queries, keys, values, alive in windows:
        for lanes in groups:
            stacked = jnp.concatenate([queries[:, lanes] * m for m in masks], axis=0)
            weights.append(jnp.exp2(matmul_nt(stacked, keys[:, lanes])).astype(BF))
    mixtures = []
    for w, (queries, keys, values, alive) in enumerate(windows):
        count, tokens = queries.shape[0], keys.shape[0]
        head = iota((count, LANES), 1) // HEAD
        ones = jnp.ones((tokens, LANES), BF) if alive is None else alive
        parts = []
        for g, lanes in enumerate(groups):
            v = values[:, lanes] if alive is None else values[:, lanes] * alive
            both = matmul(weights[w * GROUPS + g], jnp.concatenate([v, ones], axis=1))
            picked = both[:count]
            over, under = picked[:, :LANES], picked[:, LANES:]
            for h in range(1, IN_GROUP):
                block = both[h * count : (h + 1) * count]
                over = jnp.where(head == h, block[:, :LANES], over)
                under = jnp.where(head == h, block[:, LANES:], under)
            parts.append((over / under).astype(BF))
        mixtures.append(jnp.concatenate(parts, axis=1))
    return jnp.concatenate(mixtures, axis=0)


def finish(tokens, mixture, output, gain):
    branch = matmul(mixture, output)
    centre = branch - jnp.mean(branch, axis=-1, keepdims=True)
    spread = jnp.mean(centre * centre, axis=-1, keepdims=True)
    return tokens.astype(F32) + centre * lax.rsqrt(spread + NORM_EPS) * gain


def fold_kernel(*refs):
    sources, mats, landed, wide, sems = refs[:7], refs[7], refs[8:15], refs[15], refs[16]
    copies = [
        pltpu.make_async_copy(source, target, sems.at[i])
        for i, (source, target) in enumerate(zip(sources, landed))
    ]
    embed, code, gain, key_w, value_w, query, scale = landed
    for copy in copies:
        copy.start()
    for copy in copies:
        copy.wait()
    wide[...] = jnp.zeros((128, D), F32)
    w = embed[...].astype(F32)
    wide[0:PV] = w - jnp.mean(w, axis=-1, keepdims=True)
    c = code[...]
    wide[PV : PV + LEVELS] = c - jnp.mean(c, axis=-1, keepdims=True)
    centred = wide[...]
    high, low = halves(centred * gain[...])
    both = jnp.concatenate([high, low], axis=0)
    for i, weight in enumerate((key_w, value_w)):
        product = matmul(both, weight[...])
        product = product[:128] + product[128:]
        h, l = halves(product.T)
        mats[i * D : (i + 1) * D] = jnp.concatenate([h, l], axis=1)
        if i == 0:
            own = iota((HEADS, D), 1) // HEAD == iota((HEADS, D), 0)
            rows = jnp.concatenate(
                [jnp.where(own, query[l : l + 1, :], 0.0) for l in range(LATENT)], axis=0
            )
            length = jnp.sum(rows * rows, axis=-1, keepdims=True) + DIR_EPS
            rows = (rows * lax.rsqrt(length) * scale_row(scale)).astype(BF)
            kh, kl = halves(product)
            raw = matmul_nt(rows, kh) + matmul_nt(rows, kl)
            h, l = halves(raw)
            mats[GRAM + 128 : GRAM + 192] = jnp.concatenate([h, l], axis=1)
    h, l = halves(centred)
    cross = matmul_nt(h, l)
    h, l = halves((matmul_nt(h, h) + (cross + cross.T)) * (1.0 / D))
    mats[GRAM : GRAM + 128] = jnp.concatenate([h, l], axis=1)


def encode_kernel(x, order, mats, mix, f2, flat, vals, wts):
    flat[...] = matmul(order[...], x[...]).astype(BF).T
    level = (iota((48, LEVELS * LANES), 0) == iota((48, LEVELS * LANES), 1) // LANES)
    level = level.astype(F32).astype(BF)
    for top in (0, 128):
        f2[top + PV : top + 128, :] = level
        for k in range(LEVELS):
            f2[top : top + PV, k * LANES : (k + 1) * LANES] = flat[k * PV : (k + 1) * PV]

    gather = (iota((HEADS, 128), 1) // 8 == iota((HEADS, 128), 0)).astype(F32).astype(BF)
    total = jnp.zeros((64, LANES), F32)
    for start, width in ENC_SPANS:
        rhs = f2[:, start : start + width]
        keys = matmul(mats[0:D], rhs)
        part = jnp.sum((keys * keys).reshape(HEADS, 4, 8, width), axis=1).reshape(128, width)
        squares = matmul(gather, part.astype(BF))
        square = matmul(mats[GRAM : GRAM + 128], rhs) * f2[0:128, start : start + width].astype(F32)
        part = jnp.sum(square.reshape(16, 8, width), axis=0)
        spread = jnp.maximum(jnp.sum(part, axis=0, keepdims=True), 0.0) + NORM_EPS
        factor = lax.rsqrt(squares + DIR_EPS * spread)
        scores = matmul(mats[GRAM + 128 : GRAM + 192], rhs) * jnp.concatenate([factor] * LATENT, axis=0)
        weights = jnp.exp2(scores)
        scaled = weights * lax.rsqrt(spread)
        values = matmul(mats[D : 2 * D], rhs)
        for i in range(width // LANES):
            k = start // LANES + i
            lanes = slice(i * LANES, (i + 1) * LANES)
            total = total + weights[:, lanes]
            wts[k] = scaled[:, lanes]
            vals[k] = values[:, lanes]
    wts[LEVELS] = 1.0 / total

    for h in range(HEADS):
        rows = slice(h * HEAD, (h + 1) * HEAD)
        sums = [jnp.zeros((HEAD, LANES), F32) for _ in range(LATENT)]
        for k in range(LEVELS):
            v = vals[k, rows, :]
            for l in range(LATENT):
                sums[l] = sums[l] + wts[k, l * HEADS + h : l * HEADS + h + 1, :] * v
        for l in range(LATENT):
            r = wts[LEVELS, l * HEADS + h : l * HEADS + h + 1, :]
            mix[rows, l * LANES : (l + 1) * LANES] = (sums[l] * r).astype(BF)


def parities():
    lat, lon = lax.axis_index("lat"), lax.axis_index("lon")
    return lax.rem(lat, 2), lax.rem(lon, 2)


def one_hot(source, size):
    return (source == iota((size, size), 1)).astype(F32).astype(BF)


def tile_order():
    odd_lat, odd_lon = parities()
    i = iota((128, 128), 0)
    half, side, inner, row, column = i // 64, (i // 32) % 2, (i // 16) % 2, (i // 4) % 4, i % 4
    start = jnp.where(side == 1 - odd_lat, 4 * inner, 12 - 4 * inner)
    right = jnp.where(odd_lon == 1, half, 1 - half)
    return one_hot((start + row) * 8 + right * 4 + column, 128)


def edge_order():
    odd_lat, odd_lon = parities()
    i = iota((128, 128), 0)
    row, right, column, level = i // 32, (i // 16) % 2, (i // 4) % 4, i % 4
    half = jnp.where(odd_lon == 1, right, 1 - right)
    return one_hot(half * 64 + level * 16 + row * 4 + column, 128)


def middle_order():
    odd_lat, odd_lon = parities()
    i = iota((256, 256), 0)
    window, row, right = i // 128, (i // 32) % 4, (i // 16) % 2
    column, level = (i // 4) % 4, i % 4
    half = jnp.where(odd_lon == 1, right, 1 - right)
    side = jnp.where(odd_lat == 1, window, 1 - window)
    return one_hot(half * 128 + level * 32 + side * 16 + row * 4 + column, 256)


def block_tokens(ref, first, count):
    return [ref[first : first + count, l * D : (l + 1) * D] for l in range(LATENT)]


def project_keys(tokens, project, blocks):
    k = direction(matmul(tokens, project[:, D : 2 * D]), blocks).astype(BF)
    return k, matmul(tokens, project[:, 2 * D : 3 * D]).astype(BF)


def project_queries(tokens, project, blocks, scale):
    return (direction(matmul(tokens, project[:, 0:D]), blocks) * scale).astype(BF)


def setup_kernel(
    mats, first_scale, second_scale, staged, scales, order, blocks
):
    staged[...] = mats[...]
    scales[0:1] = scale_row(first_scale)
    scales[1:2] = scale_row(second_scale)
    order[...] = tile_order()
    blocks[...] = head_blocks()


def first_half(picked, keys, values, project, scale, output, gain, blocks):
    q = project_queries(picked, project, blocks, scale)
    windows = []
    for w in range(2):
        near, window = slice(w * 128, w * 128 + 128), slice(w * 256, w * 256 + 256)
        windows.append((q[near], keys[window], values[window], None))
    return finish(picked, attend(windows), output[...], gain[...]).astype(BF)


def first_edges_kernel(
    mix, latent_w, base, blocks, project, scales, output, gain,
    side0, side1, tokens, keys, values,
):
    levels = matmul_tn(mix[...], latent_w[...])
    for l in range(LATENT):
        merged = (levels[l * LANES : (l + 1) * LANES] + base[l : l + 1, :]).astype(BF)
        for side in range(2):
            for half in range(2):
                at, first = (side * 2 + half) * 128 + l * 32, half * 64 + side * 32
                tokens[at : at + 32] = merged[first : first + 32]
    keys[...], values[...] = project_keys(tokens[...], project, blocks[...])
    picked = jnp.concatenate([tokens[b * 32 : b * 32 + 16] for b in range(16)], axis=0)
    done = first_half(
        picked, keys, values, project, scales[0:1], output, gain, blocks[...]
    )
    for side, ref in enumerate((side0, side1)):
        for half in range(2):
            for l in range(LATENT):
                at = ((side * 2 + half) * LATENT + l) * 16
                ref[half * 16 : half * 16 + 16, l * D : (l + 1) * D] = done[at : at + 16]


def first_middle_kernel(
    tokens, keys, values, side0, side1, blocks, project, scales, output, gain, own0, own1
):
    picked = jnp.concatenate([tokens[b * 32 + 16 : b * 32 + 32] for b in range(16)], axis=0)
    done = first_half(
        picked, keys, values, project, scales[0:1], output, gain, blocks[...]
    )
    for half, own in enumerate((own0, own1)):
        own[0:16] = side0[half * 16 : half * 16 + 16]
        own[48:64] = side1[half * 16 : half * 16 + 16]
        for side in range(2):
            for l in range(LATENT):
                at = ((side * 2 + half) * LATENT + l) * 16
                own[16 + side * 16 : 32 + side * 16, l * D : (l + 1) * D] = done[at : at + 16]


PARTS = ((0, 16), (16, 32), (48, 16))


def tile_tokens(halves_of):
    return jnp.concatenate(
        [
            t
            for first, count in PARTS
            for ref in halves_of
            for t in block_tokens(ref, first, count)
        ],
        axis=0,
    )


def second_own_kernel(own0, own1, blocks, project, scales, queries, tokens, keys, values):
    tokens[...] = tile_tokens((own0, own1))
    keys[...], values[...] = project_keys(tokens[...], project, blocks[...])
    queries[...] = project_queries(tokens[...], project, blocks[...], scales[1:2])


def second_middle_kernel(
    far0, far1, queries, tokens, keys, values, blocks, project, output, gain,
    out, far_keys, far_values,
):
    far_keys[...], far_values[...] = project_keys(
        tile_tokens((far0, far1)), project, blocks[...]
    )
    windows = []
    for at in (slice(128, 256), slice(256, 384)):
        k = jnp.concatenate([keys[at], far_keys[at]], axis=0)
        v = jnp.concatenate([values[at], far_values[at]], axis=0)
        windows.append((queries[at], k, v, None))
    mixture = attend(windows)
    result = finish(tokens[128:384], mixture, output[...], gain[...]).astype(BF)
    out[...] = matmul(middle_order(), result).reshape(64, LATENT, D).astype(BF)


def second_outer_kernel(
    beyond0, beyond1, corner0, corner1, queries, tokens, keys, values, far_keys, far_values,
    middle, blocks, project, output, gain, out, halo_keys, halo_values, ends, sems,
):
    lat = lax.axis_index("lat")
    odd = lax.rem(lat, 2)
    nothing = (lat == 0) | (lat == lax.axis_size("lat") - 1)
    copies = [pltpu.make_async_copy(middle, out.at[pl.ds(32, 64)], sems.at[2])]
    for side in range(2):
        first = jnp.where(odd == side, 96, 0)
        copies.append(
            pltpu.make_async_copy(ends.at[side], out.at[pl.ds(first, 32)], sems.at[side])
        )
    copies[0].start()
    full = [
        t
        for side, beyond in enumerate((beyond0, beyond1))
        for half, corner in enumerate((corner0, corner1))
        for ref, at in ((beyond, half * 16), (corner, side * 16))
        for t in block_tokens(ref, at, 16)
    ]
    halo_keys[...], halo_values[...] = project_keys(
        jnp.concatenate(full, axis=0), project, blocks[...]
    )
    outside = (iota((256, LANES), 0) < 128) & nothing
    alive = [None, jnp.where(outside, 0.0, 1.0).astype(BF)]
    windows = []
    for side in range(2):
        for half in range(2):
            at, far = side * 384 + half * 64, side * 256 + half * 128
            at, far = slice(at, at + 64), slice(far, far + 128)
            k = [halo_keys[far], keys[at], far_keys[at]]
            v = [halo_values[far], values[at], far_values[at]]
            k, v = jnp.concatenate(k, axis=0), jnp.concatenate(v, axis=0)
            windows.append((queries[at], k, v, alive[side]))
    own = jnp.concatenate([tokens[0:128], tokens[384:512]], axis=0)
    mixture = attend(windows)
    result = finish(own, mixture, output[...], gain[...]).astype(BF)
    order = edge_order()
    for side in range(2):
        block = matmul(order, result[side * 128 : side * 128 + 128])
        ends[side] = block.reshape(32, LATENT, D).astype(BF)
        copies[1 + side].start()
    for copy in copies:
        copy.wait()


VMEM = pl.BlockSpec(memory_space=pltpu.VMEM)
HBM = pl.BlockSpec(memory_space=pltpu.HBM)
SMEM = pl.BlockSpec(memory_space=pltpu.SMEM)
MIB = 1024 * 1024


def swapped(value, axis, first):
    size = lax.axis_size(axis)
    step = 0 if first else 1
    route = [(i, ((i + step) ^ 1) - step) for i in range(size)]
    return lax.ppermute(value, axis, [(i, j % size) for i, j in route])


def swapped_inside(value):
    lons, lats = lax.axis_size("lon"), lax.axis_size("lat")
    route = []
    for lon in range(lons):
        for lat in range(lats):
            other = lat - 1 if lat % 2 == 0 else lat + 1
            inside = 0 <= other < lats
            target = (lon, other) if inside else (lon ^ 1, lat)
            route.append((lon * lats + lat, target[0] * lats + target[1]))
    return lax.ppermute(value, ("lon", "lat"), route)


def params(mib):
    return pltpu.CompilerParams(vmem_limit_bytes=mib * MIB)


def cost(microseconds):
    return pl.CostEstimate(
        flops=int(microseconds * 1e9), bytes_accessed=MIB, transcendentals=1 << 18
    )


def wide_rows(count):
    return jax.ShapeDtypeStruct((count, LATENT * D), BF)


def token_rows(count):
    return jax.ShapeDtypeStruct((count, D), BF)


def pack_kernel(x, out):
    out[...] = x[...].T


def pack_call(stripe):
    return pl.pallas_call(
        pack_kernel,
        out_shape=jax.ShapeDtypeStruct((LANES, LEVELS * PV), BF),
        in_specs=[VMEM],
        out_specs=VMEM,
        compiler_params=params(24),
        cost_estimate=cost(0.8),
        name="pack",
    )(stripe)


def fold_call(*operands):
    return pl.pallas_call(
        fold_kernel,
        out_shape=jax.ShapeDtypeStruct((GRAM + 192, 256), BF),
        in_specs=[HBM] * len(operands),
        out_specs=VMEM,
        scratch_shapes=[
            (pltpu.SMEM if x.shape == (HEADS,) else pltpu.VMEM)(x.shape, x.dtype) for x in operands
        ]
        + [pltpu.VMEM((128, D), F32), pltpu.SemaphoreType.DMA((len(operands),))],
        compiler_params=params(60),
        cost_estimate=cost(3.0),
        name="fold",
    )(*operands)


def encode_call(*operands):
    return pl.pallas_call(
        encode_kernel,
        out_shape=jax.ShapeDtypeStruct((D, LATENT * LANES), BF),
        in_specs=[VMEM] * len(operands),
        out_specs=VMEM,
        scratch_shapes=[
            pltpu.VMEM((256, LEVELS * LANES), BF),
            pltpu.VMEM((LEVELS * PV, LANES), BF),
            pltpu.VMEM((LEVELS, D, LANES), F32),
            pltpu.VMEM((LEVELS + 1, 64, LANES), F32),
        ],
        compiler_params=params(24),
        cost_estimate=cost(3.0),
        name="encode",
    )(*operands)


def setup_call(mats, first_scale, second_scale):
    square = lambda size: jax.ShapeDtypeStruct((size, size), BF)
    return pl.pallas_call(
        setup_kernel,
        out_shape=[
            jax.ShapeDtypeStruct(mats.shape, BF), jax.ShapeDtypeStruct((2, D), F32),
            square(128), square(256),
        ],
        in_specs=[VMEM, SMEM, SMEM],
        out_specs=[VMEM] * 4,
        compiler_params=params(24),
        cost_estimate=cost(0.8),
        name="setup",
    )(mats, first_scale, second_scale)


def first_edges_call(*operands):
    return pl.pallas_call(
        first_edges_kernel,
        out_shape=[wide_rows(32)] * 2 + [token_rows(512)] * 3,
        in_specs=[VMEM] * len(operands),
        out_specs=[VMEM] * 5,
        compiler_params=params(24),
        cost_estimate=cost(3.0),
        name="first_edges",
    )(*operands)


def first_middle_call(*operands):
    return pl.pallas_call(
        first_middle_kernel,
        out_shape=[wide_rows(64)] * 2,
        in_specs=[VMEM] * len(operands),
        out_specs=[VMEM] * 2,
        compiler_params=params(24),
        cost_estimate=cost(2.0),
        name="first_middle",
    )(*operands)


def second_own_call(*operands):
    return pl.pallas_call(
        second_own_kernel,
        out_shape=[token_rows(512)] * 4,
        in_specs=[VMEM] * len(operands),
        out_specs=[VMEM] * 4,
        compiler_params=params(24),
        cost_estimate=cost(1.3),
        name="second_own",
    )(*operands)


def second_middle_call(*operands):
    return pl.pallas_call(
        second_middle_kernel,
        out_shape=[jax.ShapeDtypeStruct((64, LATENT, D), BF)] + [token_rows(512)] * 2,
        in_specs=[VMEM] * len(operands),
        out_specs=[VMEM] * 3,
        compiler_params=params(24),
        cost_estimate=cost(2.6),
        name="second_middle",
    )(*operands)


def second_outer_call(*operands):
    return pl.pallas_call(
        second_outer_kernel,
        out_shape=jax.ShapeDtypeStruct((128, LATENT, D), BF),
        in_specs=[VMEM] * len(operands),
        out_specs=HBM,
        scratch_shapes=[pltpu.VMEM((512, D), BF)] * 2
        + [pltpu.VMEM((2, 32, LATENT, D), BF), pltpu.SemaphoreType.DMA((3,))],
        compiler_params=params(24),
        cost_estimate=cost(3.3),
        name="second_outer",
    )(*operands)


def per_device(
    fields,
    embed_weight,
    level_code,
    encoder_gain,
    key_weight,
    value_weight,
    latent_query,
    encoder_scale,
    latent_weight,
    latent_base,
    first_project,
    first_scale,
    first_output,
    first_gain,
    second_project,
    second_scale,
    second_output,
    second_gain,
):
    packed = pack_call(fields.reshape(LEVELS * PV, LANES))
    received = lax.all_to_all(packed, "lon", split_axis=0, concat_axis=0, tiled=True)
    mats = fold_call(
        embed_weight, level_code, encoder_gain.reshape(1, D), key_weight, value_weight,
        latent_query, encoder_scale,
    )
    mats, scales, order, blocks = setup_call(mats, first_scale, second_scale)
    mix = encode_call(received, order, mats)
    weights = (blocks, first_project, scales, first_output, first_gain.reshape(1, D))
    side0, side1, tokens, keys, values = first_edges_call(
        mix, latent_weight, latent_base, *weights
    )
    beyond1 = swapped_inside(side1)
    side0, side1 = lax.optimization_barrier((side0, side1))
    beyond0 = swapped(side0, "lat", True)
    beyond = [beyond0, beyond1]
    own = first_middle_call(tokens, keys, values, side0, side1, *weights)
    far = [swapped(own[0], "lon", True), swapped(own[1], "lon", False)]
    weights = (blocks, second_project, second_output, second_gain.reshape(1, D))
    mine = second_own_call(*own, blocks, second_project, scales)
    corners = [
        swapped(jnp.concatenate([x[i : i + 16] for x in beyond], axis=0), "lon", i == 0)
        for i in (0, 16)
    ]
    done, far_keys, far_values = second_middle_call(*far, *mine, *weights)
    out = second_outer_call(*beyond, *corners, *mine, far_keys, far_values, done, *weights)
    return out.reshape(16, 8, LATENT, D)


def solution(mesh):
    in_specs = (P("lat", "lon", None, None, None),) + (P(),) * 17
    out_specs = P("lat", "lon", None, None)
    return jax.shard_map(
        per_device, mesh=mesh, in_specs=in_specs, out_specs=out_specs, check_vma=False
    )
```

```python
import functools

import jax
import jax.numpy as jnp
from jax import lax
from jax.experimental import pallas as pl
from jax.experimental.pallas import tpu as pltpu
from jax.sharding import PartitionSpec as P

D = 512
HEADS = 16
LEVELS = 13
LATENT = 4
PV = 80
HEAD = 32
HALF = 4
LANES = 128
GROUPS = D // LANES
IN_GROUP = LANES // HEAD
NORM_EPS = 1e-05
DIR_EPS = 1e-06
GRAM = 2 * D
LOG2E = 1.4426950408889634
BF = jnp.bfloat16
F32 = jnp.float32
ENC_SPANS = [(0, 512), (512, 512), (1024, 512), (1536, 128)]


def iota(shape, dim):
    return lax.broadcasted_iota(jnp.int32, shape, dim)


def matmul(a, b):
    return jnp.dot(a, b, preferred_element_type=F32)


def matmul_nt(a, b):
    return lax.dot_general(a, b, (((1,), (1,)), ((), ())), preferred_element_type=F32)


def matmul_tn(a, b):
    return lax.dot_general(a, b, (((0,), (0,)), ((), ())), preferred_element_type=F32)


def halves(value):
    high = value.astype(BF)
    return high, (value - high.astype(F32)).astype(BF)


def scale_row(scale_ref):
    head = iota((1, D), 1) // HEAD
    row = jnp.zeros((1, D), F32)
    for h in range(HEADS):
        row = jnp.where(head == h, scale_ref[h] * LOG2E, row)
    return row


def head_blocks():
    return (iota((256, 256), 0) // HEAD == iota((256, 256), 1) // HEAD).astype(F32).astype(BF)


def head_squares(value, blocks):
    square = (value * value).astype(BF)
    return jnp.concatenate(
        [matmul(square[:, i : i + 256], blocks) for i in range(0, D, 256)], axis=1
    )


def direction(value, blocks):
    return value * lax.rsqrt(head_squares(value, blocks) + DIR_EPS)


def lane_masks():
    head = iota((1, LANES), 1) // HEAD
    return [(head == h).astype(F32).astype(BF) for h in range(IN_GROUP)]


def attend(windows):
    masks = lane_masks()
    groups = [slice(g * LANES, (g + 1) * LANES) for g in range(GROUPS)]
    weights = []
    for queries, keys, values, alive in windows:
        for lanes in groups:
            stacked = jnp.concatenate([queries[:, lanes] * m for m in masks], axis=0)
            weights.append(jnp.exp2(matmul_nt(stacked, keys[:, lanes])).astype(BF))
    mixtures = []
    for w, (queries, keys, values, alive) in enumerate(windows):
        count, tokens = queries.shape[0], keys.shape[0]
        head = iota((count, LANES), 1) // HEAD
        ones = jnp.ones((tokens, LANES), BF) if alive is None else alive
        parts = []
        for g, lanes in enumerate(groups):
            v = values[:, lanes] if alive is None else values[:, lanes] * alive
            both = matmul(weights[w * GROUPS + g], jnp.concatenate([v, ones], axis=1))
            picked = both[:count]
            over, under = picked[:, :LANES], picked[:, LANES:]
            for h in range(1, IN_GROUP):
                block = both[h * count : (h + 1) * count]
                over = jnp.where(head == h, block[:, :LANES], over)
                under = jnp.where(head == h, block[:, LANES:], under)
            parts.append((over / under).astype(BF))
        mixtures.append(jnp.concatenate(parts, axis=1))
    return jnp.concatenate(mixtures, axis=0)


def finish(tokens, mixture, output, gain):
    branch = matmul(mixture, output)
    centre = branch - jnp.mean(branch, axis=-1, keepdims=True)
    spread = jnp.mean(centre * centre, axis=-1, keepdims=True)
    return tokens.astype(F32) + centre * lax.rsqrt(spread + NORM_EPS) * gain


def fold_kernel(*refs):
    sources, mats, landed, wide, sems = refs[:7], refs[7], refs[8:15], refs[15], refs[16]
    copies = [
        pltpu.make_async_copy(source, target, sems.at[i])
        for i, (source, target) in enumerate(zip(sources, landed))
    ]
    embed, code, gain, key_w, value_w, query, scale = landed
    for copy in copies:
        copy.start()
    for copy in copies:
        copy.wait()
    wide[...] = jnp.zeros((128, D), F32)
    w = embed[...].astype(F32)
    wide[0:PV] = w - jnp.mean(w, axis=-1, keepdims=True)
    c = code[...]
    wide[PV : PV + LEVELS] = c - jnp.mean(c, axis=-1, keepdims=True)
    centred = wide[...]
    high, low = halves(centred * gain[...])
    both = jnp.concatenate([high, low], axis=0)
    for i, weight in enumerate((key_w, value_w)):
        product = matmul(both, weight[...])
        product = product[:128] + product[128:]
        h, l = halves(product.T)
        mats[i * D : (i + 1) * D] = jnp.concatenate([h, l], axis=1)
        if i == 0:
            own = iota((HEADS, D), 1) // HEAD == iota((HEADS, D), 0)
            rows = jnp.concatenate(
                [jnp.where(own, query[l : l + 1, :], 0.0) for l in range(LATENT)], axis=0
            )
            length = jnp.sum(rows * rows, axis=-1, keepdims=True) + DIR_EPS
            rows = (rows * lax.rsqrt(length) * scale_row(scale)).astype(BF)
            kh, kl = halves(product)
            raw = matmul_nt(rows, kh) + matmul_nt(rows, kl)
            h, l = halves(raw)
            mats[GRAM + 128 : GRAM + 192] = jnp.concatenate([h, l], axis=1)
    h, l = halves(centred)
    cross = matmul_nt(h, l)
    h, l = halves((matmul_nt(h, h) + (cross + cross.T)) * (1.0 / D))
    mats[GRAM : GRAM + 128] = jnp.concatenate([h, l], axis=1)


def encode_kernel(x, order, mats, mix, f2, flat, vals, wts):
    flat[...] = matmul(order[...], x[...]).astype(BF).T
    level = (iota((48, LEVELS * LANES), 0) == iota((48, LEVELS * LANES), 1) // LANES)
    level = level.astype(F32).astype(BF)
    for top in (0, 128):
        f2[top + PV : top + 128, :] = level
        for k in range(LEVELS):
            f2[top : top + PV, k * LANES : (k + 1) * LANES] = flat[k * PV : (k + 1) * PV]

    gather = (iota((HEADS, 128), 1) // 8 == iota((HEADS, 128), 0)).astype(F32).astype(BF)
    total = jnp.zeros((64, LANES), F32)
    for start, width in ENC_SPANS:
        rhs = f2[:, start : start + width]
        keys = matmul(mats[0:D], rhs)
        part = jnp.sum((keys * keys).reshape(HEADS, 4, 8, width), axis=1).reshape(128, width)
        squares = matmul(gather, part.astype(BF))
        square = matmul(mats[GRAM : GRAM + 128], rhs) * f2[0:128, start : start + width].astype(F32)
        part = jnp.sum(square.reshape(16, 8, width), axis=0)
        spread = jnp.maximum(jnp.sum(part, axis=0, keepdims=True), 0.0) + NORM_EPS
        factor = lax.rsqrt(squares + DIR_EPS * spread)
        scores = matmul(mats[GRAM + 128 : GRAM + 192], rhs) * jnp.concatenate([factor] * LATENT, axis=0)
        weights = jnp.exp2(scores)
        scaled = weights * lax.rsqrt(spread)
        values = matmul(mats[D : 2 * D], rhs)
        for i in range(width // LANES):
            k = start // LANES + i
            lanes = slice(i * LANES, (i + 1) * LANES)
            total = total + weights[:, lanes]
            wts[k] = scaled[:, lanes]
            vals[k] = values[:, lanes]
    wts[LEVELS] = 1.0 / total

    for h in range(HEADS):
        rows = slice(h * HEAD, (h + 1) * HEAD)
        sums = [jnp.zeros((HEAD, LANES), F32) for _ in range(LATENT)]
        for k in range(LEVELS):
            v = vals[k, rows, :]
            for l in range(LATENT):
                sums[l] = sums[l] + wts[k, l * HEADS + h : l * HEADS + h + 1, :] * v
        for l in range(LATENT):
            r = wts[LEVELS, l * HEADS + h : l * HEADS + h + 1, :]
            mix[rows, l * LANES : (l + 1) * LANES] = (sums[l] * r).astype(BF)


def parities():
    lat, lon = lax.axis_index("lat"), lax.axis_index("lon")
    return lax.rem(lat, 2), lax.rem(lon, 2)


def one_hot(source, size):
    return (source == iota((size, size), 1)).astype(F32).astype(BF)


def tile_order():
    odd_lat, odd_lon = parities()
    i = iota((128, 128), 0)
    half, side, inner, row, column = i // 64, (i // 32) % 2, (i // 16) % 2, (i // 4) % 4, i % 4
    start = jnp.where(side == 1 - odd_lat, 4 * inner, 12 - 4 * inner)
    right = jnp.where(odd_lon == 1, half, 1 - half)
    return one_hot((start + row) * 8 + right * 4 + column, 128)


def edge_order():
    odd_lat, odd_lon = parities()
    i = iota((128, 128), 0)
    row, right, column, level = i // 32, (i // 16) % 2, (i // 4) % 4, i % 4
    half = jnp.where(odd_lon == 1, right, 1 - right)
    return one_hot(half * 64 + level * 16 + row * 4 + column, 128)


def middle_order():
    odd_lat, odd_lon = parities()
    i = iota((256, 256), 0)
    window, row, right = i // 128, (i // 32) % 4, (i // 16) % 2
    column, level = (i // 4) % 4, i % 4
    half = jnp.where(odd_lon == 1, right, 1 - right)
    side = jnp.where(odd_lat == 1, window, 1 - window)
    return one_hot(half * 128 + level * 32 + side * 16 + row * 4 + column, 256)


def block_tokens(ref, first, count):
    return [ref[first : first + count, l * D : (l + 1) * D] for l in range(LATENT)]


def project_keys(tokens, project, blocks):
    k = direction(matmul(tokens, project[:, D : 2 * D]), blocks).astype(BF)
    return k, matmul(tokens, project[:, 2 * D : 3 * D]).astype(BF)


def project_queries(tokens, project, blocks, scale):
    return (direction(matmul(tokens, project[:, 0:D]), blocks) * scale).astype(BF)


def setup_kernel(
    mats, first_scale, second_scale, staged, scales, order, blocks
):
    staged[...] = mats[...]
    scales[0:1] = scale_row(first_scale)
    scales[1:2] = scale_row(second_scale)
    order[...] = tile_order()
    blocks[...] = head_blocks()


def first_half(picked, keys, values, project, scale, output, gain, blocks):
    q = project_queries(picked, project, blocks, scale)
    windows = []
    for w in range(2):
        near, window = slice(w * 128, w * 128 + 128), slice(w * 256, w * 256 + 256)
        windows.append((q[near], keys[window], values[window], None))
    return finish(picked, attend(windows), output[...], gain[...]).astype(BF)


def first_edges_kernel(
    mix, latent_w, base, blocks, project, scales, output, gain,
    side0, side1, tokens, keys, values,
):
    levels = matmul_tn(mix[...], latent_w[...])
    for l in range(LATENT):
        merged = (levels[l * LANES : (l + 1) * LANES] + base[l : l + 1, :]).astype(BF)
        for side in range(2):
            for half in range(2):
                at, first = (side * 2 + half) * 128 + l * 32, half * 64 + side * 32
                tokens[at : at + 32] = merged[first : first + 32]
    keys[...], values[...] = project_keys(tokens[...], project, blocks[...])
    picked = jnp.concatenate([tokens[b * 32 : b * 32 + 16] for b in range(16)], axis=0)
    done = first_half(
        picked, keys, values, project, scales[0:1], output, gain, blocks[...]
    )
    for side, ref in enumerate((side0, side1)):
        for half in range(2):
            for l in range(LATENT):
                at = ((side * 2 + half) * LATENT + l) * 16
                ref[half * 16 : half * 16 + 16, l * D : (l + 1) * D] = done[at : at + 16]


def first_middle_kernel(
    tokens, keys, values, side0, side1, blocks, project, scales, output, gain, own0, own1
):
    picked = jnp.concatenate([tokens[b * 32 + 16 : b * 32 + 32] for b in range(16)], axis=0)
    done = first_half(
        picked, keys, values, project, scales[0:1], output, gain, blocks[...]
    )
    for half, own in enumerate((own0, own1)):
        own[0:16] = side0[half * 16 : half * 16 + 16]
        own[48:64] = side1[half * 16 : half * 16 + 16]
        for side in range(2):
            for l in range(LATENT):
                at = ((side * 2 + half) * LATENT + l) * 16
                own[16 + side * 16 : 32 + side * 16, l * D : (l + 1) * D] = done[at : at + 16]


PARTS = ((0, 16), (16, 32), (48, 16))


def tile_tokens(halves_of):
    return jnp.concatenate(
        [
            t
            for first, count in PARTS
            for ref in halves_of
            for t in block_tokens(ref, first, count)
        ],
        axis=0,
    )


def second_own_kernel(own0, own1, blocks, project, scales, queries, tokens, keys, values):
    tokens[...] = tile_tokens((own0, own1))
    keys[...], values[...] = project_keys(tokens[...], project, blocks[...])
    queries[...] = project_queries(tokens[...], project, blocks[...], scales[1:2])


def second_middle_kernel(half, *refs):
    far, queries, tokens, keys, values, blocks, project, output, gain = refs[:9]
    out, far_keys, far_values = refs[-3:]
    full = [t for first, count in PARTS for t in block_tokens(far, first, count)]
    full = jnp.concatenate(full, axis=0)
    far_keys[...], far_values[...] = project_keys(full, project, blocks[...])
    at = slice(128 + half * 128, 256 + half * 128)
    k = jnp.concatenate([keys[at], far_keys[64:192]], axis=0)
    v = jnp.concatenate([values[at], far_values[64:192]], axis=0)
    mixture = attend([(queries[at], k, v, None)])
    result = finish(tokens[at], mixture, output[...], gain[...]).astype(BF)
    if half == 0:
        out[...] = result
    else:
        both = jnp.concatenate([refs[9][...], result], axis=0)
        out[...] = matmul(middle_order(), both).reshape(64, LATENT, D).astype(BF)


def second_outer_kernel(
    beyond0, beyond1, corner0, corner1, queries, tokens, keys, values,
    far_keys0, far_values0, far_keys1, far_values1, middle, blocks, project, output, gain,
    out, halo_keys, halo_values, ends, sems,
):
    lat = lax.axis_index("lat")
    odd = lax.rem(lat, 2)
    nothing = (lat == 0) | (lat == lax.axis_size("lat") - 1)
    copies = [pltpu.make_async_copy(middle, out.at[pl.ds(32, 64)], sems.at[2])]
    for side in range(2):
        first = jnp.where(odd == side, 96, 0)
        copies.append(
            pltpu.make_async_copy(ends.at[side], out.at[pl.ds(first, 32)], sems.at[side])
        )
    copies[0].start()
    full = [
        t
        for side, beyond in enumerate((beyond0, beyond1))
        for half, corner in enumerate((corner0, corner1))
        for ref, at in ((beyond, half * 16), (corner, side * 16))
        for t in block_tokens(ref, at, 16)
    ]
    halo_keys[...], halo_values[...] = project_keys(
        jnp.concatenate(full, axis=0), project, blocks[...]
    )
    outside = (iota((256, LANES), 0) < 128) & nothing
    alive = [None, jnp.where(outside, 0.0, 1.0).astype(BF)]
    windows = []
    for side in range(2):
        for half in range(2):
            at, far = side * 384 + half * 64, side * 256 + half * 128
            at, far = slice(at, at + 64), slice(far, far + 128)
            side_at = slice(side * 192, side * 192 + 64)
            k = [halo_keys[far], keys[at], (far_keys0, far_keys1)[half][side_at]]
            v = [halo_values[far], values[at], (far_values0, far_values1)[half][side_at]]
            k, v = jnp.concatenate(k, axis=0), jnp.concatenate(v, axis=0)
            windows.append((queries[at], k, v, alive[side]))
    own = jnp.concatenate([tokens[0:128], tokens[384:512]], axis=0)
    mixture = attend(windows)
    result = finish(own, mixture, output[...], gain[...]).astype(BF)
    order = edge_order()
    for side in range(2):
        block = matmul(order, result[side * 128 : side * 128 + 128])
        ends[side] = block.reshape(32, LATENT, D).astype(BF)
        copies[1 + side].start()
    for copy in copies:
        copy.wait()


VMEM = pl.BlockSpec(memory_space=pltpu.VMEM)
HBM = pl.BlockSpec(memory_space=pltpu.HBM)
SMEM = pl.BlockSpec(memory_space=pltpu.SMEM)
MIB = 1024 * 1024


def swapped(value, axis, first):
    size = lax.axis_size(axis)
    step = 0 if first else 1
    route = [(i, ((i + step) ^ 1) - step) for i in range(size)]
    return lax.ppermute(value, axis, [(i, j % size) for i, j in route])


def swapped_inside(value):
    lons, lats = lax.axis_size("lon"), lax.axis_size("lat")
    route = []
    for lon in range(lons):
        for lat in range(lats):
            other = lat - 1 if lat % 2 == 0 else lat + 1
            inside = 0 <= other < lats
            target = (lon, other) if inside else (lon ^ 1, lat)
            route.append((lon * lats + lat, target[0] * lats + target[1]))
    return lax.ppermute(value, ("lon", "lat"), route)


def params(mib):
    return pltpu.CompilerParams(vmem_limit_bytes=mib * MIB)


def cost(microseconds):
    return pl.CostEstimate(
        flops=int(microseconds * 1e9), bytes_accessed=MIB, transcendentals=1 << 18
    )


def wide_rows(count):
    return jax.ShapeDtypeStruct((count, LATENT * D), BF)


def token_rows(count):
    return jax.ShapeDtypeStruct((count, D), BF)


def pack_kernel(x, out):
    out[...] = x[...].T


def pack_call(stripe):
    return pl.pallas_call(
        pack_kernel,
        out_shape=jax.ShapeDtypeStruct((LANES, LEVELS * PV), BF),
        in_specs=[VMEM],
        out_specs=VMEM,
        compiler_params=params(24),
        cost_estimate=cost(0.8),
        name="pack",
    )(stripe)


def fold_call(*operands):
    return pl.pallas_call(
        fold_kernel,
        out_shape=jax.ShapeDtypeStruct((GRAM + 192, 256), BF),
        in_specs=[HBM] * len(operands),
        out_specs=VMEM,
        scratch_shapes=[
            (pltpu.SMEM if x.shape == (HEADS,) else pltpu.VMEM)(x.shape, x.dtype) for x in operands
        ]
        + [pltpu.VMEM((128, D), F32), pltpu.SemaphoreType.DMA((len(operands),))],
        compiler_params=params(60),
        cost_estimate=cost(3.0),
        name="fold",
    )(*operands)


def encode_call(*operands):
    return pl.pallas_call(
        encode_kernel,
        out_shape=jax.ShapeDtypeStruct((D, LATENT * LANES), BF),
        in_specs=[VMEM] * len(operands),
        out_specs=VMEM,
        scratch_shapes=[
            pltpu.VMEM((256, LEVELS * LANES), BF),
            pltpu.VMEM((LEVELS * PV, LANES), BF),
            pltpu.VMEM((LEVELS, D, LANES), F32),
            pltpu.VMEM((LEVELS + 1, 64, LANES), F32),
        ],
        compiler_params=params(24),
        cost_estimate=cost(3.0),
        name="encode",
    )(*operands)


def setup_call(mats, first_scale, second_scale):
    square = lambda size: jax.ShapeDtypeStruct((size, size), BF)
    return pl.pallas_call(
        setup_kernel,
        out_shape=[
            jax.ShapeDtypeStruct(mats.shape, BF), jax.ShapeDtypeStruct((2, D), F32),
            square(128), square(256),
        ],
        in_specs=[VMEM, SMEM, SMEM],
        out_specs=[VMEM] * 4,
        compiler_params=params(24),
        cost_estimate=cost(0.8),
        name="setup",
    )(mats, first_scale, second_scale)


def first_edges_call(*operands):
    return pl.pallas_call(
        first_edges_kernel,
        out_shape=[wide_rows(32)] * 2 + [token_rows(512)] * 3,
        in_specs=[VMEM] * len(operands),
        out_specs=[VMEM] * 5,
        compiler_params=params(24),
        cost_estimate=cost(3.0),
        name="first_edges",
    )(*operands)


def first_middle_call(*operands):
    return pl.pallas_call(
        first_middle_kernel,
        out_shape=[wide_rows(64)] * 2,
        in_specs=[VMEM] * len(operands),
        out_specs=[VMEM] * 2,
        compiler_params=params(24),
        cost_estimate=cost(2.0),
        name="first_middle",
    )(*operands)


def second_own_call(*operands):
    return pl.pallas_call(
        second_own_kernel,
        out_shape=[token_rows(512)] * 4,
        in_specs=[VMEM] * len(operands),
        out_specs=[VMEM] * 4,
        compiler_params=params(24),
        cost_estimate=cost(1.3),
        name="second_own",
    )(*operands)


def second_middle_call(half, *operands):
    out = jax.ShapeDtypeStruct((64, LATENT, D), BF) if half else token_rows(128)
    return pl.pallas_call(
        functools.partial(second_middle_kernel, half),
        out_shape=[out] + [token_rows(256)] * 2,
        in_specs=[VMEM] * len(operands),
        out_specs=[VMEM] * 3,
        compiler_params=params(24),
        cost_estimate=cost(1.5),
        name=f"second_middle{half}",
    )(*operands)


def second_outer_call(*operands):
    return pl.pallas_call(
        second_outer_kernel,
        out_shape=jax.ShapeDtypeStruct((128, LATENT, D), BF),
        in_specs=[VMEM] * len(operands),
        out_specs=HBM,
        scratch_shapes=[pltpu.VMEM((512, D), BF)] * 2
        + [pltpu.VMEM((2, 32, LATENT, D), BF), pltpu.SemaphoreType.DMA((3,))],
        compiler_params=params(24),
        cost_estimate=cost(3.3),
        name="second_outer",
    )(*operands)


def per_device(
    fields,
    embed_weight,
    level_code,
    encoder_gain,
    key_weight,
    value_weight,
    latent_query,
    encoder_scale,
    latent_weight,
    latent_base,
    first_project,
    first_scale,
    first_output,
    first_gain,
    second_project,
    second_scale,
    second_output,
    second_gain,
):
    packed = pack_call(fields.reshape(LEVELS * PV, LANES))
    received = lax.all_to_all(packed, "lon", split_axis=0, concat_axis=0, tiled=True)
    mats = fold_call(
        embed_weight, level_code, encoder_gain.reshape(1, D), key_weight, value_weight,
        latent_query, encoder_scale,
    )
    mats, scales, order, blocks = setup_call(mats, first_scale, second_scale)
    mix = encode_call(received, order, mats)
    weights = (blocks, first_project, scales, first_output, first_gain.reshape(1, D))
    side0, side1, tokens, keys, values = first_edges_call(
        mix, latent_weight, latent_base, *weights
    )
    beyond1 = swapped_inside(side1)
    side0, side1 = lax.optimization_barrier((side0, side1))
    beyond0 = swapped(side0, "lat", True)
    beyond = [beyond0, beyond1]
    own = first_middle_call(tokens, keys, values, side0, side1, *weights)
    far = [swapped(own[0], "lon", True), swapped(own[1], "lon", False)]
    weights = (blocks, second_project, second_output, second_gain.reshape(1, D))
    mine = second_own_call(*own, blocks, second_project, scales)
    corners = [
        swapped(jnp.concatenate([x[i : i + 16] for x in beyond], axis=0), "lon", i == 0)
        for i in (0, 16)
    ]
    part, *far0 = second_middle_call(0, far[0], *mine, *weights)
    done, *far1 = second_middle_call(1, far[1], *mine, *weights, part)
    out = second_outer_call(*beyond, *corners, *mine, *far0, *far1, done, *weights)
    return out.reshape(16, 8, LATENT, D)


def solution(mesh):
    in_specs = (P("lat", "lon", None, None, None),) + (P(),) * 17
    out_specs = P("lat", "lon", None, None)
    return jax.shard_map(
        per_device, mesh=mesh, in_specs=in_specs, out_specs=out_specs, check_vma=False
    )
```

```python
import functools

import jax
import jax.numpy as jnp
from jax import lax
from jax.experimental import pallas as pl
from jax.experimental.pallas import tpu as pltpu
from jax.sharding import PartitionSpec as P

D = 512
HEADS = 16
LEVELS = 13
LATENT = 4
PV = 80
HEAD = 32
HALF = 4
LANES = 128
GROUPS = D // LANES
IN_GROUP = LANES // HEAD
NORM_EPS = 1e-05
DIR_EPS = 1e-06
GRAM = 2 * D
LOG2E = 1.4426950408889634
BF = jnp.bfloat16
F32 = jnp.float32
ENC_SPANS = [(0, 512), (512, 512), (1024, 512), (1536, 128)]


def iota(shape, dim):
    return lax.broadcasted_iota(jnp.int32, shape, dim)


def matmul(a, b):
    return jnp.dot(a, b, preferred_element_type=F32)


def matmul_nt(a, b):
    return lax.dot_general(a, b, (((1,), (1,)), ((), ())), preferred_element_type=F32)


def matmul_tn(a, b):
    return lax.dot_general(a, b, (((0,), (0,)), ((), ())), preferred_element_type=F32)


def halves(value):
    high = value.astype(BF)
    return high, (value - high.astype(F32)).astype(BF)


def scale_row(scale_ref):
    head = iota((1, D), 1) // HEAD
    row = jnp.zeros((1, D), F32)
    for h in range(HEADS):
        row = jnp.where(head == h, scale_ref[h] * LOG2E, row)
    return row


def head_blocks():
    return (iota((256, 256), 0) // HEAD == iota((256, 256), 1) // HEAD).astype(F32).astype(BF)


def head_squares(value, blocks):
    square = (value * value).astype(BF)
    return jnp.concatenate(
        [matmul(square[:, i : i + 256], blocks) for i in range(0, D, 256)], axis=1
    )


def direction(value, blocks):
    return value * lax.rsqrt(head_squares(value, blocks) + DIR_EPS)


def lane_masks():
    head = iota((1, LANES), 1) // HEAD
    return [(head == h).astype(F32).astype(BF) for h in range(IN_GROUP)]


def attend(windows):
    masks = lane_masks()
    groups = [slice(g * LANES, (g + 1) * LANES) for g in range(GROUPS)]
    weights = []
    for queries, keys, values, alive in windows:
        for lanes in groups:
            stacked = jnp.concatenate([queries[:, lanes] * m for m in masks], axis=0)
            weights.append(jnp.exp2(matmul_nt(stacked, keys[:, lanes])).astype(BF))
    mixtures = []
    for w, (queries, keys, values, alive) in enumerate(windows):
        count, tokens = queries.shape[0], keys.shape[0]
        head = iota((count, LANES), 1) // HEAD
        ones = jnp.ones((tokens, LANES), BF) if alive is None else alive
        parts = []
        for g, lanes in enumerate(groups):
            v = values[:, lanes] if alive is None else values[:, lanes] * alive
            both = matmul(weights[w * GROUPS + g], jnp.concatenate([v, ones], axis=1))
            picked = both[:count]
            over, under = picked[:, :LANES], picked[:, LANES:]
            for h in range(1, IN_GROUP):
                block = both[h * count : (h + 1) * count]
                over = jnp.where(head == h, block[:, :LANES], over)
                under = jnp.where(head == h, block[:, LANES:], under)
            parts.append((over / under).astype(BF))
        mixtures.append(jnp.concatenate(parts, axis=1))
    return jnp.concatenate(mixtures, axis=0)


def finish(tokens, mixture, output, gain):
    branch = matmul(mixture, output)
    centre = branch - jnp.mean(branch, axis=-1, keepdims=True)
    spread = jnp.mean(centre * centre, axis=-1, keepdims=True)
    return tokens.astype(F32) + centre * lax.rsqrt(spread + NORM_EPS) * gain


def fold_kernel(*refs):
    sources, mats, landed, wide, sems = refs[:7], refs[7], refs[8:15], refs[15], refs[16]
    copies = [
        pltpu.make_async_copy(source, target, sems.at[i])
        for i, (source, target) in enumerate(zip(sources, landed))
    ]
    embed, code, gain, key_w, value_w, query, scale = landed
    for copy in copies:
        copy.start()
    for copy in copies:
        copy.wait()
    wide[...] = jnp.zeros((128, D), F32)
    w = embed[...].astype(F32)
    wide[0:PV] = w - jnp.mean(w, axis=-1, keepdims=True)
    c = code[...]
    wide[PV : PV + LEVELS] = c - jnp.mean(c, axis=-1, keepdims=True)
    centred = wide[...]
    high, low = halves(centred * gain[...])
    both = jnp.concatenate([high, low], axis=0)
    for i, weight in enumerate((key_w, value_w)):
        product = matmul(both, weight[...])
        product = product[:128] + product[128:]
        h, l = halves(product.T)
        mats[i * D : (i + 1) * D] = jnp.concatenate([h, l], axis=1)
        if i == 0:
            own = iota((HEADS, D), 1) // HEAD == iota((HEADS, D), 0)
            rows = jnp.concatenate(
                [jnp.where(own, query[l : l + 1, :], 0.0) for l in range(LATENT)], axis=0
            )
            length = jnp.sum(rows * rows, axis=-1, keepdims=True) + DIR_EPS
            rows = (rows * lax.rsqrt(length) * scale_row(scale)).astype(BF)
            kh, kl = halves(product)
            raw = matmul_nt(rows, kh) + matmul_nt(rows, kl)
            h, l = halves(raw)
            mats[GRAM + 128 : GRAM + 192] = jnp.concatenate([h, l], axis=1)
    h, l = halves(centred)
    cross = matmul_nt(h, l)
    h, l = halves((matmul_nt(h, h) + (cross + cross.T)) * (1.0 / D))
    mats[GRAM : GRAM + 128] = jnp.concatenate([h, l], axis=1)


def encode_kernel(x, order, mats, mix, f2, flat, vals, wts):
    flat[...] = matmul(order[...], x[...]).astype(BF).T
    level = (iota((48, LEVELS * LANES), 0) == iota((48, LEVELS * LANES), 1) // LANES)
    level = level.astype(F32).astype(BF)
    for top in (0, 128):
        f2[top + PV : top + 128, :] = level
        for k in range(LEVELS):
            f2[top : top + PV, k * LANES : (k + 1) * LANES] = flat[k * PV : (k + 1) * PV]

    gather = (iota((HEADS, 128), 1) // 8 == iota((HEADS, 128), 0)).astype(F32).astype(BF)
    total = jnp.zeros((64, LANES), F32)
    for start, width in ENC_SPANS:
        rhs = f2[:, start : start + width]
        keys = matmul(mats[0:D], rhs)
        part = jnp.sum((keys * keys).reshape(HEADS, 4, 8, width), axis=1).reshape(128, width)
        squares = matmul(gather, part.astype(BF))
        square = matmul(mats[GRAM : GRAM + 128], rhs) * f2[0:128, start : start + width].astype(F32)
        part = jnp.sum(square.reshape(16, 8, width), axis=0)
        spread = jnp.maximum(jnp.sum(part, axis=0, keepdims=True), 0.0) + NORM_EPS
        factor = lax.rsqrt(squares + DIR_EPS * spread)
        scores = matmul(mats[GRAM + 128 : GRAM + 192], rhs) * jnp.concatenate([factor] * LATENT, axis=0)
        weights = jnp.exp2(scores)
        scaled = weights * lax.rsqrt(spread)
        values = matmul(mats[D : 2 * D], rhs)
        for i in range(width // LANES):
            k = start // LANES + i
            lanes = slice(i * LANES, (i + 1) * LANES)
            total = total + weights[:, lanes]
            wts[k] = scaled[:, lanes]
            vals[k] = values[:, lanes]
    wts[LEVELS] = 1.0 / total

    for h in range(HEADS):
        rows = slice(h * HEAD, (h + 1) * HEAD)
        sums = [jnp.zeros((HEAD, LANES), F32) for _ in range(LATENT)]
        for k in range(LEVELS):
            v = vals[k, rows, :]
            for l in range(LATENT):
                sums[l] = sums[l] + wts[k, l * HEADS + h : l * HEADS + h + 1, :] * v
        for l in range(LATENT):
            r = wts[LEVELS, l * HEADS + h : l * HEADS + h + 1, :]
            mix[rows, l * LANES : (l + 1) * LANES] = (sums[l] * r).astype(BF)


def parities():
    lat, lon = lax.axis_index("lat"), lax.axis_index("lon")
    return lax.rem(lat, 2), lax.rem(lon, 2)


def one_hot(source, size):
    return (source == iota((size, size), 1)).astype(F32).astype(BF)


def tile_order():
    odd_lat, odd_lon = parities()
    i = iota((128, 128), 0)
    half, side, inner, row, column = i // 64, (i // 32) % 2, (i // 16) % 2, (i // 4) % 4, i % 4
    start = jnp.where(side == 1 - odd_lat, 4 * inner, 12 - 4 * inner)
    right = jnp.where(odd_lon == 1, half, 1 - half)
    return one_hot((start + row) * 8 + right * 4 + column, 128)


def edge_order():
    odd_lat, odd_lon = parities()
    i = iota((128, 128), 0)
    row, right, column, level = i // 32, (i // 16) % 2, (i // 4) % 4, i % 4
    half = jnp.where(odd_lon == 1, right, 1 - right)
    return one_hot(half * 64 + level * 16 + row * 4 + column, 128)


def middle_order():
    odd_lat, odd_lon = parities()
    i = iota((256, 256), 0)
    window, row, right = i // 128, (i // 32) % 4, (i // 16) % 2
    column, level = (i // 4) % 4, i % 4
    half = jnp.where(odd_lon == 1, right, 1 - right)
    side = jnp.where(odd_lat == 1, window, 1 - window)
    return one_hot(half * 128 + level * 32 + side * 16 + row * 4 + column, 256)


def block_tokens(ref, first, count):
    return [ref[first : first + count, l * D : (l + 1) * D] for l in range(LATENT)]


def project_keys(tokens, project, blocks):
    k = direction(matmul(tokens, project[:, D : 2 * D]), blocks).astype(BF)
    return k, matmul(tokens, project[:, 2 * D : 3 * D]).astype(BF)


def project_queries(tokens, project, blocks, scale):
    return (direction(matmul(tokens, project[:, 0:D]), blocks) * scale).astype(BF)


def setup_kernel(
    mats, first_scale, second_scale, staged, scales, order, blocks
):
    staged[...] = mats[...]
    scales[0:1] = scale_row(first_scale)
    scales[1:2] = scale_row(second_scale)
    order[...] = tile_order()
    blocks[...] = head_blocks()


def first_half(picked, keys, values, project, scale, output, gain, blocks):
    q = project_queries(picked, project, blocks, scale)
    windows = []
    for w in range(2):
        near, window = slice(w * 128, w * 128 + 128), slice(w * 256, w * 256 + 256)
        windows.append((q[near], keys[window], values[window], None))
    return finish(picked, attend(windows), output[...], gain[...]).astype(BF)


def first_edges_kernel(
    mix, latent_w, base, blocks, project, scales, output, gain,
    side0, side1, tokens, keys, values,
):
    levels = matmul_tn(mix[...], latent_w[...])
    for l in range(LATENT):
        merged = (levels[l * LANES : (l + 1) * LANES] + base[l : l + 1, :]).astype(BF)
        for side in range(2):
            for half in range(2):
                at, first = (side * 2 + half) * 128 + l * 32, half * 64 + side * 32
                tokens[at : at + 32] = merged[first : first + 32]
    keys[...], values[...] = project_keys(tokens[...], project, blocks[...])
    picked = jnp.concatenate([tokens[b * 32 : b * 32 + 16] for b in range(16)], axis=0)
    done = first_half(
        picked, keys, values, project, scales[0:1], output, gain, blocks[...]
    )
    for side, ref in enumerate((side0, side1)):
        for half in range(2):
            for l in range(LATENT):
                at = ((side * 2 + half) * LATENT + l) * 16
                ref[half * 16 : half * 16 + 16, l * D : (l + 1) * D] = done[at : at + 16]


def first_middle_kernel(
    tokens, keys, values, side0, side1, blocks, project, scales, output, gain, own0, own1
):
    picked = jnp.concatenate([tokens[b * 32 + 16 : b * 32 + 32] for b in range(16)], axis=0)
    done = first_half(
        picked, keys, values, project, scales[0:1], output, gain, blocks[...]
    )
    for half, own in enumerate((own0, own1)):
        own[0:16] = side0[half * 16 : half * 16 + 16]
        own[48:64] = side1[half * 16 : half * 16 + 16]
        for side in range(2):
            for l in range(LATENT):
                at = ((side * 2 + half) * LATENT + l) * 16
                own[16 + side * 16 : 32 + side * 16, l * D : (l + 1) * D] = done[at : at + 16]


PARTS = ((0, 16), (16, 32), (48, 16))


def tile_tokens(halves_of):
    return jnp.concatenate(
        [
            t
            for first, count in PARTS
            for ref in halves_of
            for t in block_tokens(ref, first, count)
        ],
        axis=0,
    )


def second_own_kernel(own0, own1, blocks, project, scales, queries, tokens, keys, values):
    tokens[...] = tile_tokens((own0, own1))
    keys[...], values[...] = project_keys(tokens[...], project, blocks[...])
    queries[...] = project_queries(tokens[...], project, blocks[...], scales[1:2])


def second_middle_kernel(half, *refs):
    far, queries, tokens, keys, values, blocks, project, output, gain = refs[:9]
    out, far_keys, far_values = refs[-3:]
    full = [t for first, count in PARTS for t in block_tokens(far, first, count)]
    full = jnp.concatenate(full, axis=0)
    far_keys[...], far_values[...] = project_keys(full, project, blocks[...])
    at = slice(128 + half * 128, 256 + half * 128)
    k = jnp.concatenate([keys[at], far_keys[64:192]], axis=0)
    v = jnp.concatenate([values[at], far_values[64:192]], axis=0)
    mixture = attend([(queries[at], k, v, None)])
    result = finish(tokens[at], mixture, output[...], gain[...]).astype(BF)
    if half == 0:
        out[...] = result
    else:
        both = jnp.concatenate([refs[9][...], result], axis=0)
        out[...] = matmul(middle_order(), both).reshape(64, LATENT, D).astype(BF)


def second_outer_kernel(
    beyond0, beyond1, corner0, corner1, queries, tokens, keys, values,
    far_keys0, far_values0, far_keys1, far_values1, middle, blocks, project, output, gain,
    out, halo_keys, halo_values, ends, sems,
):
    lat = lax.axis_index("lat")
    odd = lax.rem(lat, 2)
    nothing = (lat == 0) | (lat == lax.axis_size("lat") - 1)
    copies = [pltpu.make_async_copy(middle, out.at[pl.ds(32, 64)], sems.at[2])]
    for side in range(2):
        first = jnp.where(odd == side, 96, 0)
        copies.append(
            pltpu.make_async_copy(ends.at[side], out.at[pl.ds(first, 32)], sems.at[side])
        )
    copies[0].start()
    full = [
        t
        for side, beyond in enumerate((beyond0, beyond1))
        for half, corner in enumerate((corner0, corner1))
        for ref, at in ((beyond, half * 16), (corner, side * 16))
        for t in block_tokens(ref, at, 16)
    ]
    halo_keys[...], halo_values[...] = project_keys(
        jnp.concatenate(full, axis=0), project, blocks[...]
    )
    outside = (iota((256, LANES), 0) < 128) & nothing
    alive = [None, jnp.where(outside, 0.0, 1.0).astype(BF)]
    windows = []
    for side in range(2):
        for half in range(2):
            at, far = side * 384 + half * 64, side * 256 + half * 128
            at, far = slice(at, at + 64), slice(far, far + 128)
            side_at = slice(side * 192, side * 192 + 64)
            k = [halo_keys[far], keys[at], (far_keys0, far_keys1)[half][side_at]]
            v = [halo_values[far], values[at], (far_values0, far_values1)[half][side_at]]
            k, v = jnp.concatenate(k, axis=0), jnp.concatenate(v, axis=0)
            windows.append((queries[at], k, v, alive[side]))
    own = jnp.concatenate([tokens[0:128], tokens[384:512]], axis=0)
    mixture = attend(windows)
    result = finish(own, mixture, output[...], gain[...]).astype(BF)
    order = edge_order()
    for side in range(2):
        block = matmul(order, result[side * 128 : side * 128 + 128])
        ends[side] = block.reshape(32, LATENT, D).astype(BF)
        copies[1 + side].start()
    for copy in copies:
        copy.wait()


VMEM = pl.BlockSpec(memory_space=pltpu.VMEM)
HBM = pl.BlockSpec(memory_space=pltpu.HBM)
SMEM = pl.BlockSpec(memory_space=pltpu.SMEM)
MIB = 1024 * 1024


def swapped(value, axis, first):
    size = lax.axis_size(axis)
    step = 0 if first else 1
    route = [(i, ((i + step) ^ 1) - step) for i in range(size)]
    return lax.ppermute(value, axis, [(i, j % size) for i, j in route])


def swapped_inside(value):
    lons, lats = lax.axis_size("lon"), lax.axis_size("lat")
    route = []
    for lon in range(lons):
        for lat in range(lats):
            other = lat - 1 if lat % 2 == 0 else lat + 1
            inside = 0 <= other < lats
            target = (lon, other) if inside else (lon ^ 1, lat)
            route.append((lon * lats + lat, target[0] * lats + target[1]))
    return lax.ppermute(value, ("lon", "lat"), route)


def params(mib):
    return pltpu.CompilerParams(vmem_limit_bytes=mib * MIB)


def cost(microseconds):
    return pl.CostEstimate(
        flops=int(microseconds * 1e9), bytes_accessed=MIB, transcendentals=1 << 18
    )


def wide_rows(count):
    return jax.ShapeDtypeStruct((count, LATENT * D), BF)


def token_rows(count):
    return jax.ShapeDtypeStruct((count, D), BF)


def pack_kernel(x, out):
    out[...] = x[...].T


def pack_call(stripe):
    return pl.pallas_call(
        pack_kernel,
        out_shape=jax.ShapeDtypeStruct((LANES, LEVELS * PV), BF),
        in_specs=[VMEM],
        out_specs=VMEM,
        compiler_params=params(24),
        cost_estimate=cost(0.8),
        name="pack",
    )(stripe)


def fold_call(*operands):
    return pl.pallas_call(
        fold_kernel,
        out_shape=jax.ShapeDtypeStruct((GRAM + 192, 256), BF),
        in_specs=[HBM] * len(operands),
        out_specs=VMEM,
        scratch_shapes=[
            (pltpu.SMEM if x.shape == (HEADS,) else pltpu.VMEM)(x.shape, x.dtype) for x in operands
        ]
        + [pltpu.VMEM((128, D), F32), pltpu.SemaphoreType.DMA((len(operands),))],
        compiler_params=params(60),
        cost_estimate=cost(3.0),
        name="fold",
    )(*operands)


def encode_call(*operands):
    return pl.pallas_call(
        encode_kernel,
        out_shape=jax.ShapeDtypeStruct((D, LATENT * LANES), BF),
        in_specs=[VMEM] * len(operands),
        out_specs=VMEM,
        scratch_shapes=[
            pltpu.VMEM((256, LEVELS * LANES), BF),
            pltpu.VMEM((LEVELS * PV, LANES), BF),
            pltpu.VMEM((LEVELS, D, LANES), F32),
            pltpu.VMEM((LEVELS + 1, 64, LANES), F32),
        ],
        compiler_params=params(24),
        cost_estimate=cost(3.0),
        name="encode",
    )(*operands)


def setup_call(mats, first_scale, second_scale):
    square = lambda size: jax.ShapeDtypeStruct((size, size), BF)
    return pl.pallas_call(
        setup_kernel,
        out_shape=[
            jax.ShapeDtypeStruct(mats.shape, BF), jax.ShapeDtypeStruct((2, D), F32),
            square(128), square(256),
        ],
        in_specs=[VMEM, SMEM, SMEM],
        out_specs=[VMEM] * 4,
        compiler_params=params(24),
        cost_estimate=cost(0.8),
        name="setup",
    )(mats, first_scale, second_scale)


def first_edges_call(*operands):
    return pl.pallas_call(
        first_edges_kernel,
        out_shape=[wide_rows(32)] * 2 + [token_rows(512)] * 3,
        in_specs=[VMEM] * len(operands),
        out_specs=[VMEM] * 5,
        compiler_params=params(24),
        cost_estimate=cost(3.0),
        name="first_edges",
    )(*operands)


def first_middle_call(*operands):
    return pl.pallas_call(
        first_middle_kernel,
        out_shape=[wide_rows(64)] * 2,
        in_specs=[VMEM] * len(operands),
        out_specs=[VMEM] * 2,
        compiler_params=params(24),
        cost_estimate=cost(2.0),
        name="first_middle",
    )(*operands)


def second_own_call(*operands):
    return pl.pallas_call(
        second_own_kernel,
        out_shape=[token_rows(512)] * 4,
        in_specs=[VMEM] * len(operands),
        out_specs=[VMEM] * 4,
        compiler_params=params(24),
        cost_estimate=cost(1.3),
        name="second_own",
    )(*operands)


def second_middle_call(half, *operands):
    out = jax.ShapeDtypeStruct((64, LATENT, D), BF) if half else token_rows(128)
    return pl.pallas_call(
        functools.partial(second_middle_kernel, half),
        out_shape=[out] + [token_rows(256)] * 2,
        in_specs=[VMEM] * len(operands),
        out_specs=[VMEM] * 3,
        compiler_params=params(24),
        cost_estimate=cost(1.5),
        name=f"second_middle{half}",
    )(*operands)


def second_outer_call(*operands):
    return pl.pallas_call(
        second_outer_kernel,
        out_shape=jax.ShapeDtypeStruct((128, LATENT, D), BF),
        in_specs=[VMEM] * len(operands),
        out_specs=HBM,
        scratch_shapes=[pltpu.VMEM((512, D), BF)] * 2
        + [pltpu.VMEM((2, 32, LATENT, D), BF), pltpu.SemaphoreType.DMA((3,))],
        compiler_params=params(24),
        cost_estimate=cost(3.3),
        name="second_outer",
    )(*operands)


def per_device(
    fields,
    embed_weight,
    level_code,
    encoder_gain,
    key_weight,
    value_weight,
    latent_query,
    encoder_scale,
    latent_weight,
    latent_base,
    first_project,
    first_scale,
    first_output,
    first_gain,
    second_project,
    second_scale,
    second_output,
    second_gain,
):
    packed = pack_call(fields.reshape(LEVELS * PV, LANES))
    received = lax.all_to_all(packed, "lon", split_axis=0, concat_axis=0, tiled=True)
    mats = fold_call(
        embed_weight, level_code, encoder_gain.reshape(1, D), key_weight, value_weight,
        latent_query, encoder_scale,
    )
    mats, scales, order, blocks = setup_call(mats, first_scale, second_scale)
    mix = encode_call(received, order, mats)
    weights = (blocks, first_project, scales, first_output, first_gain.reshape(1, D))
    side0, side1, tokens, keys, values = first_edges_call(
        mix, latent_weight, latent_base, *weights
    )
    beyond1 = swapped_inside(side1)
    side0, side1 = lax.optimization_barrier((side0, side1))
    beyond0 = swapped(side0, "lat", True)
    beyond = [beyond0, beyond1]
    own = first_middle_call(tokens, keys, values, side0, side1, *weights)
    far = [swapped(own[0], "lon", True), swapped(own[1], "lon", False)]
    weights = (blocks, second_project, second_output, second_gain.reshape(1, D))
    ends = [jnp.concatenate([x[i : i + 16] for x in beyond], axis=0) for i in (0, 16)]
    own, ends = lax.optimization_barrier((own, ends))
    corners = [swapped(ends[0], "lon", True), swapped(ends[1], "lon", False)]
    mine = second_own_call(*own, blocks, second_project, scales)
    part, *far0 = second_middle_call(0, far[0], *mine, *weights)
    done, *far1 = second_middle_call(1, far[1], *mine, *weights, part)
    out = second_outer_call(*beyond, *corners, *mine, *far0, *far1, done, *weights)
    return out.reshape(16, 8, LATENT, D)


def solution(mesh):
    in_specs = (P("lat", "lon", None, None, None),) + (P(),) * 17
    out_specs = P("lat", "lon", None, None)
    return jax.shard_map(
        per_device, mesh=mesh, in_specs=in_specs, out_specs=out_specs, check_vma=False
    )
```

```python
import jax
import jax.numpy as jnp
from jax import lax
from jax.experimental import pallas as pl
from jax.experimental.pallas import tpu as pltpu
from jax.sharding import PartitionSpec as P

D = 512
HEADS = 16
LEVELS = 13
LATENT = 4
PV = 80
HEAD = 32
HALF = 4
LANES = 128
GROUPS = D // LANES
IN_GROUP = LANES // HEAD
NORM_EPS = 1e-05
DIR_EPS = 1e-06
GRAM = 2 * D
LOG2E = 1.4426950408889634
BF = jnp.bfloat16
F32 = jnp.float32
ENC_SPANS = [(0, 512), (512, 512), (1024, 512), (1536, 128)]


def iota(shape, dim):
    return lax.broadcasted_iota(jnp.int32, shape, dim)


def matmul(a, b):
    return jnp.dot(a, b, preferred_element_type=F32)


def matmul_nt(a, b):
    return lax.dot_general(a, b, (((1,), (1,)), ((), ())), preferred_element_type=F32)


def matmul_tn(a, b):
    return lax.dot_general(a, b, (((0,), (0,)), ((), ())), preferred_element_type=F32)


def halves(value):
    high = value.astype(BF)
    return high, (value - high.astype(F32)).astype(BF)


def scale_row(scale_ref):
    head = iota((1, D), 1) // HEAD
    row = jnp.zeros((1, D), F32)
    for h in range(HEADS):
        row = jnp.where(head == h, scale_ref[h] * LOG2E, row)
    return row


def head_blocks():
    return (iota((256, 256), 0) // HEAD == iota((256, 256), 1) // HEAD).astype(F32).astype(BF)


def head_squares(value, blocks):
    square = (value * value).astype(BF)
    return jnp.concatenate(
        [matmul(square[:, i : i + 256], blocks) for i in range(0, D, 256)], axis=1
    )


def direction(value, blocks):
    return value * lax.rsqrt(head_squares(value, blocks) + DIR_EPS)


def lane_masks():
    head = iota((1, LANES), 1) // HEAD
    return [(head == h).astype(F32).astype(BF) for h in range(IN_GROUP)]


def attend(windows):
    masks = lane_masks()
    groups = [slice(g * LANES, (g + 1) * LANES) for g in range(GROUPS)]
    weights = []
    for queries, keys, values, alive in windows:
        for lanes in groups:
            stacked = jnp.concatenate([queries[:, lanes] * m for m in masks], axis=0)
            weights.append(jnp.exp2(matmul_nt(stacked, keys[:, lanes])).astype(BF))
    mixtures = []
    for w, (queries, keys, values, alive) in enumerate(windows):
        count, tokens = queries.shape[0], keys.shape[0]
        head = iota((count, LANES), 1) // HEAD
        ones = jnp.ones((tokens, LANES), BF) if alive is None else alive
        parts = []
        for g, lanes in enumerate(groups):
            v = values[:, lanes] if alive is None else values[:, lanes] * alive
            both = matmul(weights[w * GROUPS + g], jnp.concatenate([v, ones], axis=1))
            picked = both[:count]
            over, under = picked[:, :LANES], picked[:, LANES:]
            for h in range(1, IN_GROUP):
                block = both[h * count : (h + 1) * count]
                over = jnp.where(head == h, block[:, :LANES], over)
                under = jnp.where(head == h, block[:, LANES:], under)
            parts.append((over / under).astype(BF))
        mixtures.append(jnp.concatenate(parts, axis=1))
    return jnp.concatenate(mixtures, axis=0)


def finish(tokens, mixture, output, gain):
    branch = matmul(mixture, output)
    centre = branch - jnp.mean(branch, axis=-1, keepdims=True)
    spread = jnp.mean(centre * centre, axis=-1, keepdims=True)
    return tokens.astype(F32) + centre * lax.rsqrt(spread + NORM_EPS) * gain


def fold_kernel(*refs):
    sources, mats, landed, wide, sems = refs[:7], refs[7], refs[8:15], refs[15], refs[16]
    copies = [
        pltpu.make_async_copy(source, target, sems.at[i])
        for i, (source, target) in enumerate(zip(sources, landed))
    ]
    embed, code, gain, key_w, value_w, query, scale = landed
    for copy in copies:
        copy.start()
    for copy in copies:
        copy.wait()
    wide[...] = jnp.zeros((128, D), F32)
    w = embed[...].astype(F32)
    wide[0:PV] = w - jnp.mean(w, axis=-1, keepdims=True)
    c = code[...]
    wide[PV : PV + LEVELS] = c - jnp.mean(c, axis=-1, keepdims=True)
    centred = wide[...]
    high, low = halves(centred * gain[...])
    both = jnp.concatenate([high, low], axis=0)
    for i, weight in enumerate((key_w, value_w)):
        product = matmul(both, weight[...])
        product = product[:128] + product[128:]
        h, l = halves(product.T)
        mats[i * D : (i + 1) * D] = jnp.concatenate([h, l], axis=1)
        if i == 0:
            own = iota((HEADS, D), 1) // HEAD == iota((HEADS, D), 0)
            rows = jnp.concatenate(
                [jnp.where(own, query[l : l + 1, :], 0.0) for l in range(LATENT)], axis=0
            )
            length = jnp.sum(rows * rows, axis=-1, keepdims=True) + DIR_EPS
            rows = (rows * lax.rsqrt(length) * scale_row(scale)).astype(BF)
            kh, kl = halves(product)
            raw = matmul_nt(rows, kh) + matmul_nt(rows, kl)
            h, l = halves(raw)
            mats[GRAM + 128 : GRAM + 192] = jnp.concatenate([h, l], axis=1)
    h, l = halves(centred)
    cross = matmul_nt(h, l)
    h, l = halves((matmul_nt(h, h) + (cross + cross.T)) * (1.0 / D))
    mats[GRAM : GRAM + 128] = jnp.concatenate([h, l], axis=1)


def encode_kernel(x, order, mats, mix, f2, flat, vals, wts):
    flat[...] = matmul(order[...], x[...]).astype(BF).T
    level = (iota((48, LEVELS * LANES), 0) == iota((48, LEVELS * LANES), 1) // LANES)
    level = level.astype(F32).astype(BF)
    for top in (0, 128):
        f2[top + PV : top + 128, :] = level
        for k in range(LEVELS):
            f2[top : top + PV, k * LANES : (k + 1) * LANES] = flat[k * PV : (k + 1) * PV]

    gather = (iota((HEADS, 128), 1) // 8 == iota((HEADS, 128), 0)).astype(F32).astype(BF)
    total = jnp.zeros((64, LANES), F32)
    for start, width in ENC_SPANS:
        rhs = f2[:, start : start + width]
        keys = matmul(mats[0:D], rhs)
        part = jnp.sum((keys * keys).reshape(HEADS, 4, 8, width), axis=1).reshape(128, width)
        squares = matmul(gather, part.astype(BF))
        square = matmul(mats[GRAM : GRAM + 128], rhs) * f2[0:128, start : start + width].astype(F32)
        part = jnp.sum(square.reshape(16, 8, width), axis=0)
        spread = jnp.maximum(jnp.sum(part, axis=0, keepdims=True), 0.0) + NORM_EPS
        factor = lax.rsqrt(squares + DIR_EPS * spread)
        scores = matmul(mats[GRAM + 128 : GRAM + 192], rhs) * jnp.concatenate([factor] * LATENT, axis=0)
        weights = jnp.exp2(scores)
        scaled = weights * lax.rsqrt(spread)
        values = matmul(mats[D : 2 * D], rhs)
        for i in range(width // LANES):
            k = start // LANES + i
            lanes = slice(i * LANES, (i + 1) * LANES)
            total = total + weights[:, lanes]
            wts[k] = scaled[:, lanes]
            vals[k] = values[:, lanes]
    wts[LEVELS] = 1.0 / total

    for h in range(HEADS):
        rows = slice(h * HEAD, (h + 1) * HEAD)
        sums = [jnp.zeros((HEAD, LANES), F32) for _ in range(LATENT)]
        for k in range(LEVELS):
            v = vals[k, rows, :]
            for l in range(LATENT):
                sums[l] = sums[l] + wts[k, l * HEADS + h : l * HEADS + h + 1, :] * v
        for l in range(LATENT):
            r = wts[LEVELS, l * HEADS + h : l * HEADS + h + 1, :]
            mix[rows, l * LANES : (l + 1) * LANES] = (sums[l] * r).astype(BF)


def parities():
    lat, lon = lax.axis_index("lat"), lax.axis_index("lon")
    return lax.rem(lat, 2), lax.rem(lon, 2)


def one_hot(source, size):
    return (source == iota((size, size), 1)).astype(F32).astype(BF)


def tile_order():
    odd_lat, odd_lon = parities()
    i = iota((128, 128), 0)
    half, side, inner, row, column = i // 64, (i // 32) % 2, (i // 16) % 2, (i // 4) % 4, i % 4
    start = jnp.where(side == 1 - odd_lat, 4 * inner, 12 - 4 * inner)
    right = jnp.where(odd_lon == 1, half, 1 - half)
    return one_hot((start + row) * 8 + right * 4 + column, 128)


def edge_order():
    odd_lat, odd_lon = parities()
    i = iota((128, 128), 0)
    row, right, column, level = i // 32, (i // 16) % 2, (i // 4) % 4, i % 4
    half = jnp.where(odd_lon == 1, right, 1 - right)
    return one_hot(half * 64 + level * 16 + row * 4 + column, 128)


def middle_order():
    odd_lat, odd_lon = parities()
    i = iota((256, 256), 0)
    window, row, right = i // 128, (i // 32) % 4, (i // 16) % 2
    column, level = (i // 4) % 4, i % 4
    half = jnp.where(odd_lon == 1, right, 1 - right)
    side = jnp.where(odd_lat == 1, window, 1 - window)
    return one_hot(half * 128 + level * 32 + side * 16 + row * 4 + column, 256)


def block_tokens(ref, first, count):
    return [ref[first : first + count, l * D : (l + 1) * D] for l in range(LATENT)]


def project_keys(tokens, project, blocks):
    k = direction(matmul(tokens, project[:, D : 2 * D]), blocks).astype(BF)
    return k, matmul(tokens, project[:, 2 * D : 3 * D]).astype(BF)


def project_queries(tokens, project, blocks, scale):
    return (direction(matmul(tokens, project[:, 0:D]), blocks) * scale).astype(BF)


def setup_kernel(
    mats, first_scale, second_scale, staged, scales, order, blocks
):
    staged[...] = mats[...]
    scales[0:1] = scale_row(first_scale)
    scales[1:2] = scale_row(second_scale)
    order[...] = tile_order()
    blocks[...] = head_blocks()


def first_half(picked, keys, values, project, scale, output, gain, blocks):
    q = project_queries(picked, project, blocks, scale)
    windows = []
    for w in range(2):
        near, window = slice(w * 128, w * 128 + 128), slice(w * 256, w * 256 + 256)
        windows.append((q[near], keys[window], values[window], None))
    return finish(picked, attend(windows), output[...], gain[...]).astype(BF)


def first_edges_kernel(
    mix, latent_w, base, blocks, project, scales, output, gain,
    side0, side1, tokens, keys, values,
):
    levels = matmul_tn(mix[...], latent_w[...])
    for l in range(LATENT):
        merged = (levels[l * LANES : (l + 1) * LANES] + base[l : l + 1, :]).astype(BF)
        for side in range(2):
            for half in range(2):
                at, first = (side * 2 + half) * 128 + l * 32, half * 64 + side * 32
                tokens[at : at + 32] = merged[first : first + 32]
    keys[...], values[...] = project_keys(tokens[...], project, blocks[...])
    picked = jnp.concatenate([tokens[b * 32 : b * 32 + 16] for b in range(16)], axis=0)
    done = first_half(
        picked, keys, values, project, scales[0:1], output, gain, blocks[...]
    )
    for side, ref in enumerate((side0, side1)):
        for half in range(2):
            for l in range(LATENT):
                at = ((side * 2 + half) * LATENT + l) * 16
                ref[half * 16 : half * 16 + 16, l * D : (l + 1) * D] = done[at : at + 16]


def first_middle_kernel(
    tokens, keys, values, side0, side1, blocks, project, scales, output, gain, own0, own1
):
    picked = jnp.concatenate([tokens[b * 32 + 16 : b * 32 + 32] for b in range(16)], axis=0)
    done = first_half(
        picked, keys, values, project, scales[0:1], output, gain, blocks[...]
    )
    for half, own in enumerate((own0, own1)):
        own[0:16] = side0[half * 16 : half * 16 + 16]
        own[48:64] = side1[half * 16 : half * 16 + 16]
        for side in range(2):
            for l in range(LATENT):
                at = ((side * 2 + half) * LATENT + l) * 16
                own[16 + side * 16 : 32 + side * 16, l * D : (l + 1) * D] = done[at : at + 16]


PARTS = ((0, 16), (16, 32), (48, 16))


def tile_tokens(halves_of):
    return jnp.concatenate(
        [
            t
            for first, count in PARTS
            for ref in halves_of
            for t in block_tokens(ref, first, count)
        ],
        axis=0,
    )


def second_own_kernel(
    own0, own1, far, blocks, project, scales, output, gain,
    queries, tokens, keys, values, out, far_keys, far_values,
):
    tokens[...] = tile_tokens((own0, own1))
    keys[...], values[...] = project_keys(tokens[...], project, blocks[...])
    queries[...] = project_queries(tokens[...], project, blocks[...], scales[1:2])
    middle_windows(
        0, far, queries, tokens, keys, values, blocks, project, output, gain, out, far_keys,
        far_values,
    )


def middle_windows(
    half, far, queries, tokens, keys, values, blocks, project, output, gain, out, far_keys,
    far_values, before=None,
):
    full = [t for first, count in PARTS for t in block_tokens(far, first, count)]
    full = jnp.concatenate(full, axis=0)
    far_keys[...], far_values[...] = project_keys(full, project, blocks[...])
    at = slice(128 + half * 128, 256 + half * 128)
    k = jnp.concatenate([keys[at], far_keys[64:192]], axis=0)
    v = jnp.concatenate([values[at], far_values[64:192]], axis=0)
    mixture = attend([(queries[at], k, v, None)])
    result = finish(tokens[at], mixture, output[...], gain[...]).astype(BF)
    if before is None:
        out[...] = result
    else:
        both = jnp.concatenate([before[...], result], axis=0)
        out[...] = matmul(middle_order(), both).reshape(64, LATENT, D).astype(BF)


def second_middle_kernel(*refs):
    middle_windows(1, *refs[:9], *refs[-3:], before=refs[9])


def second_outer_kernel(
    beyond0, beyond1, corner0, corner1, queries, tokens, keys, values,
    far_keys0, far_values0, far_keys1, far_values1, middle, blocks, project, output, gain,
    out, halo_keys, halo_values, ends, sems,
):
    lat = lax.axis_index("lat")
    odd = lax.rem(lat, 2)
    nothing = (lat == 0) | (lat == lax.axis_size("lat") - 1)
    copies = [pltpu.make_async_copy(middle, out.at[pl.ds(32, 64)], sems.at[2])]
    for side in range(2):
        first = jnp.where(odd == side, 96, 0)
        copies.append(
            pltpu.make_async_copy(ends.at[side], out.at[pl.ds(first, 32)], sems.at[side])
        )
    copies[0].start()
    full = [
        t
        for side, beyond in enumerate((beyond0, beyond1))
        for half, corner in enumerate((corner0, corner1))
        for ref, at in ((beyond, half * 16), (corner, side * 16))
        for t in block_tokens(ref, at, 16)
    ]
    halo_keys[...], halo_values[...] = project_keys(
        jnp.concatenate(full, axis=0), project, blocks[...]
    )
    outside = (iota((256, LANES), 0) < 128) & nothing
    alive = [None, jnp.where(outside, 0.0, 1.0).astype(BF)]
    windows = []
    for side in range(2):
        for half in range(2):
            at, far = side * 384 + half * 64, side * 256 + half * 128
            at, far = slice(at, at + 64), slice(far, far + 128)
            side_at = slice(side * 192, side * 192 + 64)
            k = [halo_keys[far], keys[at], (far_keys0, far_keys1)[half][side_at]]
            v = [halo_values[far], values[at], (far_values0, far_values1)[half][side_at]]
            k, v = jnp.concatenate(k, axis=0), jnp.concatenate(v, axis=0)
            windows.append((queries[at], k, v, alive[side]))
    own = jnp.concatenate([tokens[0:128], tokens[384:512]], axis=0)
    mixture = attend(windows)
    result = finish(own, mixture, output[...], gain[...]).astype(BF)
    order = edge_order()
    for side in range(2):
        block = matmul(order, result[side * 128 : side * 128 + 128])
        ends[side] = block.reshape(32, LATENT, D).astype(BF)
        copies[1 + side].start()
    for copy in copies:
        copy.wait()


VMEM = pl.BlockSpec(memory_space=pltpu.VMEM)
HBM = pl.BlockSpec(memory_space=pltpu.HBM)
SMEM = pl.BlockSpec(memory_space=pltpu.SMEM)
MIB = 1024 * 1024


def swapped(value, axis, first):
    size = lax.axis_size(axis)
    step = 0 if first else 1
    route = [(i, ((i + step) ^ 1) - step) for i in range(size)]
    return lax.ppermute(value, axis, [(i, j % size) for i, j in route])


def swapped_inside(value):
    lons, lats = lax.axis_size("lon"), lax.axis_size("lat")
    route = []
    for lon in range(lons):
        for lat in range(lats):
            other = lat - 1 if lat % 2 == 0 else lat + 1
            inside = 0 <= other < lats
            target = (lon, other) if inside else (lon ^ 1, lat)
            route.append((lon * lats + lat, target[0] * lats + target[1]))
    return lax.ppermute(value, ("lon", "lat"), route)


def params(mib):
    return pltpu.CompilerParams(vmem_limit_bytes=mib * MIB)


def cost(microseconds):
    return pl.CostEstimate(
        flops=int(microseconds * 1e9), bytes_accessed=MIB, transcendentals=1 << 18
    )


def wide_rows(count):
    return jax.ShapeDtypeStruct((count, LATENT * D), BF)


def token_rows(count):
    return jax.ShapeDtypeStruct((count, D), BF)


def pack_kernel(x, out):
    out[...] = x[...].T


def pack_call(stripe):
    return pl.pallas_call(
        pack_kernel,
        out_shape=jax.ShapeDtypeStruct((LANES, LEVELS * PV), BF),
        in_specs=[VMEM],
        out_specs=VMEM,
        compiler_params=params(24),
        cost_estimate=cost(0.8),
        name="pack",
    )(stripe)


def fold_call(*operands):
    return pl.pallas_call(
        fold_kernel,
        out_shape=jax.ShapeDtypeStruct((GRAM + 192, 256), BF),
        in_specs=[HBM] * len(operands),
        out_specs=VMEM,
        scratch_shapes=[
            (pltpu.SMEM if x.shape == (HEADS,) else pltpu.VMEM)(x.shape, x.dtype) for x in operands
        ]
        + [pltpu.VMEM((128, D), F32), pltpu.SemaphoreType.DMA((len(operands),))],
        compiler_params=params(60),
        cost_estimate=cost(3.0),
        name="fold",
    )(*operands)


def encode_call(*operands):
    return pl.pallas_call(
        encode_kernel,
        out_shape=jax.ShapeDtypeStruct((D, LATENT * LANES), BF),
        in_specs=[VMEM] * len(operands),
        out_specs=VMEM,
        scratch_shapes=[
            pltpu.VMEM((256, LEVELS * LANES), BF),
            pltpu.VMEM((LEVELS * PV, LANES), BF),
            pltpu.VMEM((LEVELS, D, LANES), F32),
            pltpu.VMEM((LEVELS + 1, 64, LANES), F32),
        ],
        compiler_params=params(24),
        cost_estimate=cost(3.0),
        name="encode",
    )(*operands)


def setup_call(mats, first_scale, second_scale):
    square = lambda size: jax.ShapeDtypeStruct((size, size), BF)
    return pl.pallas_call(
        setup_kernel,
        out_shape=[
            jax.ShapeDtypeStruct(mats.shape, BF), jax.ShapeDtypeStruct((2, D), F32),
            square(128), square(256),
        ],
        in_specs=[VMEM, SMEM, SMEM],
        out_specs=[VMEM] * 4,
        compiler_params=params(24),
        cost_estimate=cost(0.8),
        name="setup",
    )(mats, first_scale, second_scale)


def first_edges_call(*operands):
    return pl.pallas_call(
        first_edges_kernel,
        out_shape=[wide_rows(32)] * 2 + [token_rows(512)] * 3,
        in_specs=[VMEM] * len(operands),
        out_specs=[VMEM] * 5,
        compiler_params=params(24),
        cost_estimate=cost(3.0),
        name="first_edges",
    )(*operands)


def first_middle_call(*operands):
    return pl.pallas_call(
        first_middle_kernel,
        out_shape=[wide_rows(64)] * 2,
        in_specs=[VMEM] * len(operands),
        out_specs=[VMEM] * 2,
        compiler_params=params(24),
        cost_estimate=cost(2.0),
        name="first_middle",
    )(*operands)


def second_own_call(*operands):
    return pl.pallas_call(
        second_own_kernel,
        out_shape=[token_rows(512)] * 4 + [token_rows(128)] + [token_rows(256)] * 2,
        in_specs=[VMEM] * len(operands),
        out_specs=[VMEM] * 7,
        compiler_params=params(24),
        cost_estimate=cost(2.6),
        name="second_own",
    )(*operands)


def second_middle_call(*operands):
    return pl.pallas_call(
        second_middle_kernel,
        out_shape=[jax.ShapeDtypeStruct((64, LATENT, D), BF)] + [token_rows(256)] * 2,
        in_specs=[VMEM] * len(operands),
        out_specs=[VMEM] * 3,
        compiler_params=params(24),
        cost_estimate=cost(1.7),
        name="second_middle",
    )(*operands)


def second_outer_call(*operands):
    return pl.pallas_call(
        second_outer_kernel,
        out_shape=jax.ShapeDtypeStruct((128, LATENT, D), BF),
        in_specs=[VMEM] * len(operands),
        out_specs=HBM,
        scratch_shapes=[pltpu.VMEM((512, D), BF)] * 2
        + [pltpu.VMEM((2, 32, LATENT, D), BF), pltpu.SemaphoreType.DMA((3,))],
        compiler_params=params(24),
        cost_estimate=cost(3.3),
        name="second_outer",
    )(*operands)


def per_device(
    fields,
    embed_weight,
    level_code,
    encoder_gain,
    key_weight,
    value_weight,
    latent_query,
    encoder_scale,
    latent_weight,
    latent_base,
    first_project,
    first_scale,
    first_output,
    first_gain,
    second_project,
    second_scale,
    second_output,
    second_gain,
):
    packed = pack_call(fields.reshape(LEVELS * PV, LANES))
    received = lax.all_to_all(packed, "lon", split_axis=0, concat_axis=0, tiled=True)
    mats = fold_call(
        embed_weight, level_code, encoder_gain.reshape(1, D), key_weight, value_weight,
        latent_query, encoder_scale,
    )
    mats, scales, order, blocks = setup_call(mats, first_scale, second_scale)
    mix = encode_call(received, order, mats)
    weights = (blocks, first_project, scales, first_output, first_gain.reshape(1, D))
    side0, side1, tokens, keys, values = first_edges_call(
        mix, latent_weight, latent_base, *weights
    )
    beyond1 = swapped_inside(side1)
    side0, side1 = lax.optimization_barrier((side0, side1))
    beyond0 = swapped(side0, "lat", True)
    beyond = [beyond0, beyond1]
    own = first_middle_call(tokens, keys, values, side0, side1, *weights)
    far = [swapped(own[0], "lon", True), swapped(own[1], "lon", False)]
    weights = (blocks, second_project, second_output, second_gain.reshape(1, D))
    ends = [jnp.concatenate([x[i : i + 16] for x in beyond], axis=0) for i in (0, 16)]
    own, ends = lax.optimization_barrier((own, ends))
    corners = [swapped(ends[0], "lon", True), swapped(ends[1], "lon", False)]
    *mine, part, far_keys0, far_values0 = second_own_call(
        *own, far[0], blocks, second_project, scales, *weights[2:]
    )
    far0 = (far_keys0, far_values0)
    done, *far1 = second_middle_call(far[1], *mine, *weights, part)
    out = second_outer_call(*beyond, *corners, *mine, *far0, *far1, done, *weights)
    return out.reshape(16, 8, LATENT, D)


def solution(mesh):
    in_specs = (P("lat", "lon", None, None, None),) + (P(),) * 17
    out_specs = P("lat", "lon", None, None)
    return jax.shard_map(
        per_device, mesh=mesh, in_specs=in_specs, out_specs=out_specs, check_vma=False
    )
```
